256 devices in a mesh: slab: 32 (over x_hi, z, core), sub: 8 (over x_lo, y).
Axes of the slice: x: 4 (x_hi: 2, x_lo: 2; x = x_hi * 2 + x_lo), y: 4, z: 8, core: 2. Of those that a mesh axis runs over, the one named last changes fastest.
Arguments:
- velocity: float32 [3, 256, 128, 128], P(None, 'slab'), may hold values from -6 to 6
- part_vel: float32 [3, 4194304], P(None, ('slab', 'sub')), may hold values from -4 to 4
- fraction: float32 [3, 4194304], P(None, ('slab', 'sub')), may hold values from 0 to 1
- base_cell: int32 [4194304], P(('slab', 'sub')), may hold values from 0 to 438, as said below
- drag_coeff: float32 [4194304], P(('slab', 'sub')), may hold values from 2 to 20
- part_volume: float32 [4194304], P(('slab', 'sub')), may hold values from 0.005 to 0.05
- brick_of_block: int32 [32768], P(('slab', 'sub')), may hold values from 0 to 255
Outputs:
- new_velocity: float32 [3, 256, 128, 128], P(None, 'slab')
- voidfraction: float32 [256, 128, 128], P('slab')
- drag: float32 [3, 4194304], P(None, ('slab', 'sub'))
The draws below stay inside these ranges and needn't reach their ends.
Inputs may be any that keep to these rules, and one draw needn't show every extreme that they name: `base_cell`: every particle's base plus one in each direction stays inside its brick: vertical base at most 6, horizontal bases at most 6.
All inputs are finite; a program needn't handle non-finite values.
Results may differ from the reference program's by a relative error of at most 0.0003.
Values sent between devices are 32-bit elements; how exact they have to be, the bound alone decides.
No kernel may reach another device: no remote copies, remote signals or barrier semaphores. Data moves between devices by JAX's collectives and lax.ppermute only.
A program may use at most 128 MiB of HBM per device.

```python
import math
import jax
import jax.numpy as jnp
import numpy as np
from jax import lax

BLOCK = 128
BLOCKS_DEV = 128
NX = 128
NY = 128
CZ = 8
ITERS = 4
NZ = 256
NBRICK = 256
NBLK = 32768
PARTS_SIZE = 4194304
N_SLAB = 32
N_SUB = 8


def draw_base_cell(key, part):
    key = jax.random.fold_in(key, 11)
    first, second, third = jax.random.split(key, 3)
    zbase = jax.random.randint(first, (PARTS_SIZE,), 0, CZ - 1)
    xbase = jax.random.randint(second, (PARTS_SIZE,), 0, 7)
    ybase = jax.random.randint(third, (PARTS_SIZE,), 0, 7)
    cell = zbase * 64 + xbase * 8 + ybase
    where_at = jnp.arange(PARTS_SIZE)
    cell = jnp.where(where_at == 0, 0, cell)
    cell = jnp.where(where_at == PARTS_SIZE - 1, 64 * CZ - 74, cell)
    return cell.astype(jnp.int32)


def touch_ends(values, stream_key, low, largest):
    shape = values.shape
    place = [jax.random.randint(jax.random.fold_in(stream_key, axis), (), 0, shape[axis]) for axis in range(len(shape))]
    values = values.at[tuple(place)].set(low)
    longest = shape.index(max(shape))
    place[longest] = (place[longest] + 1) % shape[longest]
    return values.at[tuple(place)].set(largest)


def block_scale(own_key, dims, pieces, smallest, largest):
    loudness = 1.0
    for position, blocks in pieces:
        heights = jax.random.uniform(jax.random.fold_in(jax.random.fold_in(own_key, 6), position), (blocks,), jnp.float32, smallest / len(pieces), largest / len(pieces))
        loudness = loudness * jnp.repeat(jnp.exp(heights), dims[position] // blocks).reshape((-1,) + (1,) * (len(dims) - 1 - position))
    return loudness


def rank_table(number_of, slope):
    loads = [(1 << 20) // math.isqrt(rank ** slope) + 1 for rank in range(1, number_of + 1)]
    deviation = 1 + sum(loads) // (1 << 30)
    return np.cumsum(np.array([max(1, weight // deviation) for weight in loads]))


def ranked_ids(stream_key, dims, number_of, skew):
    table = rank_table(number_of, skew)
    ticket = jax.random.randint(jax.random.fold_in(stream_key, 1), dims, 0, int(table[number_of - 1]))
    standing = jnp.searchsorted(jnp.asarray(table, jnp.int32), ticket, side="right")
    return jax.random.permutation(jax.random.fold_in(stream_key, 2), number_of)[standing].astype(jnp.int32)


def noise(rng, extent, spread, reach, cuts=(), kind=jnp.bfloat16):
    result = spread * jax.random.normal(rng, extent, jnp.float32)
    if cuts:
        result = result * block_scale(rng, extent, cuts, -0.22, 0.18)
    return jnp.clip(result, -reach, reach).astype(kind)


def setup_inputs(seed: int = 0) -> dict:
    splits = jax.random.split(jax.random.key(seed), 8)
    velocity = noise(splits[0], (3, NZ, NX, NY), 1.0, 6.0, ((1, 32),), jnp.float32)
    part_vel = noise(splits[1], (3, PARTS_SIZE), 0.5, 4.0, ((1, 256),), jnp.float32)
    fraction = jnp.clip(1.0 * jax.random.uniform(splits[2], (3, PARTS_SIZE), jnp.float32) ** block_scale(splits[2], (3, PARTS_SIZE), ((1, 256),), -0.2, 0.2), 0.0, 1.0)
    base_cell = draw_base_cell(jax.random.fold_in(splits[7], 71), 0)
    drag_coeff = jnp.clip(jnp.exp(math.log(20.0) - 2.3025851 * jax.random.uniform(splits[4], (PARTS_SIZE,), jnp.float32) ** block_scale(splits[4], (PARTS_SIZE,), ((0, 256),), -0.2, 0.2)), 2.0, 20.0)
    part_volume = jnp.clip(jnp.exp(math.log(0.05) - 2.3025851 * jax.random.uniform(splits[5], (PARTS_SIZE,), jnp.float32) ** block_scale(splits[5], (PARTS_SIZE,), ((0, 256),), -0.2, 0.2)), 0.005, 0.05)
    brick_of_block = touch_ends(ranked_ids(splits[6], (NBLK,), NBRICK, 2), jax.random.fold_in(splits[6], 3), 0, NBRICK - 1).astype(jnp.int32)
    return dict(velocity=velocity, part_vel=part_vel, fraction=fraction, base_cell=base_cell, drag_coeff=drag_coeff, part_volume=part_volume, brick_of_block=brick_of_block)


EPS_MIN = 0.35
FLOW_POWER = -0.2
DRAG_POWER = -2.65
VISCOSITY = 1.2
TIME_STEP = 0.05


def kernel_weights(base, frac, depth):
    zbase = (base // 64)[:, None, :]
    xbase = ((base // 8) % 8)[:, None, :]
    ybase = (base % 8)[:, None, :]
    zrange = jnp.arange(depth, dtype=jnp.int32)[None, :, None]
    erange = jnp.arange(8, dtype=jnp.int32)[None, :, None]
    fz = frac[0][:, None, :]
    fx = frac[1][:, None, :]
    fy = frac[2][:, None, :]
    zero = jnp.float32(0.0)
    wz = jnp.where(zrange == zbase, 1.0 - fz, zero) + jnp.where(zrange == zbase + 1, fz, zero)
    wx = jnp.where(erange == xbase, 1.0 - fx, zero) + jnp.where(erange == xbase + 1, fx, zero)
    wy = jnp.where(erange == ybase, 1.0 - fy, zero) + jnp.where(erange == ybase + 1, fy, zero)
    full = wz[:, :, None, None, :] * wx[:, None, :, None, :] * wy[:, None, None, :, :]
    return full.reshape(base.shape[0], depth * 64, base.shape[1])


def particle_drag(weights, eps_rows, vel_rows, pvel, coef, pvol):
    eps_p = jnp.einsum("bcp,bc->bp", weights, eps_rows, precision=lax.Precision.HIGHEST)
    fluid = jnp.einsum("bcp,bkc->bkp", weights, vel_rows, precision=lax.Precision.HIGHEST)
    rel = fluid - pvel
    speed = jnp.sum(rel * rel, axis=1)
    factor = coef * pvol * (speed + 0.01) ** FLOW_POWER * eps_p ** DRAG_POWER
    force = factor[:, None, :] * rel
    deposit = jnp.einsum("bcp,bkp->bkc", weights, force, precision=lax.Precision.HIGHEST)
    return force, deposit


def advance(zpad, source):
    padded = jnp.pad(zpad, ((0, 0), (0, 0), (1, 1), (1, 1)))
    centre = padded[:, 1:-1, 1:-1, 1:-1]
    upper = padded[:, 2:, 1:-1, 1:-1]
    lower = padded[:, :-2, 1:-1, 1:-1]
    east = padded[:, 1:-1, 2:, 1:-1]
    west = padded[:, 1:-1, :-2, 1:-1]
    north = padded[:, 1:-1, 1:-1, 2:]
    south = padded[:, 1:-1, 1:-1, :-2]
    shear = jnp.sum((upper - centre) ** 2 + (east - centre) ** 2 + (north - centre) ** 2, axis=0)
    viscous = VISCOSITY * (shear + 0.01) ** FLOW_POWER
    laplace = upper + lower + east + west + north + south - 6.0 * centre
    return centre + TIME_STEP * (viscous[None] * laplace + source)


def reference(velocity, part_vel, fraction, base_cell, drag_coeff, part_volume, brick_of_block):
    depth = CZ
    cells = depth * 64
    bricks = (NX // 8) * (NY // 8)
    blocks = brick_of_block.shape[0]
    group = math.gcd(BLOCKS_DEV, 16)
    count = blocks // group
    base = base_cell.reshape(count, group, BLOCK)
    frac = fraction.reshape(3, count, group, BLOCK).transpose(1, 0, 2, 3)
    pvel = part_vel.reshape(3, count, group, BLOCK).transpose(1, 2, 0, 3)
    coef = drag_coeff.reshape(count, group, BLOCK)
    pvol = part_volume.reshape(count, group, BLOCK)
    slab_of = jnp.arange(blocks, dtype=jnp.int32) // (N_SUB * BLOCKS_DEV)
    global_brick = slab_of * bricks + brick_of_block
    group_bricks = global_brick.reshape(count, group)

    def volume_group(items):
        weights = kernel_weights(items[0], items[1], depth)
        return jnp.einsum("bcp,bp->bc", weights, items[2], precision=lax.Precision.HIGHEST)

    volumes = lax.map(volume_group, (base, frac, pvol)).reshape(blocks, cells)
    solid = jax.ops.segment_sum(volumes, global_brick, num_segments=N_SLAB * bricks)
    eps_brick = jnp.maximum(1.0 - solid, EPS_MIN)
    vel_bricks = velocity.reshape(3, N_SLAB, depth, NX // 8, 8, NY // 8, 8)
    vel_bricks = vel_bricks.transpose(1, 3, 5, 0, 2, 4, 6).reshape(N_SLAB * bricks, 3, cells)

    def drag_group(items):
        weights = kernel_weights(items[0], items[1], depth)
        rows = items[5]
        return particle_drag(weights, eps_brick[rows], vel_bricks[rows], items[2], items[3], items[4])

    forces, deposits = lax.map(drag_group, (base, frac, pvel, coef, pvol, group_bricks))
    force_field = jax.ops.segment_sum(deposits.reshape(blocks, 3 * cells), global_brick, num_segments=N_SLAB * bricks)
    source_brick = -force_field.reshape(N_SLAB * bricks, 3, cells) / eps_brick[:, None, :]

    def to_grid(field, comps):
        grid = field.reshape(N_SLAB, NX // 8, NY // 8, comps, depth, 8, 8)
        return grid.transpose(3, 0, 4, 1, 5, 2, 6).reshape(comps, N_SLAB * depth, NX, NY)

    source = to_grid(source_brick, 3)
    voidfraction = to_grid(eps_brick[:, None, :], 1)[0]
    current = velocity
    for step in range(ITERS):
        zpad = jnp.pad(current, ((0, 0), (1, 1), (0, 0), (0, 0)))
        current = advance(zpad, source)
    drag = forces.reshape(blocks, 3, BLOCK).transpose(1, 0, 2).reshape(3, blocks * BLOCK)
    return current, voidfraction, drag
```

```python
import functools

import jax
import jax.numpy as jnp
from jax import lax
from jax.experimental import pallas as pl
from jax.experimental.pallas import tpu as pltpu
from jax.sharding import PartitionSpec as P

BLOCK = 128
LANES = 128
EPS_MIN = 0.35
FLOW_POWER = -0.2
DRAG_POWER = -2.65
VISCOSITY = 1.2
TIME_STEP = 0.05
ITERS = 4
UNROLL = 8
F32 = jnp.float32
PARAMS = pltpu.CompilerParams(vmem_limit_bytes=32 * 1024 * 1024)
FULL = pltpu.CompilerParams(vmem_limit_bytes=60 * 1024 * 1024)
VMEM = pl.BlockSpec(memory_space=pltpu.VMEM)
SMEM = pl.BlockSpec(memory_space=pltpu.SMEM)
HBM = pl.BlockSpec(memory_space=pltpu.HBM)
ANY = pl.BlockSpec(memory_space=pl.ANY)


def transpose_granules(tiles, lane):
    for bit in (1, 2, 4):
        shift = 8 * bit
        high = (lane & shift) != 0
        new = list(tiles)
        for a in range(8):
            if a & bit:
                continue
            b = a | bit
            va, vb = tiles[a], tiles[b]
            new[a] = jnp.where(high, pltpu.roll(vb, shift, 1), va)
            new[b] = jnp.where(high, vb, pltpu.roll(va, LANES - shift, 1))
        tiles = new
    return tiles


def fetch(pairs, sems):
    copies = [pltpu.make_async_copy(a, b, sems.at[i]) for i, (a, b) in enumerate(pairs)]
    for copy in copies:
        copy.start()
    return copies


def lanes_iota():
    return lax.broadcasted_iota(jnp.int32, (8, LANES), 1)


def rows_iota():
    return lax.broadcasted_iota(jnp.int32, (8, LANES), 0)


def spread(row):
    return jnp.broadcast_to(row, (8, LANES))


def particles(base_ref, frac_ref, block):
    at = pl.ds(pl.multiple_of(block * BLOCK, BLOCK), BLOCK)
    base = spread(base_ref[pl.ds(block, 1), :])
    fz = spread(frac_ref[0:1, at])
    fx = spread(frac_ref[1:2, at])
    fy = spread(frac_ref[2:3, at])
    return at, base >> 6, (base >> 3) & 7, base & 7, fz, fx, fy


def axis_weights(rows, first, frac):
    zero = jnp.zeros_like(frac)
    return jnp.where(rows == first, 1.0 - frac, jnp.where(rows == first + 1, frac, zero))


def plane_weights(rows, zb, yb, fz, fy):
    ky = axis_weights(rows, yb, fy)
    parts = []
    for z in range(8):
        kz = jnp.where(zb == z, 1.0 - fz, jnp.where(zb == z - 1, fz, jnp.zeros_like(fz)))
        parts.append(kz * ky)
    full = jnp.concatenate(parts, axis=0)
    high = full.astype(jnp.bfloat16)
    low = (full - high.astype(F32)).astype(jnp.bfloat16)
    return jnp.concatenate([high, low], axis=0)


def split_rows(parts):
    full = jnp.concatenate(parts, axis=0)
    high = full.astype(jnp.bfloat16).astype(F32)
    return jnp.concatenate([high, full - high], axis=0).astype(jnp.bfloat16)


def deposit(parts, weights):
    left = split_rows(parts)
    both = lax.dot_general(
        left, weights, (((1,), (1,)), ((), ())), preferred_element_type=F32
    )
    half = both.shape[0] // 2
    both = both[:half] + both[half:]
    return both + pltpu.roll(both, 64, 1)


def corner_terms(zb, yb, fz, fy, offset):
    index = (zb << 3) + yb + offset
    gz, gy = 1.0 - fz, 1.0 - fy
    return (
        (index, gz * gy),
        (index + 1, gz * fy),
        (index + 8, fz * gy),
        (index + 9, fz * fy),
    )


def interpolate(tile, kx, corners):
    total = None
    for index, weight in corners:
        term = weight * jnp.take_along_axis(tile, index, axis=1, mode="promise_in_bounds")
        total = term if total is None else total + term
    return jnp.sum(kx * total, axis=0, keepdims=True)


def brick_place(brick):
    return brick >> 4, brick & 7, (brick >> 3) & 1


def solid_kernel(
    brick_hbm, base_hbm, frac_hbm, pvol_hbm, out_ref, brick_ref, base_ref, frac_ref, pvol_ref, sems
):
    copies = fetch(
        [(brick_hbm, brick_ref), (base_hbm, base_ref), (frac_hbm, frac_ref), (pvol_hbm, pvol_ref)],
        sems,
    )
    out_ref[...] = jnp.zeros_like(out_ref)
    for copy in copies:
        copy.wait()
    rows, lane = rows_iota(), lanes_iota()

    def step(number, carry):
        found = []
        for k in range(UNROLL):
            block = number * UNROLL + k
            _, zb, xb, yb, fz, fx, fy = particles(base_ref, frac_ref, block)
            kx = axis_weights(rows, xb, fx) * spread(pvol_ref[pl.ds(block, 1), :])
            found.append(deposit([kx], plane_weights(rows, zb, yb, fz, fy)))
        for k in range(UNROLL):
            tx, t3, t1 = brick_place(brick_ref[number * UNROLL + k])
            tile = tx * 8 + t3
            out_ref[tile] += jnp.where((lane >> 6) == t1, found[k], 0.0)
        return carry

    lax.fori_loop(0, base_ref.shape[0] // UNROLL, step, 0)


def eps_kernel(parts_ref, out_ref, copies_ref):
    total = parts_ref[0]
    for j in range(1, parts_ref.shape[0]):
        total = total + parts_ref[j]
    total = jnp.maximum(1.0 - total, EPS_MIN)
    out_ref[...] = total
    for j in range(copies_ref.shape[0]):
        copies_ref[j] = total


def slip_kernel(
    solid_any, sub_ref, brick_hbm, base_hbm, frac_hbm, pvel_hbm, coef_hbm, pvol_hbm, velocity_hbm,
    out_ref, window_ref,
    brick_ref, base_ref, frac_ref, pvel_ref, coef_ref, pvol_ref, velocity_ref, table, sems,
):
    copies = fetch(
        [(velocity_hbm.at[c], velocity_ref.at[c]) for c in range(3)]
        + [
            (brick_hbm, brick_ref),
            (base_hbm, base_ref),
            (frac_hbm, frac_ref),
            (pvel_hbm, pvel_ref),
            (coef_hbm, coef_ref),
            (pvol_hbm, pvol_ref),
        ],
        sems,
    )
    rows, lane = rows_iota(), lanes_iota()
    tiles_x = velocity_ref.shape[2] // 8

    for c in range(3):
        copies[c].wait()

        def convert(tx, carry, c=c):
            at = pl.ds(pl.multiple_of(tx * 8, 8), 8)
            tiles = transpose_granules([velocity_ref[c, z, at, :] for z in range(8)], lane)
            for t3 in range(8):
                table[(tx * 3 + c) * 8 + t3] = tiles[t3]
            return carry

        lax.fori_loop(0, tiles_x, convert, 0)
    for copy in copies[3:]:
        copy.wait()

    for r in range(4):
        want = sub_ref[0] * 2 + r - 1
        inside = jnp.logical_and(want >= 0, want < tiles_x)
        at = pl.ds(pl.multiple_of(jnp.clip(want, 0, tiles_x - 1) * 8, 8), 8)
        window_ref[:, :, 8 * r : 8 * r + 8, :] = jnp.where(inside, velocity_ref[:, :, at, :], 0.0)

    def step(number, carry):
        for k in range(UNROLL):
            block = number * UNROLL + k
            at, zb, xb, yb, fz, fx, fy = particles(base_ref, frac_ref, block)
            tx, t3, t1 = brick_place(brick_ref[block])
            kx = axis_weights(rows, xb, fx)
            corners = corner_terms(zb, yb, fz, fy, t1 * 64)
            rel = [
                interpolate(table[(tx * 3 + c) * 8 + t3], kx, corners) - pvel_ref[c : c + 1, at]
                for c in range(3)
            ]
            speed = rel[0] * rel[0] + rel[1] * rel[1] + rel[2] * rel[2]
            factor = coef_ref[pl.ds(block, 1), :] * pvol_ref[pl.ds(block, 1), :]
            factor = factor * jnp.exp(FLOW_POWER * jnp.log(speed + 0.01))
            for c in range(3):
                out_ref[c : c + 1, at] = factor * rel[c]
        return carry

    lax.fori_loop(0, base_ref.shape[0] // UNROLL, step, 0)


def drag_kernel(
    brick_ref, base_ref, frac_ref, slip_ref, eps_ref, below_any, above_any, drag_ref, out_ref
):
    out_ref[...] = jnp.zeros_like(out_ref)
    rows, lane = rows_iota(), lanes_iota()

    def step(number, carry):
        found = []
        for k in range(UNROLL):
            block = number * UNROLL + k
            at, zb, xb, yb, fz, fx, fy = particles(base_ref, frac_ref, block)
            tx, t3, t1 = brick_place(brick_ref[block])
            kx = axis_weights(rows, xb, fx)
            eps = interpolate(eps_ref[tx * 8 + t3], kx, corner_terms(zb, yb, fz, fy, t1 * 64))
            factor = jnp.exp(DRAG_POWER * jnp.log(eps))
            parts = []
            for c in range(3):
                force = factor * slip_ref[c : c + 1, at]
                drag_ref[c : c + 1, at] = force
                parts.append(kx * spread(force))
            found.append(deposit(parts, plane_weights(rows, zb, yb, fz, fy)))
        for k in range(UNROLL):
            tx, t3, t1 = brick_place(brick_ref[number * UNROLL + k])
            mine = (lane >> 6) == t1
            for c in range(3):
                tile = (tx * 3 + c) * 8 + t3
                out_ref[tile] += jnp.where(mine, found[k][8 * c : 8 * c + 8], 0.0)
        return carry

    lax.fori_loop(0, base_ref.shape[0] // UNROLL, step, 0)


def source_kernel(parts_ref, eps_ref, own_ref, low_ref, high_ref):
    lane = lanes_iota()
    for t in range(2):
        for c in range(3):
            tiles = []
            for t3 in range(8):
                at = (t * 3 + c) * 8 + t3
                total = parts_ref[0, at]
                for j in range(1, parts_ref.shape[0]):
                    total = total + parts_ref[j, at]
                tiles.append(-total / eps_ref[t * 8 + t3])
            tiles = transpose_granules(tiles, lane)
            for z in range(8):
                own_ref[c, z, 8 * t : 8 * t + 8, :] = tiles[z]
                if z < 3:
                    low_ref[c, z, 8 * t : 8 * t + 8, :] = tiles[z]
                if z >= 5:
                    high_ref[c, z - 5, 8 * t : 8 * t + 8, :] = tiles[z]


def void_kernel(eps_ref, out_ref):
    lane = lanes_iota()

    def convert(tx, carry):
        tiles = transpose_granules([eps_ref[tx * 8 + t3] for t3 in range(8)], lane)
        for z in range(8):
            out_ref[z, pl.ds(pl.multiple_of(tx * 8, 8), 8), :] = tiles[z]
        return carry

    lax.fori_loop(0, out_ref.shape[1] // 8, convert, 0)


def stencil_kernel(
    place_ref, window_ref, below_ref, above_ref, own_ref, low_ref, high_ref, left_ref, right_ref, out_ref, first, second, source
):
    slab, sub, planes, width = place_ref[0], place_ref[1], place_ref[2], place_ref[3]
    first[:, 0:4] = below_ref[...]
    first[:, 4:12] = window_ref[...]
    first[:, 12:16] = above_ref[...]
    source[:, 0:3, 8:24, :] = low_ref[...]
    source[:, 3:11, 8:24, :] = own_ref[...]
    source[:, 11:14, 8:24, :] = high_ref[...]
    source[:, :, 0:8, :] = left_ref[...]
    source[:, :, 24:32, :] = right_ref[...]
    lane = lax.broadcasted_iota(jnp.int32, (32, LANES), 1)
    row = lax.broadcasted_iota(jnp.int32, (32, LANES), 0) + sub * 16 - 8
    inside_x = jnp.logical_and(row >= 0, row < width)
    buffers = (first, second)
    for number in range(ITERS):
        old, new = buffers[number % 2], buffers[(number + 1) % 2]

        def plane(z, carry, old=old, new=new):
            shear = None
            centres, laps = [], []
            for c in range(3):
                centre = old[c, z]
                upper = old[c, z + 1]
                lower = old[c, z - 1]
                east = pltpu.roll(centre, 31, 0)
                west = pltpu.roll(centre, 1, 0)
                north = jnp.where(lane == LANES - 1, 0.0, pltpu.roll(centre, LANES - 1, 1))
                south = jnp.where(lane == 0, 0.0, pltpu.roll(centre, 1, 1))
                term = (upper - centre) ** 2 + (east - centre) ** 2 + (north - centre) ** 2
                shear = term if shear is None else shear + term
                centres.append(centre)
                laps.append(upper + lower + east + west + north + south - 6.0 * centre)
            viscous = VISCOSITY * jnp.exp(FLOW_POWER * jnp.log(shear + 0.01))
            height = slab * 8 - 4 + z
            keep = jnp.logical_and(inside_x, jnp.logical_and(height >= 0, height < planes))
            for c in range(3):
                moved = centres[c] + TIME_STEP * (viscous * laps[c] + source[c, z - 1])
                new[c, z] = jnp.where(keep, moved, 0.0)
            return carry

        lax.fori_loop(number + 1, 15 - number, plane, 0)
    last = buffers[ITERS % 2]
    for j in range(out_ref.shape[0]):
        out_ref[j] = last[:, 4:12, 8:24, :]


def place_kernel(parts_ref, out_ref, sems):
    rows = parts_ref.shape[3]
    copies = fetch(
        [
            (parts_ref.at[j], out_ref.at[:, :, pl.ds(j * rows, rows), :])
            for j in range(parts_ref.shape[0])
        ],
        sems,
    )
    for copy in copies:
        copy.wait()


def call(kernel, out_shapes, ins, scratch=(), outs=None, us=1.0, params=PARAMS):
    return pl.pallas_call(
        kernel,
        out_shape=[jax.ShapeDtypeStruct(s, F32) for s in out_shapes],
        in_specs=ins,
        out_specs=outs or [VMEM] * len(out_shapes),
        scratch_shapes=list(scratch),
        compiler_params=params,
        cost_estimate=pl.CostEstimate(flops=int(us * 1e9), bytes_accessed=int(us * 3.6e6), transcendentals=0),
    )


def shift(x, axis, up):
    peers = lax.axis_size(axis)
    pairs = [(i, i + 1) if up else (i + 1, i) for i in range(peers - 1)]
    return lax.ppermute(x, axis, pairs)


def body(velocity, part_vel, fraction, base_cell, drag_coeff, part_volume, brick_of_block):
    depth, width_x = velocity.shape[1], velocity.shape[2]
    blocks = brick_of_block.shape[0]
    subs = lax.axis_size("sub")
    slab = lax.axis_index("slab").astype(jnp.int32)
    sub = lax.axis_index("sub").astype(jnp.int32)
    tiles_x = width_x // 8
    tiles = tiles_x * 8
    share = tiles // subs
    base = base_cell.reshape(blocks, BLOCK)
    coef = drag_coeff.reshape(blocks, BLOCK)
    pvol = part_volume.reshape(blocks, BLOCK)

    particles_vmem = [
        pltpu.SMEM((blocks,), jnp.int32),
        pltpu.VMEM((blocks, BLOCK), jnp.int32),
        pltpu.VMEM((3, blocks * BLOCK), F32),
    ]
    row_vmem = pltpu.VMEM((blocks, BLOCK), F32)
    (solid,) = call(
        solid_kernel,
        [(tiles, 8, LANES)],
        [HBM] * 4,
        particles_vmem + [row_vmem, pltpu.SemaphoreType.DMA((4,))],
        us=6.0,
        params=FULL,
    )(brick_of_block, base, fraction, pvol)
    solid_parts = lax.all_to_all(solid.reshape(subs, share, 8, LANES), "sub", 0, 0)
    slip, window = call(
        slip_kernel,
        [(3, blocks * BLOCK), (3, depth, 32, LANES)],
        [ANY, SMEM] + [HBM] * 7,
        particles_vmem
        + [
            pltpu.VMEM((3, blocks * BLOCK), F32),
            row_vmem,
            row_vmem,
            pltpu.VMEM(velocity.shape, F32),
            pltpu.VMEM((3 * tiles, 8, LANES), F32),
            pltpu.SemaphoreType.DMA((9,)),
        ],
        us=9.0,
        params=FULL,
    )(solid, sub.reshape(1), brick_of_block, base, fraction, part_vel, coef, pvol, velocity)
    below = shift(window[:, depth - 4 :], "slab", True)
    above = shift(window[:, :4], "slab", False)

    eps_own, eps_copies = call(
        eps_kernel, [(share, 8, LANES), (subs, share, 8, LANES)], [VMEM], us=0.5
    )(solid_parts)
    eps = lax.all_to_all(eps_copies, "sub", 0, 0).reshape(tiles, 8, LANES)
    drag, force = call(
        drag_kernel,
        [(3, blocks * BLOCK), (3 * tiles, 8, LANES)],
        [SMEM] + [VMEM] * 4 + [ANY] * 2,
        us=8.0,
    )(brick_of_block, base, fraction, slip, eps, below, above)
    force_parts = lax.all_to_all(force.reshape(subs, 3 * share, 8, LANES), "sub", 0, 0)
    (voidfraction,) = call(void_kernel, [(depth, width_x, LANES)], [VMEM], us=3.0)(eps)

    rows = width_x // subs
    own, first, last = call(
        source_kernel,
        [(3, depth, rows, LANES), (3, 3, rows, LANES), (3, 3, rows, LANES)],
        [VMEM, VMEM],
    )(force_parts, eps_own)
    low = shift(last, "slab", True)
    high = shift(first, "slab", False)
    whole = jnp.concatenate([low, own, high], axis=1)
    left = shift(whole[:, :, 8:16], "sub", True)
    right = shift(whole[:, :, 0:8], "sub", False)
    planes = depth * lax.axis_size("slab")
    place = jnp.stack([slab, sub, jnp.int32(planes), jnp.int32(width_x)])
    (moved,) = call(
        stencil_kernel,
        [(subs, 3, depth, rows, LANES)],
        [SMEM] + [VMEM] * 8,
        [
            pltpu.VMEM((3, 16, 32, LANES), F32),
            pltpu.VMEM((3, 16, 32, LANES), F32),
            pltpu.VMEM((3, 14, 32, LANES), F32),
        ],
        us=6.0,
    )(place, window, below, above, own, low, high, left, right)
    moved = lax.all_to_all(moved, "sub", 0, 0)
    (new_velocity,) = call(
        place_kernel,
        [velocity.shape],
        [ANY],
        [pltpu.SemaphoreType.DMA((subs,))],
        outs=[ANY],
    )(moved)
    return new_velocity, voidfraction, drag


def solution(mesh):
    in_specs = (
        P(None, "slab", None, None),
        P(None, ("slab", "sub")),
        P(None, ("slab", "sub")),
        P(("slab", "sub")),
        P(("slab", "sub")),
        P(("slab", "sub")),
        P(("slab", "sub")),
    )
    out_specs = (P(None, "slab", None, None), P("slab", None, None), P(None, ("slab", "sub")))
    return jax.shard_map(body, mesh=mesh, in_specs=in_specs, out_specs=out_specs, check_vma=False)
```

```python
import functools

import jax
import jax.numpy as jnp
from jax import lax
from jax.experimental import pallas as pl
from jax.experimental.pallas import tpu as pltpu
from jax.sharding import PartitionSpec as P

BLOCK = 128
LANES = 128
EPS_MIN = 0.35
FLOW_POWER = -0.2
DRAG_POWER = -2.65
VISCOSITY = 1.2
TIME_STEP = 0.05
ITERS = 4
UNROLL = 16
F32 = jnp.float32
PARAMS = pltpu.CompilerParams(vmem_limit_bytes=16 * 1024 * 1024)
FULL = pltpu.CompilerParams(vmem_limit_bytes=60 * 1024 * 1024)
VMEM = pl.BlockSpec(memory_space=pltpu.VMEM)
SMEM = pl.BlockSpec(memory_space=pltpu.SMEM)
HBM = pl.BlockSpec(memory_space=pltpu.HBM)
ANY = pl.BlockSpec(memory_space=pl.ANY)


def transpose_granules(tiles, lane):
    for bit in (1, 2, 4):
        shift = 8 * bit
        high = (lane & shift) != 0
        new = list(tiles)
        for a in range(8):
            if a & bit:
                continue
            b = a | bit
            va, vb = tiles[a], tiles[b]
            new[a] = jnp.where(high, pltpu.roll(vb, shift, 1), va)
            new[b] = jnp.where(high, vb, pltpu.roll(va, LANES - shift, 1))
        tiles = new
    return tiles


def fetch(pairs, sems):
    copies = [pltpu.make_async_copy(a, b, sems.at[i]) for i, (a, b) in enumerate(pairs)]
    for copy in copies:
        copy.start()
    return copies


def lanes_iota():
    return lax.broadcasted_iota(jnp.int32, (8, LANES), 1)


def rows_iota():
    return lax.broadcasted_iota(jnp.int32, (8, LANES), 0)


def spread(row):
    return jnp.broadcast_to(row, (8, LANES))


def particles(base_ref, frac_ref, block):
    at = pl.ds(pl.multiple_of(block * BLOCK, BLOCK), BLOCK)
    base = spread(base_ref[pl.ds(block, 1), :])
    fz = spread(frac_ref[0:1, at])
    fx = spread(frac_ref[1:2, at])
    fy = spread(frac_ref[2:3, at])
    return at, base >> 6, (base >> 3) & 7, base & 7, fz, fx, fy


def axis_weights(rows, first, frac):
    zero = jnp.zeros_like(frac)
    return jnp.where(rows == first, 1.0 - frac, jnp.where(rows == first + 1, frac, zero))


def halves(value):
    high = value.astype(jnp.bfloat16).astype(F32)
    return high, value - high


def plane_weights(rows, zb, yb, fz, fy):
    ky = axis_weights(rows, yb, fy)
    zero = jnp.zeros_like(fz)
    at = [zb == z for z in range(7)]
    parts = []
    for here, above in zip(halves((1.0 - fz) * ky), halves(fz * ky)):
        for z in range(8):
            part = zero if z == 0 else jnp.where(at[z - 1], above, zero)
            parts.append(part if z == 7 else jnp.where(at[z], here, part))
    return jnp.concatenate(parts, axis=0).astype(jnp.bfloat16)


def split_rows(parts):
    full = jnp.concatenate(parts, axis=0)
    high = full.astype(jnp.bfloat16).astype(F32)
    return jnp.concatenate([high, full - high], axis=0).astype(jnp.bfloat16)


def deposit(parts, weights):
    left = split_rows(parts)
    both = lax.dot_general(
        left, weights, (((1,), (1,)), ((), ())), preferred_element_type=F32
    )
    half = both.shape[0] // 2
    both = both[:half] + both[half:]
    return both + pltpu.roll(both, 64, 1)


def corner_terms(zb, yb, fz, fy, offset):
    index = (zb << 3) + yb + offset
    gz, gy = 1.0 - fz, 1.0 - fy
    return (
        (index, gz * gy),
        (index + 1, gz * fy),
        (index + 8, fz * gy),
        (index + 9, fz * fy),
    )


def interpolate(tile, kx, corners):
    total = None
    for index, weight in corners:
        term = weight * jnp.take_along_axis(tile, index, axis=1, mode="promise_in_bounds")
        total = term if total is None else total + term
    return jnp.sum(kx * total, axis=0, keepdims=True)


def brick_place(brick):
    return brick >> 4, brick & 7, (brick >> 3) & 1


def solid_kernel(
    brick_hbm, base_hbm, frac_hbm, pvol_hbm, out_ref, brick_ref, base_ref, frac_ref, pvol_ref, sems
):
    copies = fetch(
        [(brick_hbm, brick_ref), (base_hbm, base_ref), (frac_hbm, frac_ref), (pvol_hbm, pvol_ref)],
        sems,
    )
    out_ref[...] = jnp.zeros_like(out_ref)
    for copy in copies:
        copy.wait()
    rows, lane = rows_iota(), lanes_iota()

    def step(number, carry):
        found = []
        for k in range(UNROLL):
            block = number * UNROLL + k
            _, zb, xb, yb, fz, fx, fy = particles(base_ref, frac_ref, block)
            kx = axis_weights(rows, xb, fx) * spread(pvol_ref[pl.ds(block, 1), :])
            found.append(deposit([kx], plane_weights(rows, zb, yb, fz, fy)))
        for k in range(UNROLL):
            tx, t3, t1 = brick_place(brick_ref[number * UNROLL + k])
            tile = tx * 8 + t3
            out_ref[tile] += jnp.where((lane >> 6) == t1, found[k], 0.0)
        return carry

    lax.fori_loop(0, base_ref.shape[0] // UNROLL, step, 0)


def eps_kernel(parts_ref, out_ref, copies_ref):
    total = parts_ref[0]
    for j in range(1, parts_ref.shape[0]):
        total = total + parts_ref[j]
    total = jnp.maximum(1.0 - total, EPS_MIN)
    out_ref[...] = total
    for j in range(copies_ref.shape[0]):
        copies_ref[j] = total


def slip_kernel(
    first, count,
    after_any, brick_hbm, base_hbm, frac_hbm, pvel_hbm, coef_hbm, pvol_hbm, velocity_hbm,
    out_ref,
    brick_ref, base_ref, frac_ref, pvel_ref, coef_ref, pvol_ref, velocity_ref, table_ref, sems,
):
    some = pl.ds(first, count)
    wide = pl.ds(first * BLOCK, count * BLOCK)
    copies = fetch(
        [
            (velocity_hbm, velocity_ref),
            (brick_hbm, brick_ref),
            (base_hbm.at[some], base_ref),
            (frac_hbm.at[:, wide], frac_ref),
            (pvel_hbm.at[:, wide], pvel_ref),
            (coef_hbm.at[some], coef_ref),
            (pvol_hbm.at[some], pvol_ref),
        ],
        sems,
    )
    rows, lane = rows_iota(), lanes_iota()
    tiles_x = velocity_ref.shape[2] // 8

    def convert(number, carry):
        for k in range(2):
            tx = number * 2 + k
            at = pl.ds(pl.multiple_of(tx * 8, 8), 8)
            for c in range(3):
                tiles = transpose_granules([velocity_ref[c, z, at, :] for z in range(8)], lane)
                for t3 in range(8):
                    table_ref[(tx * 3 + c) * 8 + t3] = tiles[t3]
        return carry

    copies[0].wait()
    lax.fori_loop(0, tiles_x // 2, convert, 0)
    for copy in copies[1:]:
        copy.wait()

    def step(number, carry):
        for k in range(UNROLL):
            block = number * UNROLL + k
            at, zb, xb, yb, fz, fx, fy = particles(base_ref, frac_ref, block)
            tx, t3, t1 = brick_place(brick_ref[first + block])
            kx = axis_weights(rows, xb, fx)
            corners = corner_terms(zb, yb, fz, fy, t1 * 64)
            rel = [
                interpolate(table_ref[(tx * 3 + c) * 8 + t3], kx, corners) - pvel_ref[c : c + 1, at]
                for c in range(3)
            ]
            speed = rel[0] * rel[0] + rel[1] * rel[1] + rel[2] * rel[2]
            factor = coef_ref[pl.ds(block, 1), :] * pvol_ref[pl.ds(block, 1), :]
            factor = factor * jnp.exp(FLOW_POWER * jnp.log(speed + 0.01))
            for c in range(3):
                out_ref[c : c + 1, at] = factor * rel[c]
        return carry

    lax.fori_loop(0, count // UNROLL, step, 0)


def pack_halo(rows, tiles):
    a, b, c, d = tiles
    middle = jnp.logical_or(rows == 3, rows == 4)
    first = jnp.where(middle, pltpu.roll(d, 3, 0), a)
    second = jnp.where(rows == 3, pltpu.roll(d, 1, 0), jnp.where(rows == 4, pltpu.roll(d, 7, 0), b))
    third = jnp.where(middle, pltpu.roll(d, 5, 0), c)
    return first, second, third


def unpack_halo(rows, tiles):
    a, b, c = tiles
    inner = jnp.where(rows == 2, pltpu.roll(b, 7, 0), pltpu.roll(b, 1, 0))
    d = jnp.where(rows < 2, pltpu.roll(a, 5, 0), jnp.where(rows > 5, pltpu.roll(c, 3, 0), inner))
    return a, b, c, d


def drag_kernel(
    brick_ref, base_ref, frac_ref, slip_a_hbm, slip_b_hbm, eps_ref,
    drag_ref, out_hbm, tick_ref,
    force_ref, slip_a_ref, slip_b_ref, sems,
):
    subs = force_ref.shape[0]
    rows, lane = rows_iota(), lanes_iota()
    slips = fetch([(slip_a_hbm, slip_a_ref), (slip_b_hbm, slip_b_ref)], sems)
    for j in range(subs):
        force_ref[j, 0:48] = jnp.zeros((48, 8, LANES), F32)
    halves_of = ((slip_a_ref, 0), (slip_b_ref, slip_a_ref.shape[1] // BLOCK))
    for copy in slips:
        copy.wait()

    for slip_ref, start in halves_of:

        def step(number, carry, slip_ref=slip_ref, start=start):
            found = []
            for k in range(UNROLL):
                inner = number * UNROLL + k
                block = inner + start
                at, zb, xb, yb, fz, fx, fy = particles(base_ref, frac_ref, block)
                inner_at = pl.ds(pl.multiple_of(inner * BLOCK, BLOCK), BLOCK)
                tx, t3, t1 = brick_place(brick_ref[block])
                kx = axis_weights(rows, xb, fx)
                eps = interpolate(eps_ref[tx * 8 + t3], kx, corner_terms(zb, yb, fz, fy, t1 * 64))
                factor = jnp.exp(DRAG_POWER * jnp.log(eps))
                parts = []
                for c in range(3):
                    force = factor * slip_ref[c : c + 1, inner_at]
                    drag_ref[c : c + 1, at] = force
                    parts.append(kx * spread(force))
                found.append(deposit(parts, plane_weights(rows, zb, yb, fz, fy)))
            for k in range(UNROLL):
                tx, t3, t1 = brick_place(brick_ref[number * UNROLL + k + start])
                mine = (lane >> 6) == t1
                for c in range(3):
                    tile = (tx & 1) * 24 + c * 8 + t3
                    force_ref[tx >> 1, tile] += jnp.where(mine, found[k][8 * c : 8 * c + 8], 0.0)
            return carry

        lax.fori_loop(0, slip_ref.shape[1] // BLOCK // UNROLL, step, 0)
    copies = fetch([(force_ref.at[j, 0:48], out_hbm.at[j, 0:48]) for j in range(subs)], sems)
    zero = jnp.zeros((8, LANES), F32)
    more = []
    for j in range(subs):
        for quad in range(6):
            tiles = []
            for k in range(4):
                at = quad * 4 + k
                after = force_ref[j + 1, at] if j + 1 < subs else zero
                before = force_ref[j - 1, 24 + at] if j > 0 else zero
                tiles.append(jnp.where(rows < 4, after, before))
            for k, tile in enumerate(pack_halo(rows, tiles)):
                force_ref[j, 48 + quad * 3 + k] = tile
        copy = pltpu.make_async_copy(
            force_ref.at[j, 48:66], out_hbm.at[j, 48:66], sems.at[subs + j]
        )
        copy.start()
        more.append(copy)
    tick_ref[...] = zero
    for copy in copies + more:
        copy.wait()


def source_kernel(sub_ref, parts_ref, eps_ref, first_any, void_any, own_ref, low_ref, high_ref):
    lane, rows = lanes_iota(), rows_iota()
    sub = sub_ref[0]
    tiles_x = eps_ref.shape[0] // 8
    after = jnp.minimum(sub * 2 + 2, tiles_x - 1) * 8
    before = jnp.maximum(sub * 2 - 1, 0) * 8

    def summed(at):
        total = parts_ref[0, at]
        for j in range(1, parts_ref.shape[0]):
            total = total + parts_ref[j, at]
        return total

    for t in range(3):
        for c in range(3):
            if t < 2:
                forces = [summed(t * 24 + c * 8 + t3) for t3 in range(8)]
            else:
                forces = []
                for quad in (2 * c, 2 * c + 1):
                    forces += unpack_halo(rows, [summed(48 + quad * 3 + k) for k in range(3)])
            tiles = []
            for t3 in range(8):
                if t < 2:
                    eps = eps_ref[(sub * 2 + t) * 8 + t3]
                else:
                    eps = jnp.where(rows < 4, eps_ref[after + t3], eps_ref[before + t3])
                tiles.append(-forces[t3] / eps)
            tiles = transpose_granules(tiles, lane)
            first = 8 * (t + 1) % 24
            for z in range(8):
                own_ref[c, z, first : first + 8, :] = tiles[z]
                if z < 3:
                    low_ref[c, z, first : first + 8, :] = tiles[z]
                if z >= 5:
                    high_ref[c, z - 5, first : first + 8, :] = tiles[z]


def window_kernel(sub_ref, after_any, velocity_hbm, out_ref, top_ref, bottom_ref, sems):
    depth = velocity_hbm.shape[1]
    tiles_x = velocity_hbm.shape[2] // 8
    pairs, inside = [], []
    for r in range(4):
        want = sub_ref[0] * 2 + r - 1
        inside.append(jnp.logical_and(want >= 0, want < tiles_x))
        at = pl.ds(pl.multiple_of(jnp.clip(want, 0, tiles_x - 1) * 8, 8), 8)
        pairs.append((velocity_hbm.at[:, :, at, :], out_ref.at[:, :, 8 * r : 8 * r + 8, :]))
    for copy in fetch(pairs, sems):
        copy.wait()
    for r in range(4):
        at = slice(8 * r, 8 * r + 8)
        rows = jnp.where(inside[r], out_ref[:, :, at, :], 0.0)
        out_ref[:, :, at, :] = rows
        top_ref[:, :, at, :] = rows[:, depth - 4 :]
        bottom_ref[:, :, at, :] = rows[:, :4]


def void_kernel(after_any, eps_ref, out_ref, tick_ref):
    tick_ref[...] = jnp.zeros_like(tick_ref)
    lane = lanes_iota()

    def convert(number, carry):
        for k in range(4):
            tx = number * 4 + k
            tiles = transpose_granules([eps_ref[tx * 8 + t3] for t3 in range(8)], lane)
            for z in range(8):
                out_ref[z, pl.ds(pl.multiple_of(tx * 8, 8), 8), :] = tiles[z]
        return carry

    lax.fori_loop(0, out_ref.shape[1] // 32, convert, 0)


def edges(slab, sub, planes, width):
    row = lax.broadcasted_iota(jnp.int32, (32, LANES), 0) + sub * 16 - 8
    inside_x = jnp.logical_and(row >= 0, row < width)

    def keep(z):
        height = slab * 8 - 4 + z
        return jnp.logical_and(inside_x, jnp.logical_and(height >= 0, height < planes))

    return keep


def unforced(old, z, lane):
    shear = None
    centres, laps = [], []
    for c in range(3):
        centre = old[c, z]
        upper = old[c, z + 1]
        lower = old[c, z - 1]
        east = pltpu.roll(centre, 31, 0)
        west = pltpu.roll(centre, 1, 0)
        north = jnp.where(lane == LANES - 1, 0.0, pltpu.roll(centre, LANES - 1, 1))
        south = jnp.where(lane == 0, 0.0, pltpu.roll(centre, 1, 1))
        term = (upper - centre) ** 2 + (east - centre) ** 2 + (north - centre) ** 2
        shear = term if shear is None else shear + term
        centres.append(centre)
        laps.append(upper + lower + east + west + north + south - 6.0 * centre)
    viscous = (TIME_STEP * VISCOSITY) * jnp.exp(FLOW_POWER * jnp.log(shear + 0.01))
    return [centres[c] + viscous * laps[c] for c in range(3)]


def first_kernel(window_ref, below_ref, above_ref, out_ref, tick_ref, old):
    tick_ref[...] = jnp.zeros_like(tick_ref)
    old[:, 0:4] = below_ref[...]
    old[:, 4:12] = window_ref[...]
    old[:, 12:16] = above_ref[...]
    lane = lax.broadcasted_iota(jnp.int32, (32, LANES), 1)

    def plane(number, carry):
        for k in range(2):
            z = number * 2 + k
            moved = unforced(old, z + 1, lane)
            for c in range(3):
                out_ref[c, z] = moved[c]
        return carry

    lax.fori_loop(0, 7, plane, 0)


def stencil_kernel(
    place_ref, first_ref, own_ref, low_ref, high_ref, out_ref, even, odd, source
):
    keep = edges(place_ref[0], place_ref[1], place_ref[2], place_ref[3])
    lane = lax.broadcasted_iota(jnp.int32, (32, LANES), 1)
    for part, planes in ((low_ref, slice(0, 3)), (own_ref, slice(3, 11)), (high_ref, slice(11, 14))):
        source[:, planes, 0:24, :] = part[...]
        source[:, planes, 24:32, :] = part[:, :, 0:8, :]

    def first(number, carry):
        for k in range(2):
            z = number * 2 + k
            inside = keep(z + 1)
            for c in range(3):
                moved = first_ref[c, z] + TIME_STEP * source[c, z]
                odd[c, z + 1] = jnp.where(inside, moved, 0.0)
        return carry

    lax.fori_loop(0, 7, first, 0)
    buffers = (even, odd)
    for step in range(1, ITERS):
        old, new = buffers[step % 2], buffers[(step + 1) % 2]

        def plane(number, carry, old=old, new=new, step=step):
            for k in range(2):
                z = number * 2 + k + step + 1
                moved = unforced(old, z, lane)
                inside = keep(z)
                for c in range(3):
                    forced = moved[c] + TIME_STEP * source[c, z - 1]
                    new[c, z] = jnp.where(inside, forced, 0.0)
            return carry

        lax.fori_loop(0, 7 - step, plane, 0)
    for j in range(out_ref.shape[0]):
        out_ref[j] = even[:, 4:12, 8:24, :]


def place_kernel(parts_ref, out_ref, sems):
    rows = parts_ref.shape[3]
    copies = fetch(
        [
            (parts_ref.at[j], out_ref.at[:, :, pl.ds(j * rows, rows), :])
            for j in range(parts_ref.shape[0])
        ],
        sems,
    )
    for copy in copies:
        copy.wait()


def call(kernel, out_shapes, ins, scratch=(), outs=None, us=1.0, params=PARAMS):
    return pl.pallas_call(
        kernel,
        out_shape=[jax.ShapeDtypeStruct(s, F32) for s in out_shapes],
        in_specs=ins,
        out_specs=outs or [VMEM] * len(out_shapes),
        scratch_shapes=list(scratch),
        compiler_params=params,
        cost_estimate=pl.CostEstimate(flops=int(us * 1e9), bytes_accessed=int(us * 3.6e6), transcendentals=0),
    )


def shift(x, axis, up):
    peers = lax.axis_size(axis)
    pairs = [(i, i + 1) if up else (i + 1, i) for i in range(peers - 1)]
    return lax.ppermute(x, axis, pairs)


def body(velocity, part_vel, fraction, base_cell, drag_coeff, part_volume, brick_of_block):
    depth, width_x = velocity.shape[1], velocity.shape[2]
    blocks = brick_of_block.shape[0]
    subs = lax.axis_size("sub")
    slab = lax.axis_index("slab").astype(jnp.int32)
    sub = lax.axis_index("sub").astype(jnp.int32)
    tiles_x = width_x // 8
    tiles = tiles_x * 8
    share = tiles // subs
    base = base_cell.reshape(blocks, BLOCK)
    coef = drag_coeff.reshape(blocks, BLOCK)
    pvol = part_volume.reshape(blocks, BLOCK)

    particles_vmem = [
        pltpu.SMEM((blocks,), jnp.int32),
        pltpu.VMEM((blocks, BLOCK), jnp.int32),
        pltpu.VMEM((3, blocks * BLOCK), F32),
    ]
    row_vmem = pltpu.VMEM((blocks, BLOCK), F32)
    (solid,) = call(
        solid_kernel,
        [(tiles, 8, LANES)],
        [HBM] * 4,
        particles_vmem + [row_vmem, pltpu.SemaphoreType.DMA((4,))],
        us=5.0,
        params=FULL,
    )(brick_of_block, base, fraction, pvol)
    solid_parts = lax.all_to_all(solid.reshape(subs, share, 8, LANES), "sub", 0, 0)
    sub_at = sub.reshape(1)
    half = blocks // 2

    def slip_of(first, after):
        (slip,) = call(
            functools.partial(slip_kernel, first, half),
            [(3, half * BLOCK)],
            [ANY] + [HBM] * 7,
            [
                pltpu.SMEM((blocks,), jnp.int32),
                pltpu.VMEM((half, BLOCK), jnp.int32),
                pltpu.VMEM((3, half * BLOCK), F32),
                pltpu.VMEM((3, half * BLOCK), F32),
                pltpu.VMEM((half, BLOCK), F32),
                pltpu.VMEM((half, BLOCK), F32),
                pltpu.VMEM(velocity.shape, F32),
                pltpu.VMEM((3 * tiles, 8, LANES), F32),
                pltpu.SemaphoreType.DMA((7,)),
            ],
            us=5.0,
            params=FULL,
        )(after, brick_of_block, base, fraction, part_vel, coef, pvol, velocity)
        return slip

    slip_a = slip_of(0, solid)
    eps_own, eps_copies = call(
        eps_kernel, [(share, 8, LANES), (subs, share, 8, LANES)], [VMEM], us=0.5
    )(solid_parts)
    slip_b = slip_of(half, eps_own)
    eps = lax.all_to_all(eps_copies, "sub", 0, 0).reshape(tiles, 8, LANES)
    drag, force, drag_tick = call(
        drag_kernel,
        [(3, blocks * BLOCK), (subs, 66, 8, LANES), (8, LANES)],
        [SMEM, VMEM, VMEM, HBM, HBM, VMEM],
        [
            pltpu.VMEM((subs, 66, 8, LANES), F32),
            pltpu.VMEM((3, half * BLOCK), F32),
            pltpu.VMEM((3, half * BLOCK), F32),
            pltpu.SemaphoreType.DMA((2 * subs,)),
        ],
        outs=[VMEM, HBM, VMEM],
        us=6.0,
        params=FULL,
    )(brick_of_block, base, fraction, slip_a, slip_b, eps)
    force_parts = lax.all_to_all(force, "sub", 0, 0)
    window, top, bottom = call(
        window_kernel,
        [(3, depth, 32, LANES), (3, 4, 32, LANES), (3, 4, 32, LANES)],
        [SMEM, ANY, HBM],
        [pltpu.SemaphoreType.DMA((4,))],
    )(sub_at, drag_tick, velocity)
    below = shift(top, "slab", True)
    above = shift(bottom, "slab", False)
    voidfraction, void_tick = call(
        void_kernel, [(depth, width_x, LANES), (8, LANES)], [ANY, VMEM], us=2.0
    )(drag_tick, eps)
    first, first_tick = call(
        first_kernel,
        [(3, 14, 32, LANES), (8, LANES)],
        [VMEM] * 3,
        [pltpu.VMEM((3, 16, 32, LANES), F32)],
        us=1.0,
    )(window, below, above)

    rows = width_x // subs
    own, low_own, high_own = call(
        source_kernel,
        [(3, depth, 24, LANES), (3, 3, 24, LANES), (3, 3, 24, LANES)],
        [SMEM, VMEM, VMEM, ANY, ANY],
    )(sub_at, force_parts, eps, first_tick, void_tick)
    low = shift(high_own, "slab", True)
    high = shift(low_own, "slab", False)
    planes = depth * lax.axis_size("slab")
    place = jnp.stack([slab, sub, jnp.int32(planes), jnp.int32(width_x)])
    (moved,) = call(
        stencil_kernel,
        [(subs, 3, depth, rows, LANES)],
        [SMEM] + [VMEM] * 4,
        [
            pltpu.VMEM((3, 16, 32, LANES), F32),
            pltpu.VMEM((3, 16, 32, LANES), F32),
            pltpu.VMEM((3, 14, 32, LANES), F32),
        ],
        us=4.0,
    )(place, first, own, low, high)
    moved = lax.all_to_all(moved, "sub", 0, 0)
    (new_velocity,) = call(
        place_kernel,
        [velocity.shape],
        [ANY],
        [pltpu.SemaphoreType.DMA((subs,))],
        outs=[ANY],
    )(moved)
    return new_velocity, voidfraction, drag


def solution(mesh):
    in_specs = (
        P(None, "slab", None, None),
        P(None, ("slab", "sub")),
        P(None, ("slab", "sub")),
        P(("slab", "sub")),
        P(("slab", "sub")),
        P(("slab", "sub")),
        P(("slab", "sub")),
    )
    out_specs = (P(None, "slab", None, None), P("slab", None, None), P(None, ("slab", "sub")))
    return jax.shard_map(body, mesh=mesh, in_specs=in_specs, out_specs=out_specs, check_vma=False)
```

```python
import functools

import jax
import jax.numpy as jnp
from jax import lax
from jax.experimental import pallas as pl
from jax.experimental.pallas import tpu as pltpu
from jax.sharding import PartitionSpec as P

BLOCK = 128
LANES = 128
EPS_MIN = 0.35
FLOW_POWER = -0.2
DRAG_POWER = -2.65
VISCOSITY = 1.2
TIME_STEP = 0.05
ITERS = 4
OUTER = (0, 1, 2, 5, 6, 7)
INNER = (3, 4)
UNROLL = 16
F32 = jnp.float32
PARAMS = pltpu.CompilerParams(vmem_limit_bytes=16 * 1024 * 1024)
VMEM = pl.BlockSpec(memory_space=pltpu.VMEM)
SMEM = pl.BlockSpec(memory_space=pltpu.SMEM)
HBM = pl.BlockSpec(memory_space=pltpu.HBM)
ANY = pl.BlockSpec(memory_space=pl.ANY)


def transpose_granules(tiles, lane):
    for bit in (1, 2, 4):
        shift = 8 * bit
        high = (lane & shift) != 0
        new = list(tiles)
        for a in range(8):
            if a & bit:
                continue
            b = a | bit
            va, vb = tiles[a], tiles[b]
            new[a] = jnp.where(high, pltpu.roll(vb, shift, 1), va)
            new[b] = jnp.where(high, vb, pltpu.roll(va, LANES - shift, 1))
        tiles = new
    return tiles


def fetch(pairs, sems):
    copies = [pltpu.make_async_copy(a, b, sems.at[i]) for i, (a, b) in enumerate(pairs)]
    for copy in copies:
        copy.start()
    return copies


def lanes_iota():
    return lax.broadcasted_iota(jnp.int32, (8, LANES), 1)


def rows_iota():
    return lax.broadcasted_iota(jnp.int32, (8, LANES), 0)


def spread(row):
    return jnp.broadcast_to(row, (8, LANES))


def particles(base_ref, frac_ref, block):
    at = pl.ds(pl.multiple_of(block * BLOCK, BLOCK), BLOCK)
    base = spread(base_ref[pl.ds(block, 1), :])
    fz = spread(frac_ref[0:1, at])
    fx = spread(frac_ref[1:2, at])
    fy = spread(frac_ref[2:3, at])
    return at, base >> 6, (base >> 3) & 7, base & 7, fz, fx, fy


def axis_weights(rows, first, frac):
    zero = jnp.zeros_like(frac)
    return jnp.where(rows == first, 1.0 - frac, jnp.where(rows == first + 1, frac, zero))


def halves(value):
    high = value.astype(jnp.bfloat16).astype(F32)
    return high, value - high


def plane_weights(rows, zb, yb, fz, fy):
    ky = axis_weights(rows, yb, fy)
    zero = jnp.zeros_like(fz)
    at = [zb == z for z in range(7)]
    parts = []
    for here, above in zip(halves((1.0 - fz) * ky), halves(fz * ky)):
        for z in range(8):
            part = zero if z == 0 else jnp.where(at[z - 1], above, zero)
            parts.append(part if z == 7 else jnp.where(at[z], here, part))
    return jnp.concatenate(parts, axis=0).astype(jnp.bfloat16)


def split_rows(parts):
    full = jnp.concatenate(parts, axis=0)
    high = full.astype(jnp.bfloat16).astype(F32)
    return jnp.concatenate([high, full - high], axis=0).astype(jnp.bfloat16)


def deposit(parts, weights):
    left = split_rows(parts)
    both = lax.dot_general(
        left, weights, (((1,), (1,)), ((), ())), preferred_element_type=F32
    )
    half = both.shape[0] // 2
    both = both[:half] + both[half:]
    return both + pltpu.roll(both, 64, 1)


def corner_terms(zb, yb, fz, fy, offset):
    index = (zb << 3) + yb + offset
    gz, gy = 1.0 - fz, 1.0 - fy
    return (
        (index, gz * gy),
        (index + 1, gz * fy),
        (index + 8, fz * gy),
        (index + 9, fz * fy),
    )


def interpolate(tile, kx, corners):
    total = None
    for index, weight in corners:
        term = weight * jnp.take_along_axis(tile, index, axis=1, mode="promise_in_bounds")
        total = term if total is None else total + term
    return jnp.sum(kx * total, axis=0, keepdims=True)


def brick_place(brick):
    return brick >> 4, brick & 7, (brick >> 3) & 1


def solid_kernel(
    brick_hbm, base_hbm, frac_hbm, pvol_hbm, out_hbm,
    out_ref, brick_ref, base_ref, frac_ref, pvol_ref, sems,
):
    copies = fetch(
        [(brick_hbm, brick_ref), (base_hbm, base_ref), (frac_hbm, frac_ref), (pvol_hbm, pvol_ref)],
        sems,
    )
    out_ref[...] = jnp.zeros_like(out_ref)
    for copy in copies:
        copy.wait()
    rows, lane = rows_iota(), lanes_iota()

    def step(number, carry):
        found = []
        for k in range(UNROLL):
            block = number * UNROLL + k
            _, zb, xb, yb, fz, fx, fy = particles(base_ref, frac_ref, block)
            kx = axis_weights(rows, xb, fx) * spread(pvol_ref[pl.ds(block, 1), :])
            found.append(deposit([kx], plane_weights(rows, zb, yb, fz, fy)))
        for k in range(UNROLL):
            tx, t3, t1 = brick_place(brick_ref[number * UNROLL + k])
            tile = tx * 8 + t3
            out_ref[tile] += jnp.where((lane >> 6) == t1, found[k], 0.0)
        return carry

    lax.fori_loop(0, base_ref.shape[0] // UNROLL, step, 0)
    (copy,) = fetch([(out_ref, out_hbm)], sems)
    copy.wait()


def eps_kernel(parts_ref, copies_hbm, out_ref, sems):
    total = parts_ref[0]
    for j in range(1, parts_ref.shape[0]):
        total = total + parts_ref[j]
    total = jnp.maximum(1.0 - total, EPS_MIN)
    out_ref[...] = total
    for copy in fetch([(out_ref, copies_hbm.at[j]) for j in range(copies_hbm.shape[0])], sems):
        copy.wait()


def slip_kernel(
    first, count,
    after_any, brick_hbm, base_hbm, frac_hbm, pvel_hbm, coef_hbm, pvol_hbm, velocity_hbm,
    out_any,
    out_ref, brick_ref, base_ref, frac_ref, pvel_ref, coef_ref, pvol_ref, velocity_ref, table_ref, sems,
):
    some = pl.ds(first, count)
    wide = pl.ds(first * BLOCK, count * BLOCK)
    copies = fetch(
        [
            (velocity_hbm, velocity_ref),
            (brick_hbm, brick_ref),
            (base_hbm.at[some], base_ref),
            (frac_hbm.at[:, wide], frac_ref),
            (pvel_hbm.at[:, wide], pvel_ref),
            (coef_hbm.at[some], coef_ref),
            (pvol_hbm.at[some], pvol_ref),
        ],
        sems,
    )
    rows, lane = rows_iota(), lanes_iota()
    tiles_x = velocity_ref.shape[2] // 8

    def convert(number, carry):
        for k in range(2):
            tx = number * 2 + k
            at = pl.ds(pl.multiple_of(tx * 8, 8), 8)
            for c in range(3):
                tiles = transpose_granules([velocity_ref[c, z, at, :] for z in range(8)], lane)
                for t3 in range(8):
                    table_ref[(tx * 3 + c) * 8 + t3] = tiles[t3]
        return carry

    copies[0].wait()
    lax.fori_loop(0, tiles_x // 2, convert, 0)
    for copy in copies[1:]:
        copy.wait()

    def step(number, carry):
        for k in range(UNROLL):
            block = number * UNROLL + k
            at, zb, xb, yb, fz, fx, fy = particles(base_ref, frac_ref, block)
            tx, t3, t1 = brick_place(brick_ref[first + block])
            kx = axis_weights(rows, xb, fx)
            corners = corner_terms(zb, yb, fz, fy, t1 * 64)
            rel = [
                interpolate(table_ref[(tx * 3 + c) * 8 + t3], kx, corners) - pvel_ref[c : c + 1, at]
                for c in range(3)
            ]
            speed = rel[0] * rel[0] + rel[1] * rel[1] + rel[2] * rel[2]
            factor = coef_ref[pl.ds(block, 1), :] * pvol_ref[pl.ds(block, 1), :]
            factor = factor * jnp.exp(FLOW_POWER * jnp.log(speed + 0.01))
            for c in range(3):
                out_ref[c : c + 1, at] = factor * rel[c]
        return carry

    lax.fori_loop(0, count // UNROLL, step, 0)
    (copy,) = fetch([(out_ref, out_any)], sems)
    copy.wait()


def pack_halo(rows, tiles):
    a, b, c, d = tiles
    middle = jnp.logical_or(rows == 3, rows == 4)
    first = jnp.where(middle, pltpu.roll(d, 3, 0), a)
    second = jnp.where(rows == 3, pltpu.roll(d, 1, 0), jnp.where(rows == 4, pltpu.roll(d, 7, 0), b))
    third = jnp.where(middle, pltpu.roll(d, 5, 0), c)
    return first, second, third


def unpack_halo(rows, tiles):
    a, b, c = tiles
    inner = jnp.where(rows == 2, pltpu.roll(b, 7, 0), pltpu.roll(b, 1, 0))
    d = jnp.where(rows < 2, pltpu.roll(a, 5, 0), jnp.where(rows > 5, pltpu.roll(c, 3, 0), inner))
    return a, b, c, d


def pack_all(rows, tiles):
    packed = []
    for quad in range(len(tiles) // 4):
        packed += pack_halo(rows, tiles[quad * 4 : quad * 4 + 4])
    return packed + tiles[len(tiles) // 4 * 4 :]


def unpack_all(rows, packed, count):
    tiles = []
    for quad in range(count // 4):
        tiles += unpack_halo(rows, packed[quad * 3 : quad * 3 + 3])
    return tiles + packed[count // 4 * 3 :]


def drag_kernel(
    brick_ref, base_ref, frac_ref, slip_a_hbm, slip_b_ref, eps_ref,
    drag_ref, outer_hbm, inner_hbm, tick_ref,
    force_ref, outer_ref, inner_ref, slip_a_ref, sems,
):
    subs = force_ref.shape[0]
    rows, lane = rows_iota(), lanes_iota()
    (copy,) = fetch([(slip_a_hbm, slip_a_ref)], sems)
    for j in range(subs):
        force_ref[j] = jnp.zeros(force_ref.shape[1:], F32)
    copy.wait()

    for slip_ref, start in ((slip_a_ref, 0), (slip_b_ref, slip_a_ref.shape[1] // BLOCK)):

        def step(number, carry, slip_ref=slip_ref, start=start):
            found = []
            for k in range(UNROLL):
                inner = number * UNROLL + k
                block = inner + start
                at, zb, xb, yb, fz, fx, fy = particles(base_ref, frac_ref, block)
                inner_at = pl.ds(pl.multiple_of(inner * BLOCK, BLOCK), BLOCK)
                tx, t3, t1 = brick_place(brick_ref[block])
                kx = axis_weights(rows, xb, fx)
                eps = interpolate(eps_ref[tx * 8 + t3], kx, corner_terms(zb, yb, fz, fy, t1 * 64))
                factor = jnp.exp(DRAG_POWER * jnp.log(eps))
                parts = []
                for c in range(3):
                    force = factor * slip_ref[c : c + 1, inner_at]
                    drag_ref[c : c + 1, at] = force
                    parts.append(kx * spread(force))
                found.append(deposit(parts, plane_weights(rows, zb, yb, fz, fy)))
            for k in range(UNROLL):
                tx, t3, t1 = brick_place(brick_ref[number * UNROLL + k + start])
                mine = (lane >> 6) == t1
                for c in range(3):
                    tile = (tx & 1) * 24 + c * 8 + t3
                    force_ref[tx >> 1, tile] += jnp.where(mine, found[k][8 * c : 8 * c + 8], 0.0)
            return carry

        lax.fori_loop(0, slip_ref.shape[1] // BLOCK // UNROLL, step, 0)

    def convert(j, carry):
        for c in range(3):
            for t in range(2):
                tiles = [force_ref[j, t * 24 + c * 8 + t3] for t3 in range(8)]
                tiles = transpose_granules(tiles, lane)
                for ref, planes in ((outer_ref, OUTER), (inner_ref, INNER)):
                    for n, z in enumerate(planes):
                        ref[j, (c * 2 + t) * len(planes) + n] = tiles[z]
        return carry

    lax.fori_loop(0, subs, convert, 0)
    copies = []
    zero = jnp.zeros((8, LANES), F32)
    for j in range(subs):
        for ref, out_hbm, planes in ((outer_ref, outer_hbm, OUTER), (inner_ref, inner_hbm, INNER)):
            size = len(planes)
            tiles = []
            for c in range(3):
                for n in range(size):
                    after = ref[j + 1, c * 2 * size + n] if j + 1 < subs else zero
                    before = ref[j - 1, (c * 2 + 1) * size + n] if j > 0 else zero
                    tiles.append(jnp.where(rows < 4, after, before))
            for n, tile in enumerate(pack_all(rows, tiles)):
                ref[j, 6 * size + n] = tile
            copy = pltpu.make_async_copy(ref.at[j], out_hbm.at[j], sems.at[len(copies)])
            copy.start()
            copies.append(copy)
    tick_ref[...] = zero
    for copy in copies:
        copy.wait()


def source_kernel(planes, void_ref, first_any, parts_ref, *out_refs):
    rows = rows_iota()
    size = len(planes)

    def summed(at):
        total = parts_ref[0, at]
        for j in range(1, parts_ref.shape[0]):
            total = total + parts_ref[j, at]
        return total

    packed = [summed(at) for at in range(6 * size, parts_ref.shape[1])]
    halo = unpack_all(rows, packed, 3 * size)
    for n, z in enumerate(planes):
        out_ref, at = out_refs[n // 3], n % 3
        for c in range(3):
            forces = [halo[c * size + n]] + [summed((c * 2 + t) * size + n) for t in range(2)]
            for t, force in enumerate(forces):
                part = slice(8 * t, 8 * t + 8)
                out_ref[c, at, part, :] = -force / void_ref[z, part, :]


def window_kernel(sub_ref, after_any, velocity_hbm, out_ref, top_ref, bottom_ref, sems):
    depth = velocity_hbm.shape[1]
    tiles_x = velocity_hbm.shape[2] // 8
    pairs, inside = [], []
    for r in range(4):
        want = sub_ref[0] * 2 + r - 1
        inside.append(jnp.logical_and(want >= 0, want < tiles_x))
        at = pl.ds(pl.multiple_of(jnp.clip(want, 0, tiles_x - 1) * 8, 8), 8)
        pairs.append((velocity_hbm.at[:, :, at, :], out_ref.at[:, :, 8 * r : 8 * r + 8, :]))
    for copy in fetch(pairs, sems):
        copy.wait()
    for r in range(4):
        at = slice(8 * r, 8 * r + 8)
        rows = jnp.where(inside[r], out_ref[:, :, at, :], 0.0)
        out_ref[:, :, at, :] = rows
        top_ref[:, :, at, :] = rows[:, depth - 4 :]
        bottom_ref[:, :, at, :] = rows[:, :4]


def void_kernel(sub_ref, after_any, eps_ref, out_ref, window_ref):
    lane, rows = lanes_iota(), rows_iota()
    tiles_x = out_ref.shape[1] // 8

    def convert(number, carry):
        for k in range(4):
            tx = number * 4 + k
            tiles = transpose_granules([eps_ref[tx * 8 + t3] for t3 in range(8)], lane)
            for z in range(8):
                out_ref[z, pl.ds(pl.multiple_of(tx * 8, 8), 8), :] = tiles[z]
        return carry

    lax.fori_loop(0, tiles_x // 4, convert, 0)
    own = sub_ref[0] * 2

    def tile(tx):
        return out_ref[:, pl.ds(pl.multiple_of(tx * 8, 8), 8), :]

    after, before = tile(jnp.minimum(own + 2, tiles_x - 1)), tile(jnp.maximum(own - 1, 0))
    window_ref[:, 0:8, :] = jnp.where(rows[None] < 4, after, before)
    window_ref[:, 8:16, :] = tile(own)
    window_ref[:, 16:24, :] = tile(own + 1)


def edges(slab, sub, planes, width):
    row = lax.broadcasted_iota(jnp.int32, (32, LANES), 0) + sub * 16 - 8
    inside_x = jnp.logical_and(row >= 0, row < width)

    def keep(z):
        height = slab * 8 - 4 + z
        return jnp.logical_and(inside_x, jnp.logical_and(height >= 0, height < planes))

    return keep


def unforced(old, z, lane):
    shear = None
    centres, laps = [], []
    for c in range(3):
        centre = old[c, z]
        upper = old[c, z + 1]
        lower = old[c, z - 1]
        east = pltpu.roll(centre, 31, 0)
        west = pltpu.roll(centre, 1, 0)
        north = jnp.where(lane == LANES - 1, 0.0, pltpu.roll(centre, LANES - 1, 1))
        south = jnp.where(lane == 0, 0.0, pltpu.roll(centre, 1, 1))
        term = (upper - centre) ** 2 + (east - centre) ** 2 + (north - centre) ** 2
        shear = term if shear is None else shear + term
        centres.append(centre)
        laps.append(upper + lower + east + west + north + south - 6.0 * centre)
    viscous = (TIME_STEP * VISCOSITY) * jnp.exp(FLOW_POWER * jnp.log(shear + 0.01))
    return [centres[c] + viscous * laps[c] for c in range(3)]


def first_kernel(window_ref, below_ref, above_ref, out_ref, tick_ref, old):
    tick_ref[...] = jnp.zeros_like(tick_ref)
    old[:, 0:4] = below_ref[...]
    old[:, 4:12] = window_ref[...]
    old[:, 12:16] = above_ref[...]
    lane = lax.broadcasted_iota(jnp.int32, (32, LANES), 1)

    def plane(number, carry):
        for k in range(2):
            z = number * 2 + k
            moved = unforced(old, z + 1, lane)
            for c in range(3):
                out_ref[c, z] = moved[c]
        return carry

    lax.fori_loop(0, 7, plane, 0)


def stencil_kernel(
    place_ref, first_ref, below_ref, low_ref, inner_ref, high_ref, above_ref, out_ref, even, odd, source
):
    keep = edges(place_ref[0], place_ref[1], place_ref[2], place_ref[3])
    lane = lax.broadcasted_iota(jnp.int32, (32, LANES), 1)
    start = 0
    for part in (below_ref, low_ref, inner_ref, high_ref, above_ref):
        planes = slice(start, start + part.shape[1])
        source[:, planes, 0:24, :] = part[...]
        source[:, planes, 24:32, :] = part[:, :, 0:8, :]
        start += part.shape[1]

    def first(number, carry):
        for k in range(2):
            z = number * 2 + k
            inside = keep(z + 1)
            for c in range(3):
                moved = first_ref[c, z] + TIME_STEP * source[c, z]
                odd[c, z + 1] = jnp.where(inside, moved, 0.0)
        return carry

    lax.fori_loop(0, 7, first, 0)
    buffers = (even, odd)
    for step in range(1, ITERS):
        old, new = buffers[step % 2], buffers[(step + 1) % 2]

        def plane(number, carry, old=old, new=new, step=step):
            for k in range(2):
                z = number * 2 + k + step + 1
                moved = unforced(old, z, lane)
                inside = keep(z)
                for c in range(3):
                    forced = moved[c] + TIME_STEP * source[c, z - 1]
                    new[c, z] = jnp.where(inside, forced, 0.0)
            return carry

        lax.fori_loop(0, 7 - step, plane, 0)
    for j in range(out_ref.shape[0]):
        out_ref[j] = even[:, 4:12, 8:24, :]


def place_kernel(parts_ref, out_ref, sems):
    rows = parts_ref.shape[3]
    pairs = []
    for j in range(parts_ref.shape[0]):
        pairs.append((parts_ref.at[j], out_ref.at[:, :, j * rows : (j + 1) * rows, :]))
    for copy in fetch(pairs, sems):
        copy.wait()


def pinned(*arrays):
    return [pltpu.with_memory_space_constraint(x, pltpu.HBM) for x in arrays]


def call(kernel, out_shapes, ins, scratch=(), outs=None, us=1.0):
    outs = outs or [VMEM] * len(out_shapes)
    return pl.pallas_call(
        kernel,
        out_shape=[
            pltpu.HBM(s, F32) if spec is HBM else jax.ShapeDtypeStruct(s, F32)
            for s, spec in zip(out_shapes, outs)
        ],
        in_specs=ins,
        out_specs=outs,
        scratch_shapes=list(scratch),
        compiler_params=PARAMS,
        cost_estimate=pl.CostEstimate(flops=int(us * 1e9), bytes_accessed=int(us * 3.6e6), transcendentals=0),
    )


def shift(x, axis, up):
    peers = lax.axis_size(axis)
    pairs = [(i, i + 1) if up else (i + 1, i) for i in range(peers - 1)]
    return lax.ppermute(x, axis, pairs)


def body(velocity, part_vel, fraction, base_cell, drag_coeff, part_volume, brick_of_block):
    depth, width_x = velocity.shape[1], velocity.shape[2]
    blocks = brick_of_block.shape[0]
    subs = lax.axis_size("sub")
    slab = lax.axis_index("slab").astype(jnp.int32)
    sub = lax.axis_index("sub").astype(jnp.int32)
    tiles_x = width_x // 8
    tiles = tiles_x * 8
    share = tiles // subs
    base = base_cell.reshape(blocks, BLOCK)
    coef = drag_coeff.reshape(blocks, BLOCK)
    pvol = part_volume.reshape(blocks, BLOCK)

    particles_vmem = [
        pltpu.SMEM((blocks,), jnp.int32),
        pltpu.VMEM((blocks, BLOCK), jnp.int32),
        pltpu.VMEM((3, blocks * BLOCK), F32),
    ]
    row_vmem = pltpu.VMEM((blocks, BLOCK), F32)
    (solid,) = call(
        solid_kernel,
        [(tiles, 8, LANES)],
        [HBM] * 4,
        [pltpu.VMEM((tiles, 8, LANES), F32)]
        + particles_vmem
        + [row_vmem, pltpu.SemaphoreType.DMA((4,))],
        outs=[HBM],
        us=5.0,
    )(*pinned(brick_of_block, base, fraction, pvol))
    solid_parts = lax.all_to_all(solid.reshape(subs, share, 8, LANES), "sub", 0, 0)
    sub_at = sub.reshape(1)
    half = blocks // 2

    def slip_of(first, after, out):
        (slip,) = call(
            functools.partial(slip_kernel, first, half),
            [(3, half * BLOCK)],
            [HBM] * 8,
            [
                pltpu.VMEM((3, half * BLOCK), F32),
                pltpu.SMEM((blocks,), jnp.int32),
                pltpu.VMEM((half, BLOCK), jnp.int32),
                pltpu.VMEM((3, half * BLOCK), F32),
                pltpu.VMEM((3, half * BLOCK), F32),
                pltpu.VMEM((half, BLOCK), F32),
                pltpu.VMEM((half, BLOCK), F32),
                pltpu.VMEM(velocity.shape, F32),
                pltpu.VMEM((3 * tiles, 8, LANES), F32),
                pltpu.SemaphoreType.DMA((7,)),
            ],
            us=5.0,
            )(after, brick_of_block, base, fraction, part_vel, coef, pvol, velocity)
        return slip

    slip_a = slip_of(0, solid, HBM)
    (eps_copies,) = call(
        eps_kernel,
        [(subs, share, 8, LANES)],
        [VMEM],
        [pltpu.VMEM((share, 8, LANES), F32), pltpu.SemaphoreType.DMA((subs,))],
        outs=[HBM],
        us=0.5,
    )(solid_parts)
    slip_b = slip_of(half, eps_copies, ANY)
    eps = lax.all_to_all(eps_copies, "sub", 0, 0).reshape(tiles, 8, LANES)
    outer_tiles = 6 * len(OUTER) + 14
    inner_tiles = 6 * len(INNER) + 5
    drag, outer, inner, tick = call(
        drag_kernel,
        [
            (3, blocks * BLOCK),
            (subs, outer_tiles, 8, LANES),
            (subs, inner_tiles, 8, LANES),
            (8, LANES),
        ],
        [SMEM, VMEM, VMEM, HBM, VMEM, VMEM],
        [
            pltpu.VMEM((subs, 48, 8, LANES), F32),
            pltpu.VMEM((subs, outer_tiles, 8, LANES), F32),
            pltpu.VMEM((subs, inner_tiles, 8, LANES), F32),
            pltpu.VMEM((3, half * BLOCK), F32),
            pltpu.SemaphoreType.DMA((2 * subs,)),
        ],
        outs=[VMEM, HBM, HBM, VMEM],
        us=7.0,
    )(brick_of_block, base, fraction, *pinned(slip_a), slip_b, eps)
    outer = lax.all_to_all(outer, "sub", 0, 0)
    inner = lax.all_to_all(inner, "sub", 0, 0)
    window, top, bottom = call(
        window_kernel,
        [(3, depth, 32, LANES), (3, 4, 32, LANES), (3, 4, 32, LANES)],
        [SMEM, ANY, HBM],
        [pltpu.SemaphoreType.DMA((4,))],
    )(sub_at, tick, *pinned(velocity))
    below = shift(top, "slab", True)
    above = shift(bottom, "slab", False)
    voidfraction, void_window = call(
        void_kernel, [(depth, width_x, LANES), (depth, 24, LANES)], [SMEM, ANY, VMEM], us=2.0
    )(sub_at, tick, eps)
    first, first_tick = call(
        first_kernel,
        [(3, 14, 32, LANES), (8, LANES)],
        [VMEM] * 3,
        [pltpu.VMEM((3, 16, 32, LANES), F32)],
        us=1.0,
    )(window, below, above)

    rows = width_x // subs
    low_own, high_own = call(
        functools.partial(source_kernel, OUTER), [(3, 3, 24, LANES)] * 2, [VMEM, ANY, VMEM]
    )(void_window, first_tick, outer)
    below = shift(high_own, "slab", True)
    above = shift(low_own, "slab", False)
    (inner_own,) = call(
        functools.partial(source_kernel, INNER), [(3, 2, 24, LANES)], [VMEM, ANY, VMEM]
    )(void_window, low_own, inner)
    planes = depth * lax.axis_size("slab")
    place = jnp.stack([slab, sub, jnp.int32(planes), jnp.int32(width_x)])
    (moved,) = call(
        stencil_kernel,
        [(subs, 3, depth, rows, LANES)],
        [SMEM] + [VMEM] * 6,
        [
            pltpu.VMEM((3, 16, 32, LANES), F32),
            pltpu.VMEM((3, 16, 32, LANES), F32),
            pltpu.VMEM((3, 14, 32, LANES), F32),
        ],
        us=4.0,
    )(place, first, below, low_own, inner_own, high_own, above)
    moved = lax.all_to_all(moved, "sub", 0, 0)
    (new_velocity,) = call(
        place_kernel,
        [velocity.shape],
        [ANY],
        [pltpu.SemaphoreType.DMA((subs,))],
        outs=[HBM],
    )(moved)
    return new_velocity, voidfraction, drag


def solution(mesh):
    in_specs = (
        P(None, "slab", None, None),
        P(None, ("slab", "sub")),
        P(None, ("slab", "sub")),
        P(("slab", "sub")),
        P(("slab", "sub")),
        P(("slab", "sub")),
        P(("slab", "sub")),
    )
    out_specs = (P(None, "slab", None, None), P("slab", None, None), P(None, ("slab", "sub")))
    return jax.shard_map(body, mesh=mesh, in_specs=in_specs, out_specs=out_specs, check_vma=False)
```

```python
import functools

import jax
import jax.numpy as jnp
from jax import lax
from jax.experimental import pallas as pl
from jax.experimental.pallas import tpu as pltpu
from jax.sharding import PartitionSpec as P

BLOCK = 128
LANES = 128
EPS_MIN = 0.35
FLOW_POWER = -0.2
DRAG_POWER = -2.65
VISCOSITY = 1.2
TIME_STEP = 0.05
ITERS = 4
UNROLL = 16
F32 = jnp.float32
PARAMS = pltpu.CompilerParams(vmem_limit_bytes=16 * 1024 * 1024)
VMEM = pl.BlockSpec(memory_space=pltpu.VMEM)
SMEM = pl.BlockSpec(memory_space=pltpu.SMEM)
HBM = pl.BlockSpec(memory_space=pltpu.HBM)
ANY = pl.BlockSpec(memory_space=pl.ANY)


def transpose_granules(tiles, lane):
    for bit in (1, 2, 4):
        shift = 8 * bit
        high = (lane & shift) != 0
        new = list(tiles)
        for a in range(8):
            if a & bit:
                continue
            b = a | bit
            va, vb = tiles[a], tiles[b]
            new[a] = jnp.where(high, pltpu.roll(vb, shift, 1), va)
            new[b] = jnp.where(high, vb, pltpu.roll(va, LANES - shift, 1))
        tiles = new
    return tiles


def fetch(pairs, sems):
    copies = [pltpu.make_async_copy(a, b, sems.at[i]) for i, (a, b) in enumerate(pairs)]
    for copy in copies:
        copy.start()
    return copies


def lanes_iota():
    return lax.broadcasted_iota(jnp.int32, (8, LANES), 1)


def rows_iota():
    return lax.broadcasted_iota(jnp.int32, (8, LANES), 0)


def spread(row):
    return jnp.broadcast_to(row, (8, LANES))


def particles(base_ref, frac_ref, block):
    at = pl.ds(pl.multiple_of(block * BLOCK, BLOCK), BLOCK)
    base = spread(base_ref[pl.ds(block, 1), :])
    fz = spread(frac_ref[0:1, at])
    fx = spread(frac_ref[1:2, at])
    fy = spread(frac_ref[2:3, at])
    return at, base >> 6, (base >> 3) & 7, base & 7, fz, fx, fy


def axis_weights(rows, first, frac):
    zero = jnp.zeros_like(frac)
    return jnp.where(rows == first, 1.0 - frac, jnp.where(rows == first + 1, frac, zero))


def halves(value):
    high = value.astype(jnp.bfloat16).astype(F32)
    return high, value - high


def plane_weights(rows, zb, yb, fz, fy):
    ky = axis_weights(rows, yb, fy)
    zero = jnp.zeros_like(fz)
    at = [zb == z for z in range(7)]
    parts = []
    for here, above in zip(halves((1.0 - fz) * ky), halves(fz * ky)):
        for z in range(8):
            part = zero if z == 0 else jnp.where(at[z - 1], above, zero)
            parts.append(part if z == 7 else jnp.where(at[z], here, part))
    return jnp.concatenate(parts, axis=0).astype(jnp.bfloat16)


def split_rows(parts):
    full = jnp.concatenate(parts, axis=0)
    high = full.astype(jnp.bfloat16).astype(F32)
    return jnp.concatenate([high, full - high], axis=0).astype(jnp.bfloat16)


def deposit(blocks):
    left = []
    for n, (parts, _) in enumerate(blocks):
        rows = split_rows(parts)
        pair = [rows, jnp.zeros_like(rows)]
        left.append(jnp.concatenate(pair if n == 0 else pair[::-1], axis=1))
    both = lax.dot_general(
        jnp.concatenate(left, axis=0),
        jnp.concatenate([weights for _, weights in blocks], axis=1),
        (((1,), (1,)), ((), ())),
        preferred_element_type=F32,
    )
    half = both.shape[0] // 4
    found = []
    for n in range(2):
        total = both[2 * n * half : (2 * n + 1) * half] + both[(2 * n + 1) * half : (2 * n + 2) * half]
        found.append(total + pltpu.roll(total, 64, 1))
    return found


def corner_terms(zb, yb, fz, fy, offset):
    index = (zb << 3) + yb + offset
    gz, gy = 1.0 - fz, 1.0 - fy
    return (
        (index, gz * gy),
        (index + 1, gz * fy),
        (index + 8, fz * gy),
        (index + 9, fz * fy),
    )


def interpolate(tile, kx, corners):
    total = None
    for index, weight in corners:
        term = weight * jnp.take_along_axis(tile, index, axis=1, mode="promise_in_bounds")
        total = term if total is None else total + term
    return jnp.sum(kx * total, axis=0, keepdims=True)


def brick_place(brick):
    return brick >> 4, brick & 7, (brick >> 3) & 1


def solid_kernel(
    brick_hbm, base_hbm, frac_hbm, pvol_hbm, out_hbm,
    out_ref, brick_ref, base_ref, frac_ref, pvol_ref, sems,
):
    copies = fetch(
        [(brick_hbm, brick_ref), (base_hbm, base_ref), (frac_hbm, frac_ref), (pvol_hbm, pvol_ref)],
        sems,
    )
    out_ref[...] = jnp.zeros_like(out_ref)
    for copy in copies:
        copy.wait()
    rows, lane = rows_iota(), lanes_iota()

    def step(number, carry):
        found = []
        for k in range(UNROLL):
            block = number * UNROLL + k
            _, zb, xb, yb, fz, fx, fy = particles(base_ref, frac_ref, block)
            kx = axis_weights(rows, xb, fx) * spread(pvol_ref[pl.ds(block, 1), :])
            found.append(([kx], plane_weights(rows, zb, yb, fz, fy)))
        found = sum((deposit(found[k : k + 2]) for k in range(0, UNROLL, 2)), [])
        for k in range(UNROLL):
            tx, t3, t1 = brick_place(brick_ref[number * UNROLL + k])
            tile = tx * 8 + t3
            out_ref[tile] += jnp.where((lane >> 6) == t1, found[k], 0.0)
        return carry

    lax.fori_loop(0, base_ref.shape[0] // UNROLL, step, 0)
    (copy,) = fetch([(out_ref, out_hbm)], sems)
    copy.wait()


def eps_kernel(parts_ref, copies_hbm, out_ref, sems):
    total = parts_ref[0]
    for j in range(1, parts_ref.shape[0]):
        total = total + parts_ref[j]
    total = jnp.maximum(1.0 - total, EPS_MIN)
    out_ref[...] = total
    for copy in fetch([(out_ref, copies_hbm.at[j]) for j in range(copies_hbm.shape[0])], sems):
        copy.wait()


def slip_kernel(
    first, count,
    after_any, brick_hbm, base_hbm, frac_hbm, pvel_hbm, coef_hbm, pvol_hbm, velocity_hbm,
    out_any,
    out_ref, brick_ref, base_ref, frac_ref, pvel_ref, coef_ref, pvol_ref, velocity_ref, table_ref, sems,
):
    some = pl.ds(first, count)
    wide = pl.ds(first * BLOCK, count * BLOCK)
    copies = fetch(
        [
            (velocity_hbm, velocity_ref),
            (brick_hbm, brick_ref),
            (base_hbm.at[some], base_ref),
            (frac_hbm.at[:, wide], frac_ref),
            (pvel_hbm.at[:, wide], pvel_ref),
            (coef_hbm.at[some], coef_ref),
            (pvol_hbm.at[some], pvol_ref),
        ],
        sems,
    )
    rows, lane = rows_iota(), lanes_iota()
    tiles_x = velocity_ref.shape[2] // 8

    def convert(number, carry):
        for k in range(2):
            tx = number * 2 + k
            at = pl.ds(pl.multiple_of(tx * 8, 8), 8)
            for c in range(3):
                tiles = transpose_granules([velocity_ref[c, z, at, :] for z in range(8)], lane)
                for t3 in range(8):
                    table_ref[(tx * 3 + c) * 8 + t3] = tiles[t3]
        return carry

    copies[0].wait()
    lax.fori_loop(0, tiles_x // 2, convert, 0)
    for copy in copies[1:]:
        copy.wait()

    def step(number, carry):
        for k in range(UNROLL):
            block = number * UNROLL + k
            at, zb, xb, yb, fz, fx, fy = particles(base_ref, frac_ref, block)
            tx, t3, t1 = brick_place(brick_ref[first + block])
            kx = axis_weights(rows, xb, fx)
            corners = corner_terms(zb, yb, fz, fy, t1 * 64)
            rel = [
                interpolate(table_ref[(tx * 3 + c) * 8 + t3], kx, corners) - pvel_ref[c : c + 1, at]
                for c in range(3)
            ]
            speed = rel[0] * rel[0] + rel[1] * rel[1] + rel[2] * rel[2]
            factor = coef_ref[pl.ds(block, 1), :] * pvol_ref[pl.ds(block, 1), :]
            factor = factor * jnp.exp(FLOW_POWER * jnp.log(speed + 0.01))
            for c in range(3):
                out_ref[c : c + 1, at] = factor * rel[c]
        return carry

    lax.fori_loop(0, count // UNROLL, step, 0)
    (copy,) = fetch([(out_ref, out_any)], sems)
    copy.wait()


def pack_halo(rows, tiles):
    a, b, c, d = tiles
    middle = jnp.logical_or(rows == 3, rows == 4)
    first = jnp.where(middle, pltpu.roll(d, 3, 0), a)
    second = jnp.where(rows == 3, pltpu.roll(d, 1, 0), jnp.where(rows == 4, pltpu.roll(d, 7, 0), b))
    third = jnp.where(middle, pltpu.roll(d, 5, 0), c)
    return first, second, third


def unpack_halo(rows, tiles):
    a, b, c = tiles
    inner = jnp.where(rows == 2, pltpu.roll(b, 7, 0), pltpu.roll(b, 1, 0))
    d = jnp.where(rows < 2, pltpu.roll(a, 5, 0), jnp.where(rows > 5, pltpu.roll(c, 3, 0), inner))
    return a, b, c, d


def drag_kernel(
    brick_ref, base_ref, frac_ref, slip_a_hbm, slip_b_ref, eps_ref,
    drag_ref, out_hbm, tick_ref,
    force_ref, slip_a_ref, sems,
):
    subs = force_ref.shape[0]
    rows, lane = rows_iota(), lanes_iota()
    (copy,) = fetch([(slip_a_hbm, slip_a_ref)], sems)
    for j in range(subs):
        force_ref[j, 0:48] = jnp.zeros((48, 8, LANES), F32)
    copy.wait()

    for slip_ref, start in ((slip_a_ref, 0), (slip_b_ref, slip_a_ref.shape[1] // BLOCK)):

        def step(number, carry, slip_ref=slip_ref, start=start):
            found = []
            for k in range(UNROLL):
                inner = number * UNROLL + k
                block = inner + start
                at, zb, xb, yb, fz, fx, fy = particles(base_ref, frac_ref, block)
                inner_at = pl.ds(pl.multiple_of(inner * BLOCK, BLOCK), BLOCK)
                tx, t3, t1 = brick_place(brick_ref[block])
                kx = axis_weights(rows, xb, fx)
                eps = interpolate(eps_ref[tx * 8 + t3], kx, corner_terms(zb, yb, fz, fy, t1 * 64))
                factor = jnp.exp(DRAG_POWER * jnp.log(eps))
                parts = []
                for c in range(3):
                    force = factor * slip_ref[c : c + 1, inner_at]
                    drag_ref[c : c + 1, at] = force
                    parts.append(kx * spread(force))
                found.append((parts, plane_weights(rows, zb, yb, fz, fy)))
            found = sum((deposit(found[k : k + 2]) for k in range(0, UNROLL, 2)), [])
            for k in range(UNROLL):
                tx, t3, t1 = brick_place(brick_ref[number * UNROLL + k + start])
                mine = (lane >> 6) == t1
                for c in range(3):
                    tile = (tx & 1) * 24 + c * 8 + t3
                    force_ref[tx >> 1, tile] += jnp.where(mine, found[k][8 * c : 8 * c + 8], 0.0)
            return carry

        lax.fori_loop(0, slip_ref.shape[1] // BLOCK // UNROLL, step, 0)
    copies = fetch([(force_ref.at[j, 0:48], out_hbm.at[j, 0:48]) for j in range(subs)], sems)
    zero = jnp.zeros((8, LANES), F32)
    tick_ref[...] = zero
    for j in range(subs):
        for quad in range(6):
            tiles = []
            for at in range(quad * 4, quad * 4 + 4):
                after = force_ref[j + 1, at] if j + 1 < subs else zero
                before = force_ref[j - 1, 24 + at] if j > 0 else zero
                tiles.append(jnp.where(rows < 4, after, before))
            for n, tile in enumerate(pack_halo(rows, tiles)):
                force_ref[j, 48 + quad * 3 + n] = tile
        copy = pltpu.make_async_copy(
            force_ref.at[j, 48:66], out_hbm.at[j, 48:66], sems.at[subs + j]
        )
        copy.start()
        copies.append(copy)
    for copy in copies:
        copy.wait()


def source_kernel(place_ref, parts_ref, eps_ref, first_any, void_any, own_ref, even_ref, odd_ref):
    lane, rows = lanes_iota(), rows_iota()
    even, sub = place_ref[0] % 2 == 0, place_ref[1]
    tiles_x = eps_ref.shape[0] // 8
    after = jnp.minimum(sub * 2 + 2, tiles_x - 1) * 8
    before = jnp.maximum(sub * 2 - 1, 0) * 8

    def summed(at):
        total = parts_ref[0, at]
        for j in range(1, parts_ref.shape[0]):
            total = total + parts_ref[j, at]
        return total

    for t in range(3):
        for c in range(3):
            if t < 2:
                forces = [summed(t * 24 + c * 8 + t3) for t3 in range(8)]
            else:
                forces = []
                for quad in (2 * c, 2 * c + 1):
                    forces += unpack_halo(rows, [summed(48 + quad * 3 + k) for k in range(3)])
            tiles = []
            for t3 in range(8):
                if t < 2:
                    eps = eps_ref[(sub * 2 + t) * 8 + t3]
                else:
                    eps = jnp.where(rows < 4, eps_ref[after + t3], eps_ref[before + t3])
                tiles.append(-forces[t3] / eps)
            tiles = transpose_granules(tiles, lane)
            first = 8 * (t + 1) % 24
            for z in range(8):
                own_ref[c, z, first : first + 8, :] = tiles[z]
            for n in range(3):
                at = slice(first, first + 8)
                even_ref[c, n, at, :] = jnp.where(even, tiles[5 + n], tiles[n])
                odd_ref[c, n, at, :] = jnp.where(even, tiles[n], tiles[5 + n])


def window_kernel(place_ref, after_any, velocity_hbm, out_ref, even_ref, odd_ref, sems):
    even = place_ref[0] % 2 == 0
    depth = velocity_hbm.shape[1]
    tiles_x = velocity_hbm.shape[2] // 8
    pairs, inside = [], []
    for r in range(4):
        want = place_ref[1] * 2 + r - 1
        inside.append(jnp.logical_and(want >= 0, want < tiles_x))
        at = pl.ds(pl.multiple_of(jnp.clip(want, 0, tiles_x - 1) * 8, 8), 8)
        pairs.append((velocity_hbm.at[:, :, at, :], out_ref.at[:, :, 8 * r : 8 * r + 8, :]))
    for copy in fetch(pairs, sems):
        copy.wait()
    for r in range(4):
        at = slice(8 * r, 8 * r + 8)
        rows = jnp.where(inside[r], out_ref[:, :, at, :], 0.0)
        out_ref[:, :, at, :] = rows
        even_ref[:, :, at, :] = jnp.where(even, rows[:, depth - 4 :], rows[:, :4])
        odd_ref[:, :, at, :] = jnp.where(even, rows[:, :4], rows[:, depth - 4 :])


def void_kernel(after_any, eps_ref, out_ref, tick_ref):
    tick_ref[...] = jnp.zeros_like(tick_ref)
    lane = lanes_iota()

    def convert(number, carry):
        for k in range(4):
            tx = number * 4 + k
            tiles = transpose_granules([eps_ref[tx * 8 + t3] for t3 in range(8)], lane)
            for z in range(8):
                out_ref[z, pl.ds(pl.multiple_of(tx * 8, 8), 8), :] = tiles[z]
        return carry

    lax.fori_loop(0, out_ref.shape[1] // 32, convert, 0)


def edges(slab, sub, planes, width):
    row = lax.broadcasted_iota(jnp.int32, (32, LANES), 0) + sub * 16 - 8
    inside_x = jnp.logical_and(row >= 0, row < width)

    def keep(z):
        height = slab * 8 - 4 + z
        return jnp.logical_and(inside_x, jnp.logical_and(height >= 0, height < planes))

    return keep


def unforced(old, z, lane):
    shear = None
    centres, laps = [], []
    for c in range(3):
        centre = old[c, z]
        upper = old[c, z + 1]
        lower = old[c, z - 1]
        east = pltpu.roll(centre, 31, 0)
        west = pltpu.roll(centre, 1, 0)
        north = jnp.where(lane == LANES - 1, 0.0, pltpu.roll(centre, LANES - 1, 1))
        south = jnp.where(lane == 0, 0.0, pltpu.roll(centre, 1, 1))
        term = (upper - centre) ** 2 + (east - centre) ** 2 + (north - centre) ** 2
        shear = term if shear is None else shear + term
        centres.append(centre)
        laps.append(upper + lower + east + west + north + south - 6.0 * centre)
    viscous = (TIME_STEP * VISCOSITY) * jnp.exp(FLOW_POWER * jnp.log(shear + 0.01))
    return [centres[c] + viscous * laps[c] for c in range(3)]


def first_kernel(place_ref, window_ref, even_ref, odd_ref, out_ref, tick_ref, old):
    tick_ref[...] = jnp.zeros_like(tick_ref)
    side = place_ref[0] % 2
    old[:, pl.ds(12 - 12 * side, 4)] = even_ref[...]
    old[:, pl.ds(12 * side, 4)] = odd_ref[...]
    old[:, 4:12] = window_ref[...]
    lane = lax.broadcasted_iota(jnp.int32, (32, LANES), 1)

    def plane(number, carry):
        for k in range(2):
            z = number * 2 + k
            moved = unforced(old, z + 1, lane)
            for c in range(3):
                out_ref[c, z] = moved[c]
        return carry

    lax.fori_loop(0, 7, plane, 0)


def stencil_kernel(
    place_ref, first_ref, own_ref, even_ref, odd_ref, out_ref, even, odd, source
):
    keep = edges(place_ref[0], place_ref[1], place_ref[2], place_ref[3])
    lane = lax.broadcasted_iota(jnp.int32, (32, LANES), 1)
    side = place_ref[0] % 2
    parts = ((even_ref, pl.ds(11 - 11 * side, 3)), (own_ref, slice(3, 11)), (odd_ref, pl.ds(11 * side, 3)))
    for part, planes in parts:
        source[:, planes, 0:24, :] = part[...]
        source[:, planes, 24:32, :] = part[:, :, 0:8, :]

    def first(number, carry):
        for k in range(2):
            z = number * 2 + k
            inside = keep(z + 1)
            for c in range(3):
                moved = first_ref[c, z] + TIME_STEP * source[c, z]
                odd[c, z + 1] = jnp.where(inside, moved, 0.0)
        return carry

    lax.fori_loop(0, 7, first, 0)
    buffers = (even, odd)
    for step in range(1, ITERS):
        old, new = buffers[step % 2], buffers[(step + 1) % 2]

        def plane(number, carry, old=old, new=new, step=step):
            for k in range(2):
                z = number * 2 + k + step + 1
                moved = unforced(old, z, lane)
                inside = keep(z)
                for c in range(3):
                    forced = moved[c] + TIME_STEP * source[c, z - 1]
                    new[c, z] = jnp.where(inside, forced, 0.0)
            return carry

        lax.fori_loop(0, 7 - step, plane, 0)
    for j in range(out_ref.shape[0]):
        out_ref[j] = even[:, 4:12, 8:24, :]


def place_kernel(parts_ref, out_ref, sems):
    rows = parts_ref.shape[3]
    pairs = []
    for j in range(parts_ref.shape[0]):
        pairs.append((parts_ref.at[j], out_ref.at[:, :, j * rows : (j + 1) * rows, :]))
    for copy in fetch(pairs, sems):
        copy.wait()


def pinned(*arrays):
    return [pltpu.with_memory_space_constraint(x, pltpu.HBM) for x in arrays]


def call(kernel, out_shapes, ins, scratch=(), outs=None, us=1.0):
    outs = outs or [VMEM] * len(out_shapes)
    return pl.pallas_call(
        kernel,
        out_shape=[
            pltpu.HBM(s, F32) if spec is HBM else jax.ShapeDtypeStruct(s, F32)
            for s, spec in zip(out_shapes, outs)
        ],
        in_specs=ins,
        out_specs=outs,
        scratch_shapes=list(scratch),
        compiler_params=PARAMS,
        cost_estimate=pl.CostEstimate(flops=int(us * 1e9), bytes_accessed=int(us * 3.6e6), transcendentals=0),
    )


def pair_up(x, first):
    pairs = [(i, i + 1) for i in range(first, lax.axis_size("slab") - 1, 2)]
    return lax.ppermute(x, "slab", pairs + [(j, i) for i, j in pairs])


def body(velocity, part_vel, fraction, base_cell, drag_coeff, part_volume, brick_of_block):
    depth, width_x = velocity.shape[1], velocity.shape[2]
    blocks = brick_of_block.shape[0]
    subs = lax.axis_size("sub")
    slab = lax.axis_index("slab").astype(jnp.int32)
    sub = lax.axis_index("sub").astype(jnp.int32)
    tiles_x = width_x // 8
    tiles = tiles_x * 8
    share = tiles // subs
    base = base_cell.reshape(blocks, BLOCK)
    coef = drag_coeff.reshape(blocks, BLOCK)
    pvol = part_volume.reshape(blocks, BLOCK)

    particles_vmem = [
        pltpu.SMEM((blocks,), jnp.int32),
        pltpu.VMEM((blocks, BLOCK), jnp.int32),
        pltpu.VMEM((3, blocks * BLOCK), F32),
    ]
    row_vmem = pltpu.VMEM((blocks, BLOCK), F32)
    (solid,) = call(
        solid_kernel,
        [(tiles, 8, LANES)],
        [HBM] * 4,
        [pltpu.VMEM((tiles, 8, LANES), F32)]
        + particles_vmem
        + [row_vmem, pltpu.SemaphoreType.DMA((4,))],
        outs=[HBM],
        us=5.0,
    )(*pinned(brick_of_block, base, fraction, pvol))
    solid_parts = lax.all_to_all(solid.reshape(subs, share, 8, LANES), "sub", 0, 0)
    half = blocks // 2

    def slip_of(first, after, out):
        (slip,) = call(
            functools.partial(slip_kernel, first, half),
            [(3, half * BLOCK)],
            [HBM] * 8,
            [
                pltpu.VMEM((3, half * BLOCK), F32),
                pltpu.SMEM((blocks,), jnp.int32),
                pltpu.VMEM((half, BLOCK), jnp.int32),
                pltpu.VMEM((3, half * BLOCK), F32),
                pltpu.VMEM((3, half * BLOCK), F32),
                pltpu.VMEM((half, BLOCK), F32),
                pltpu.VMEM((half, BLOCK), F32),
                pltpu.VMEM(velocity.shape, F32),
                pltpu.VMEM((3 * tiles, 8, LANES), F32),
                pltpu.SemaphoreType.DMA((7,)),
            ],
            us=5.0,
            )(after, brick_of_block, base, fraction, part_vel, coef, pvol, velocity)
        return slip

    slip_a = slip_of(0, solid, HBM)
    (eps_copies,) = call(
        eps_kernel,
        [(subs, share, 8, LANES)],
        [VMEM],
        [pltpu.VMEM((share, 8, LANES), F32), pltpu.SemaphoreType.DMA((subs,))],
        outs=[HBM],
        us=0.5,
    )(solid_parts)
    slip_b = slip_of(half, eps_copies, ANY)
    eps = lax.all_to_all(eps_copies, "sub", 0, 0).reshape(tiles, 8, LANES)
    drag, force, tick = call(
        drag_kernel,
        [(3, blocks * BLOCK), (subs, 66, 8, LANES), (8, LANES)],
        [SMEM, VMEM, VMEM, HBM, VMEM, VMEM],
        [
            pltpu.VMEM((subs, 66, 8, LANES), F32),
            pltpu.VMEM((3, half * BLOCK), F32),
            pltpu.SemaphoreType.DMA((2 * subs,)),
        ],
        outs=[VMEM, HBM, VMEM],
        us=6.0,
    )(brick_of_block, base, fraction, *pinned(slip_a), slip_b, eps)
    forces = lax.all_to_all(force, "sub", 0, 0)
    planes = depth * lax.axis_size("slab")
    place = jnp.stack([slab, sub, jnp.int32(planes), jnp.int32(width_x)])
    window, even, odd = call(
        window_kernel,
        [(3, depth, 32, LANES), (3, 4, 32, LANES), (3, 4, 32, LANES)],
        [SMEM, ANY, HBM],
        [pltpu.SemaphoreType.DMA((4,))],
    )(place, tick, *pinned(velocity))
    even, odd = pair_up(even, 0), pair_up(odd, 1)
    voidfraction, void_tick = call(
        void_kernel, [(depth, width_x, LANES), (8, LANES)], [ANY, VMEM], us=2.0
    )(tick, eps)
    first, first_tick = call(
        first_kernel,
        [(3, 14, 32, LANES), (8, LANES)],
        [SMEM] + [VMEM] * 3,
        [pltpu.VMEM((3, 16, 32, LANES), F32)],
        us=1.0,
    )(place, window, even, odd)

    rows = width_x // subs
    own, even, odd = call(
        source_kernel,
        [(3, depth, 24, LANES), (3, 3, 24, LANES), (3, 3, 24, LANES)],
        [SMEM, VMEM, VMEM, ANY, ANY],
    )(place, forces, eps, first_tick, void_tick)
    even, odd = pair_up(even, 0), pair_up(odd, 1)
    (moved,) = call(
        stencil_kernel,
        [(subs, 3, depth, rows, LANES)],
        [SMEM] + [VMEM] * 4,
        [
            pltpu.VMEM((3, 16, 32, LANES), F32),
            pltpu.VMEM((3, 16, 32, LANES), F32),
            pltpu.VMEM((3, 14, 32, LANES), F32),
        ],
        us=4.0,
    )(place, first, own, even, odd)
    moved = lax.all_to_all(moved, "sub", 0, 0)
    (new_velocity,) = call(
        place_kernel,
        [velocity.shape],
        [ANY],
        [pltpu.SemaphoreType.DMA((subs,))],
        outs=[HBM],
    )(moved)
    return new_velocity, voidfraction, drag


def solution(mesh):
    in_specs = (
        P(None, "slab", None, None),
        P(None, ("slab", "sub")),
        P(None, ("slab", "sub")),
        P(("slab", "sub")),
        P(("slab", "sub")),
        P(("slab", "sub")),
        P(("slab", "sub")),
    )
    out_specs = (P(None, "slab", None, None), P("slab", None, None), P(None, ("slab", "sub")))
    return jax.shard_map(body, mesh=mesh, in_specs=in_specs, out_specs=out_specs, check_vma=False)
```

```python
import functools

import jax
import jax.numpy as jnp
from jax import lax
from jax.experimental import pallas as pl
from jax.experimental.pallas import tpu as pltpu
from jax.sharding import PartitionSpec as P

BLOCK = 128
LANES = 128
EPS_MIN = 0.35
FLOW_POWER = -0.2
DRAG_POWER = -2.65
VISCOSITY = 1.2
TIME_STEP = 0.05
ITERS = 4
UNROLL = 16
F32 = jnp.float32
PARAMS = pltpu.CompilerParams(vmem_limit_bytes=16 * 1024 * 1024)
VMEM = pl.BlockSpec(memory_space=pltpu.VMEM)
SMEM = pl.BlockSpec(memory_space=pltpu.SMEM)
HBM = pl.BlockSpec(memory_space=pltpu.HBM)
ANY = pl.BlockSpec(memory_space=pl.ANY)


def transpose_granules(tiles, lane):
    for bit in (1, 2, 4):
        shift = 8 * bit
        high = (lane & shift) != 0
        new = list(tiles)
        for a in range(8):
            if a & bit:
                continue
            b = a | bit
            va, vb = tiles[a], tiles[b]
            new[a] = jnp.where(high, pltpu.roll(vb, shift, 1), va)
            new[b] = jnp.where(high, vb, pltpu.roll(va, LANES - shift, 1))
        tiles = new
    return tiles


def fetch(pairs, sems):
    copies = [pltpu.make_async_copy(a, b, sems.at[i]) for i, (a, b) in enumerate(pairs)]
    for copy in copies:
        copy.start()
    return copies


def lanes_iota():
    return lax.broadcasted_iota(jnp.int32, (8, LANES), 1)


def rows_iota():
    return lax.broadcasted_iota(jnp.int32, (8, LANES), 0)


def spread(row):
    return jnp.broadcast_to(row, (8, LANES))


def particles(base_ref, frac_ref, block):
    at = pl.ds(pl.multiple_of(block * BLOCK, BLOCK), BLOCK)
    base = spread(base_ref[pl.ds(block, 1), :])
    fz = spread(frac_ref[0:1, at])
    fx = spread(frac_ref[1:2, at])
    fy = spread(frac_ref[2:3, at])
    return at, base >> 6, (base >> 3) & 7, base & 7, fz, fx, fy


def axis_weights(rows, first, frac):
    zero = jnp.zeros_like(frac)
    return jnp.where(rows == first, 1.0 - frac, jnp.where(rows == first + 1, frac, zero))


def halves(value):
    high = value.astype(jnp.bfloat16).astype(F32)
    return high, value - high


def plane_weights(rows, zb, yb, fz, fy):
    ky = axis_weights(rows, yb, fy)
    zero = jnp.zeros_like(fz)
    at = [zb == z for z in range(7)]
    parts = []
    for here, above in zip(halves((1.0 - fz) * ky), halves(fz * ky)):
        for z in range(8):
            part = zero if z == 0 else jnp.where(at[z - 1], above, zero)
            parts.append(part if z == 7 else jnp.where(at[z], here, part))
    return jnp.concatenate(parts, axis=0).astype(jnp.bfloat16)


def split_rows(parts):
    full = jnp.concatenate(parts, axis=0)
    high = full.astype(jnp.bfloat16).astype(F32)
    return jnp.concatenate([high, full - high], axis=0).astype(jnp.bfloat16)


def deposit(blocks):
    left = []
    for n, (parts, _) in enumerate(blocks):
        rows = split_rows(parts)
        pair = [rows, jnp.zeros_like(rows)]
        left.append(jnp.concatenate(pair if n == 0 else pair[::-1], axis=1))
    both = lax.dot_general(
        jnp.concatenate(left, axis=0),
        jnp.concatenate([weights for _, weights in blocks], axis=1),
        (((1,), (1,)), ((), ())),
        preferred_element_type=F32,
    )
    half = both.shape[0] // 4
    found = []
    for n in range(2):
        total = both[2 * n * half : (2 * n + 1) * half] + both[(2 * n + 1) * half : (2 * n + 2) * half]
        found.append(total + pltpu.roll(total, 64, 1))
    return found


def corner_terms(zb, yb, fz, fy, offset):
    index = (zb << 3) + yb + offset
    gz, gy = 1.0 - fz, 1.0 - fy
    return (
        (index, gz * gy),
        (index + 1, gz * fy),
        (index + 8, fz * gy),
        (index + 9, fz * fy),
    )


def interpolate(tile, kx, corners):
    total = None
    for index, weight in corners:
        term = weight * jnp.take_along_axis(tile, index, axis=1, mode="promise_in_bounds")
        total = term if total is None else total + term
    return jnp.sum(kx * total, axis=0, keepdims=True)


def brick_place(brick):
    return brick >> 4, brick & 7, (brick >> 3) & 1


def solid_kernel(
    brick_hbm, base_hbm, frac_hbm, pvol_hbm, out_hbm,
    out_ref, brick_ref, base_ref, frac_ref, pvol_ref, sems,
):
    copies = fetch(
        [(brick_hbm, brick_ref), (base_hbm, base_ref), (frac_hbm, frac_ref), (pvol_hbm, pvol_ref)],
        sems,
    )
    out_ref[...] = jnp.zeros_like(out_ref)
    for copy in copies:
        copy.wait()
    rows, lane = rows_iota(), lanes_iota()

    def step(number, carry):
        found = []
        for k in range(UNROLL):
            block = number * UNROLL + k
            _, zb, xb, yb, fz, fx, fy = particles(base_ref, frac_ref, block)
            kx = axis_weights(rows, xb, fx) * spread(pvol_ref[pl.ds(block, 1), :])
            found.append(([kx], plane_weights(rows, zb, yb, fz, fy)))
        found = sum((deposit(found[k : k + 2]) for k in range(0, UNROLL, 2)), [])
        for k in range(UNROLL):
            tx, t3, t1 = brick_place(brick_ref[number * UNROLL + k])
            tile = tx * 8 + t3
            out_ref[tile] += jnp.where((lane >> 6) == t1, found[k], 0.0)
        return carry

    lax.fori_loop(0, base_ref.shape[0] // UNROLL, step, 0)
    (copy,) = fetch([(out_ref, out_hbm)], sems)
    copy.wait()


def eps_kernel(parts_ref, copies_hbm, out_ref, sems):
    total = parts_ref[0]
    for j in range(1, parts_ref.shape[0]):
        total = total + parts_ref[j]
    total = jnp.maximum(1.0 - total, EPS_MIN)
    out_ref[...] = total
    for copy in fetch([(out_ref, copies_hbm.at[j]) for j in range(copies_hbm.shape[0])], sems):
        copy.wait()


def slip_kernel(
    first, count,
    after_any, brick_hbm, base_hbm, frac_hbm, pvel_hbm, coef_hbm, pvol_hbm, velocity_hbm,
    out_any,
    out_ref, brick_ref, base_ref, frac_ref, pvel_ref, coef_ref, pvol_ref, velocity_ref, table_ref, sems,
):
    some = pl.ds(first, count)
    wide = pl.ds(first * BLOCK, count * BLOCK)
    copies = fetch(
        [
            (velocity_hbm, velocity_ref),
            (brick_hbm, brick_ref),
            (base_hbm.at[some], base_ref),
            (frac_hbm.at[:, wide], frac_ref),
            (pvel_hbm.at[:, wide], pvel_ref),
            (coef_hbm.at[some], coef_ref),
            (pvol_hbm.at[some], pvol_ref),
        ],
        sems,
    )
    rows, lane = rows_iota(), lanes_iota()
    tiles_x = velocity_ref.shape[2] // 8

    def convert(number, carry):
        for k in range(2):
            tx = number * 2 + k
            at = pl.ds(pl.multiple_of(tx * 8, 8), 8)
            for c in range(3):
                tiles = transpose_granules([velocity_ref[c, z, at, :] for z in range(8)], lane)
                for t3 in range(8):
                    table_ref[(tx * 3 + c) * 8 + t3] = tiles[t3]
        return carry

    copies[0].wait()
    lax.fori_loop(0, tiles_x // 2, convert, 0)
    for copy in copies[1:]:
        copy.wait()

    def step(number, carry):
        for k in range(UNROLL):
            block = number * UNROLL + k
            at, zb, xb, yb, fz, fx, fy = particles(base_ref, frac_ref, block)
            tx, t3, t1 = brick_place(brick_ref[first + block])
            kx = axis_weights(rows, xb, fx)
            corners = corner_terms(zb, yb, fz, fy, t1 * 64)
            rel = [
                interpolate(table_ref[(tx * 3 + c) * 8 + t3], kx, corners) - pvel_ref[c : c + 1, at]
                for c in range(3)
            ]
            speed = rel[0] * rel[0] + rel[1] * rel[1] + rel[2] * rel[2]
            factor = coef_ref[pl.ds(block, 1), :] * pvol_ref[pl.ds(block, 1), :]
            factor = factor * jnp.exp(FLOW_POWER * jnp.log(speed + 0.01))
            for c in range(3):
                out_ref[c : c + 1, at] = factor * rel[c]
        return carry

    lax.fori_loop(0, count // UNROLL, step, 0)
    (copy,) = fetch([(out_ref, out_any)], sems)
    copy.wait()


def drag_kernel(
    brick_ref, base_ref, frac_ref, slip_a_hbm, slip_b_ref, eps_ref,
    drag_ref, out_hbm, tick_ref,
    force_ref, slip_a_ref, sems,
):
    subs = force_ref.shape[0]
    rows, lane = rows_iota(), lanes_iota()
    (copy,) = fetch([(slip_a_hbm, slip_a_ref)], sems)
    for j in range(subs):
        force_ref[j] = jnp.zeros(force_ref.shape[1:], F32)
    copy.wait()

    for slip_ref, start in ((slip_a_ref, 0), (slip_b_ref, slip_a_ref.shape[1] // BLOCK)):

        def step(number, carry, slip_ref=slip_ref, start=start):
            found = []
            for k in range(UNROLL):
                inner = number * UNROLL + k
                block = inner + start
                at, zb, xb, yb, fz, fx, fy = particles(base_ref, frac_ref, block)
                inner_at = pl.ds(pl.multiple_of(inner * BLOCK, BLOCK), BLOCK)
                tx, t3, t1 = brick_place(brick_ref[block])
                kx = axis_weights(rows, xb, fx)
                eps = interpolate(eps_ref[tx * 8 + t3], kx, corner_terms(zb, yb, fz, fy, t1 * 64))
                factor = jnp.exp(DRAG_POWER * jnp.log(eps))
                parts = []
                for c in range(3):
                    force = factor * slip_ref[c : c + 1, inner_at]
                    drag_ref[c : c + 1, at] = force
                    parts.append(kx * spread(force))
                found.append((parts, plane_weights(rows, zb, yb, fz, fy)))
            found = sum((deposit(found[k : k + 2]) for k in range(0, UNROLL, 2)), [])
            for k in range(UNROLL):
                tx, t3, t1 = brick_place(brick_ref[number * UNROLL + k + start])
                mine = (lane >> 6) == t1
                for c in range(3):
                    tile = (tx & 1) * 24 + c * 8 + t3
                    force_ref[tx >> 1, tile] += jnp.where(mine, found[k][8 * c : 8 * c + 8], 0.0)
            return carry

        lax.fori_loop(0, slip_ref.shape[1] // BLOCK // UNROLL, step, 0)
    tick_ref[...] = jnp.zeros_like(tick_ref)
    for copy in fetch([(force_ref.at[j], out_hbm.at[j]) for j in range(subs)], sems):
        copy.wait()


def source_kernel(place_ref, parts_ref, eps_ref, first_any, own_ref, even_ref, odd_ref):
    lane, rows = lanes_iota(), rows_iota()
    even = place_ref[1] % 2 == 0
    for c in range(3):
        grid = []
        for t in range(2):
            tiles = []
            for t3 in range(8):
                at = (t * 3 + c) * 8 + t3
                total = parts_ref[0, at]
                for j in range(1, parts_ref.shape[0]):
                    total = total + parts_ref[j, at]
                tiles.append(-total / eps_ref[t * 8 + t3])
            tiles = transpose_granules(tiles, lane)
            for z in range(8):
                own_ref[c, z, 8 * t : 8 * t + 8, :] = tiles[z]
            grid.append(tiles)
        for q in range(4):
            first = jnp.where(rows < 4, grid[0][2 * q], pltpu.roll(grid[0][2 * q + 1], 4, 0))
            last = jnp.where(rows < 4, pltpu.roll(grid[1][2 * q], 4, 0), grid[1][2 * q + 1])
            even_ref[c, q] = jnp.where(even, last, first)
            odd_ref[c, q] = jnp.where(even, first, last)


def halo_kernel(place_ref, own_ref, even_ref, odd_ref, halo_ref, up_ref, down_ref):
    rows = rows_iota()
    slab_even, sub_even = place_ref[0] % 2 == 0, place_ref[1] % 2 == 0
    for c in range(3):
        tiles = []
        for q in range(4):
            after = jnp.where(sub_even, even_ref[c, q], odd_ref[c, q])
            before = jnp.where(sub_even, odd_ref[c, q], even_ref[c, q])
            tiles.append(jnp.where(rows < 4, after, pltpu.roll(before, 4, 0)))
            tiles.append(jnp.where(rows < 4, pltpu.roll(after, 4, 0), before))
        for z in range(8):
            halo_ref[c, z] = tiles[z]
        for n in range(3):
            low, high = own_ref[c, n], own_ref[c, 5 + n]
            up_ref[c, n, 0:8, :] = jnp.where(slab_even, tiles[5 + n], tiles[n])
            up_ref[c, n, 8:24, :] = jnp.where(slab_even, high, low)
            down_ref[c, n, 0:8, :] = jnp.where(slab_even, tiles[n], tiles[5 + n])
            down_ref[c, n, 8:24, :] = jnp.where(slab_even, low, high)


def window_kernel(place_ref, after_any, velocity_hbm, out_ref, even_ref, odd_ref, sems):
    even = place_ref[0] % 2 == 0
    depth = velocity_hbm.shape[1]
    tiles_x = velocity_hbm.shape[2] // 8
    pairs, inside = [], []
    for r in range(4):
        want = place_ref[1] * 2 + r - 1
        inside.append(jnp.logical_and(want >= 0, want < tiles_x))
        at = pl.ds(pl.multiple_of(jnp.clip(want, 0, tiles_x - 1) * 8, 8), 8)
        pairs.append((velocity_hbm.at[:, :, at, :], out_ref.at[:, :, 8 * r : 8 * r + 8, :]))
    for copy in fetch(pairs, sems):
        copy.wait()
    for r in range(4):
        at = slice(8 * r, 8 * r + 8)
        rows = jnp.where(inside[r], out_ref[:, :, at, :], 0.0)
        out_ref[:, :, at, :] = rows
        even_ref[:, :, at, :] = jnp.where(even, rows[:, depth - 4 :], rows[:, :4])
        odd_ref[:, :, at, :] = jnp.where(even, rows[:, :4], rows[:, depth - 4 :])


def void_kernel(place_ref, after_any, eps_ref, out_ref, own_ref):
    lane = lanes_iota()

    def convert(number, carry):
        for k in range(4):
            tx = number * 4 + k
            tiles = transpose_granules([eps_ref[tx * 8 + t3] for t3 in range(8)], lane)
            for z in range(8):
                out_ref[z, pl.ds(pl.multiple_of(tx * 8, 8), 8), :] = tiles[z]
        return carry

    lax.fori_loop(0, out_ref.shape[1] // 32, convert, 0)
    own_ref[...] = eps_ref[pl.ds(place_ref[1] * own_ref.shape[0], own_ref.shape[0])]


def edges(slab, sub, planes, width):
    row = lax.broadcasted_iota(jnp.int32, (32, LANES), 0) + sub * 16 - 8
    inside_x = jnp.logical_and(row >= 0, row < width)

    def keep(z):
        height = slab * 8 - 4 + z
        return jnp.logical_and(inside_x, jnp.logical_and(height >= 0, height < planes))

    return keep


def unforced(old, z, lane):
    shear = None
    centres, laps = [], []
    for c in range(3):
        centre = old[c, z]
        upper = old[c, z + 1]
        lower = old[c, z - 1]
        east = pltpu.roll(centre, 31, 0)
        west = pltpu.roll(centre, 1, 0)
        north = jnp.where(lane == LANES - 1, 0.0, pltpu.roll(centre, LANES - 1, 1))
        south = jnp.where(lane == 0, 0.0, pltpu.roll(centre, 1, 1))
        term = (upper - centre) ** 2 + (east - centre) ** 2 + (north - centre) ** 2
        shear = term if shear is None else shear + term
        centres.append(centre)
        laps.append(upper + lower + east + west + north + south - 6.0 * centre)
    viscous = (TIME_STEP * VISCOSITY) * jnp.exp(FLOW_POWER * jnp.log(shear + 0.01))
    return [centres[c] + viscous * laps[c] for c in range(3)]


def first_kernel(place_ref, window_ref, even_ref, odd_ref, out_ref, tick_ref, old):
    tick_ref[...] = jnp.zeros_like(tick_ref)
    side = place_ref[0] % 2
    old[:, pl.ds(12 - 12 * side, 4)] = even_ref[...]
    old[:, pl.ds(12 * side, 4)] = odd_ref[...]
    old[:, 4:12] = window_ref[...]
    lane = lax.broadcasted_iota(jnp.int32, (32, LANES), 1)

    def plane(number, carry):
        for k in range(2):
            z = number * 2 + k
            moved = unforced(old, z + 1, lane)
            for c in range(3):
                out_ref[c, z] = moved[c]
        return carry

    lax.fori_loop(0, 7, plane, 0)


def stencil_kernel(
    place_ref, first_ref, own_ref, halo_ref, even_ref, odd_ref, out_ref, even, odd, source
):
    keep = edges(place_ref[0], place_ref[1], place_ref[2], place_ref[3])
    lane = lax.broadcasted_iota(jnp.int32, (32, LANES), 1)
    side = place_ref[0] % 2
    source[:, 3:11, 0:8, :] = halo_ref[...]
    source[:, 3:11, 8:24, :] = own_ref[...]
    source[:, 3:11, 24:32, :] = halo_ref[...]
    for part, start in ((even_ref, 11 - 11 * side), (odd_ref, 11 * side)):
        planes = pl.ds(start, 3)
        source[:, planes, 0:24, :] = part[...]
        source[:, planes, 24:32, :] = part[:, :, 0:8, :]

    def first(number, carry):
        for k in range(2):
            z = number * 2 + k
            inside = keep(z + 1)
            for c in range(3):
                moved = first_ref[c, z] + TIME_STEP * source[c, z]
                odd[c, z + 1] = jnp.where(inside, moved, 0.0)
        return carry

    lax.fori_loop(0, 7, first, 0)
    buffers = (even, odd)
    for step in range(1, ITERS):
        old, new = buffers[step % 2], buffers[(step + 1) % 2]

        def plane(number, carry, old=old, new=new, step=step):
            for k in range(2):
                z = number * 2 + k + step + 1
                moved = unforced(old, z, lane)
                inside = keep(z)
                for c in range(3):
                    forced = moved[c] + TIME_STEP * source[c, z - 1]
                    new[c, z] = jnp.where(inside, forced, 0.0)
            return carry

        lax.fori_loop(0, 7 - step, plane, 0)
    for j in range(out_ref.shape[0]):
        out_ref[j] = even[:, 4:12, 8:24, :]


def place_kernel(parts_ref, out_ref, sems):
    rows = parts_ref.shape[3]
    pairs = []
    for j in range(parts_ref.shape[0]):
        pairs.append((parts_ref.at[j], out_ref.at[:, :, j * rows : (j + 1) * rows, :]))
    for copy in fetch(pairs, sems):
        copy.wait()


def pinned(*arrays):
    return [pltpu.with_memory_space_constraint(x, pltpu.HBM) for x in arrays]


def call(kernel, out_shapes, ins, scratch=(), outs=None, us=1.0):
    outs = outs or [VMEM] * len(out_shapes)
    return pl.pallas_call(
        kernel,
        out_shape=[
            pltpu.HBM(s, F32) if spec is HBM else jax.ShapeDtypeStruct(s, F32)
            for s, spec in zip(out_shapes, outs)
        ],
        in_specs=ins,
        out_specs=outs,
        scratch_shapes=list(scratch),
        compiler_params=PARAMS,
        cost_estimate=pl.CostEstimate(flops=int(us * 1e9), bytes_accessed=int(us * 3.6e6), transcendentals=0),
    )


def pair_up(x, first, axis="slab"):
    pairs = [(i, i + 1) for i in range(first, lax.axis_size(axis) - 1, 2)]
    return lax.ppermute(x, axis, pairs + [(j, i) for i, j in pairs])


def body(velocity, part_vel, fraction, base_cell, drag_coeff, part_volume, brick_of_block):
    depth, width_x = velocity.shape[1], velocity.shape[2]
    blocks = brick_of_block.shape[0]
    subs = lax.axis_size("sub")
    slab = lax.axis_index("slab").astype(jnp.int32)
    sub = lax.axis_index("sub").astype(jnp.int32)
    tiles_x = width_x // 8
    tiles = tiles_x * 8
    share = tiles // subs
    base = base_cell.reshape(blocks, BLOCK)
    coef = drag_coeff.reshape(blocks, BLOCK)
    pvol = part_volume.reshape(blocks, BLOCK)

    particles_vmem = [
        pltpu.SMEM((blocks,), jnp.int32),
        pltpu.VMEM((blocks, BLOCK), jnp.int32),
        pltpu.VMEM((3, blocks * BLOCK), F32),
    ]
    row_vmem = pltpu.VMEM((blocks, BLOCK), F32)
    (solid,) = call(
        solid_kernel,
        [(tiles, 8, LANES)],
        [HBM] * 4,
        [pltpu.VMEM((tiles, 8, LANES), F32)]
        + particles_vmem
        + [row_vmem, pltpu.SemaphoreType.DMA((4,))],
        outs=[HBM],
        us=5.0,
    )(*pinned(brick_of_block, base, fraction, pvol))
    solid_parts = lax.all_to_all(solid.reshape(subs, share, 8, LANES), "sub", 0, 0)
    half = blocks // 2

    def slip_of(first, after, out):
        (slip,) = call(
            functools.partial(slip_kernel, first, half),
            [(3, half * BLOCK)],
            [HBM] * 8,
            [
                pltpu.VMEM((3, half * BLOCK), F32),
                pltpu.SMEM((blocks,), jnp.int32),
                pltpu.VMEM((half, BLOCK), jnp.int32),
                pltpu.VMEM((3, half * BLOCK), F32),
                pltpu.VMEM((3, half * BLOCK), F32),
                pltpu.VMEM((half, BLOCK), F32),
                pltpu.VMEM((half, BLOCK), F32),
                pltpu.VMEM(velocity.shape, F32),
                pltpu.VMEM((3 * tiles, 8, LANES), F32),
                pltpu.SemaphoreType.DMA((7,)),
            ],
            us=5.0,
            )(after, brick_of_block, base, fraction, part_vel, coef, pvol, velocity)
        return slip

    slip_a = slip_of(0, solid, HBM)
    (eps_copies,) = call(
        eps_kernel,
        [(subs, share, 8, LANES)],
        [VMEM],
        [pltpu.VMEM((share, 8, LANES), F32), pltpu.SemaphoreType.DMA((subs,))],
        outs=[HBM],
        us=0.5,
    )(solid_parts)
    slip_b = slip_of(half, eps_copies, ANY)
    eps = lax.all_to_all(eps_copies, "sub", 0, 0).reshape(tiles, 8, LANES)
    drag, force, tick = call(
        drag_kernel,
        [(3, blocks * BLOCK), (subs, 48, 8, LANES), (8, LANES)],
        [SMEM, VMEM, VMEM, HBM, VMEM, VMEM],
        [
            pltpu.VMEM((subs, 48, 8, LANES), F32),
            pltpu.VMEM((3, half * BLOCK), F32),
            pltpu.SemaphoreType.DMA((subs,)),
        ],
        outs=[VMEM, HBM, VMEM],
        us=6.0,
    )(brick_of_block, base, fraction, *pinned(slip_a), slip_b, eps)
    forces = lax.all_to_all(force, "sub", 0, 0)
    planes = depth * lax.axis_size("slab")
    place = jnp.stack([slab, sub, jnp.int32(planes), jnp.int32(width_x)])
    window, even, odd = call(
        window_kernel,
        [(3, depth, 32, LANES), (3, 4, 32, LANES), (3, 4, 32, LANES)],
        [SMEM, ANY, HBM],
        [pltpu.SemaphoreType.DMA((4,))],
    )(place, tick, *pinned(velocity))
    even, odd = pair_up(even, 0), pair_up(odd, 1)
    voidfraction, eps_own = call(
        void_kernel, [(depth, width_x, LANES), (share, 8, LANES)], [SMEM, ANY, VMEM], us=2.0
    )(place, tick, eps)
    first, first_tick = call(
        first_kernel,
        [(3, 14, 32, LANES), (8, LANES)],
        [SMEM] + [VMEM] * 3,
        [pltpu.VMEM((3, 16, 32, LANES), F32)],
        us=1.0,
    )(place, window, even, odd)

    rows = width_x // subs
    own, even, odd = call(
        source_kernel,
        [(3, depth, rows, LANES), (3, 4, 8, LANES), (3, 4, 8, LANES)],
        [SMEM, VMEM, VMEM, ANY],
    )(place, forces, eps_own, first_tick)
    even, odd = pair_up(even, 0, "sub"), pair_up(odd, 1, "sub")
    halo, even, odd = call(
        halo_kernel,
        [(3, depth, 8, LANES), (3, 3, 24, LANES), (3, 3, 24, LANES)],
        [SMEM] + [VMEM] * 3,
    )(place, own, even, odd)
    even, odd = pair_up(even, 0), pair_up(odd, 1)
    (moved,) = call(
        stencil_kernel,
        [(subs, 3, depth, rows, LANES)],
        [SMEM] + [VMEM] * 5,
        [
            pltpu.VMEM((3, 16, 32, LANES), F32),
            pltpu.VMEM((3, 16, 32, LANES), F32),
            pltpu.VMEM((3, 14, 32, LANES), F32),
        ],
        us=4.0,
    )(place, first, own, halo, even, odd)
    moved = lax.all_to_all(moved, "sub", 0, 0)
    (new_velocity,) = call(
        place_kernel,
        [velocity.shape],
        [ANY],
        [pltpu.SemaphoreType.DMA((subs,))],
        outs=[HBM],
    )(moved)
    return new_velocity, voidfraction, drag


def solution(mesh):
    in_specs = (
        P(None, "slab", None, None),
        P(None, ("slab", "sub")),
        P(None, ("slab", "sub")),
        P(("slab", "sub")),
        P(("slab", "sub")),
        P(("slab", "sub")),
        P(("slab", "sub")),
    )
    out_specs = (P(None, "slab", None, None), P("slab", None, None), P(None, ("slab", "sub")))
    return jax.shard_map(body, mesh=mesh, in_specs=in_specs, out_specs=out_specs, check_vma=False)
```

```python
import functools

import jax
import jax.numpy as jnp
from jax import lax
from jax.experimental import pallas as pl
from jax.experimental.pallas import tpu as pltpu
from jax.sharding import PartitionSpec as P

BLOCK = 128
LANES = 128
EPS_MIN = 0.35
FLOW_POWER = -0.2
DRAG_POWER = -2.65
VISCOSITY = 1.2
TIME_STEP = 0.05
ITERS = 4
UNROLL = 16
F32 = jnp.float32
PARAMS = pltpu.CompilerParams(vmem_limit_bytes=16 * 1024 * 1024)
VMEM = pl.BlockSpec(memory_space=pltpu.VMEM)
SMEM = pl.BlockSpec(memory_space=pltpu.SMEM)
HBM = pl.BlockSpec(memory_space=pltpu.HBM)
ANY = pl.BlockSpec(memory_space=pl.ANY)


def transpose_granules(tiles, lane):
    for bit in (1, 2, 4):
        shift = 8 * bit
        high = (lane & shift) != 0
        new = list(tiles)
        for a in range(8):
            if a & bit:
                continue
            b = a | bit
            va, vb = tiles[a], tiles[b]
            new[a] = jnp.where(high, pltpu.roll(vb, shift, 1), va)
            new[b] = jnp.where(high, vb, pltpu.roll(va, LANES - shift, 1))
        tiles = new
    return tiles


def fetch(pairs, sems):
    copies = [pltpu.make_async_copy(a, b, sems.at[i]) for i, (a, b) in enumerate(pairs)]
    for copy in copies:
        copy.start()
    return copies


def lanes_iota():
    return lax.broadcasted_iota(jnp.int32, (8, LANES), 1)


def rows_iota():
    return lax.broadcasted_iota(jnp.int32, (8, LANES), 0)


def spread(row):
    return jnp.broadcast_to(row, (8, LANES))


def particles(base_ref, frac_ref, block):
    at = pl.ds(pl.multiple_of(block * BLOCK, BLOCK), BLOCK)
    base = spread(base_ref[pl.ds(block, 1), :])
    fz = spread(frac_ref[0:1, at])
    fx = spread(frac_ref[1:2, at])
    fy = spread(frac_ref[2:3, at])
    return at, base >> 6, (base >> 3) & 7, base & 7, fz, fx, fy


def axis_weights(rows, first, frac):
    zero = jnp.zeros_like(frac)
    return jnp.where(rows == first, 1.0 - frac, jnp.where(rows == first + 1, frac, zero))


def halves(value):
    high = value.astype(jnp.bfloat16).astype(F32)
    return high, value - high


def plane_weights(rows, zb, yb, fz, fy):
    ky = axis_weights(rows, yb, fy)
    zero = jnp.zeros_like(fz)
    at = [zb == z for z in range(7)]
    parts = []
    for here, above in zip(halves((1.0 - fz) * ky), halves(fz * ky)):
        for z in range(8):
            part = zero if z == 0 else jnp.where(at[z - 1], above, zero)
            parts.append(part if z == 7 else jnp.where(at[z], here, part))
    return jnp.concatenate(parts, axis=0).astype(jnp.bfloat16)


def split_rows(parts):
    full = jnp.concatenate(parts, axis=0)
    high = full.astype(jnp.bfloat16).astype(F32)
    return jnp.concatenate([high, full - high], axis=0).astype(jnp.bfloat16)


def deposit(blocks):
    left = []
    for n, (parts, _) in enumerate(blocks):
        rows = split_rows(parts)
        pair = [rows, jnp.zeros_like(rows)]
        left.append(jnp.concatenate(pair if n == 0 else pair[::-1], axis=1))
    both = lax.dot_general(
        jnp.concatenate(left, axis=0),
        jnp.concatenate([weights for _, weights in blocks], axis=1),
        (((1,), (1,)), ((), ())),
        preferred_element_type=F32,
    )
    half = both.shape[0] // 4
    found = []
    for n in range(2):
        total = both[2 * n * half : (2 * n + 1) * half] + both[(2 * n + 1) * half : (2 * n + 2) * half]
        found.append(total + pltpu.roll(total, 64, 1))
    return found


def corner_terms(zb, yb, fz, fy, offset):
    index = (zb << 3) + yb + offset
    gz, gy = 1.0 - fz, 1.0 - fy
    return (
        (index, gz * gy),
        (index + 1, gz * fy),
        (index + 8, fz * gy),
        (index + 9, fz * fy),
    )


def interpolate(tile, kx, corners):
    total = None
    for index, weight in corners:
        term = weight * jnp.take_along_axis(tile, index, axis=1, mode="promise_in_bounds")
        total = term if total is None else total + term
    return jnp.sum(kx * total, axis=0, keepdims=True)


def brick_place(brick):
    return brick >> 4, brick & 7, (brick >> 3) & 1


def solid_kernel(
    brick_hbm, base_hbm, frac_hbm, pvol_hbm, out_hbm, tick_ref,
    out_ref, brick_ref, base_ref, frac_ref, pvol_ref, sems,
):
    copies = fetch(
        [(brick_hbm, brick_ref), (base_hbm, base_ref), (frac_hbm, frac_ref), (pvol_hbm, pvol_ref)],
        sems,
    )
    out_ref[...] = jnp.zeros_like(out_ref)
    for copy in copies:
        copy.wait()
    rows, lane = rows_iota(), lanes_iota()

    def step(number, carry):
        found = []
        for k in range(UNROLL):
            block = number * UNROLL + k
            _, zb, xb, yb, fz, fx, fy = particles(base_ref, frac_ref, block)
            kx = axis_weights(rows, xb, fx) * spread(pvol_ref[pl.ds(block, 1), :])
            found.append(([kx], plane_weights(rows, zb, yb, fz, fy)))
        found = sum((deposit(found[k : k + 2]) for k in range(0, UNROLL, 2)), [])
        for k in range(UNROLL):
            tx, t3, t1 = brick_place(brick_ref[number * UNROLL + k])
            tile = tx * 8 + t3
            out_ref[tile] += jnp.where((lane >> 6) == t1, found[k], 0.0)
        return carry

    lax.fori_loop(0, base_ref.shape[0] // UNROLL, step, 0)
    (copy,) = fetch([(out_ref, out_hbm)], sems)
    tick_ref[...] = jnp.zeros_like(tick_ref)
    copy.wait()


def eps_kernel(parts_ref, copies_hbm, tick_ref, out_ref, sems):
    tick_ref[...] = jnp.zeros_like(tick_ref)
    total = parts_ref[0]
    for j in range(1, parts_ref.shape[0]):
        total = total + parts_ref[j]
    total = jnp.maximum(1.0 - total, EPS_MIN)
    out_ref[...] = total
    for copy in fetch([(out_ref, copies_hbm.at[j]) for j in range(copies_hbm.shape[0])], sems):
        copy.wait()


def slip_kernel(
    first, count,
    after_any, brick_hbm, base_hbm, frac_hbm, pvel_hbm, coef_hbm, pvol_hbm, velocity_hbm,
    out_ref,
    brick_ref, base_ref, frac_ref, pvel_ref, coef_ref, pvol_ref, velocity_ref, table_ref, sems,
):
    some = pl.ds(first, count)
    wide = pl.ds(first * BLOCK, count * BLOCK)
    copies = fetch(
        [
            (velocity_hbm, velocity_ref),
            (brick_hbm, brick_ref),
            (base_hbm.at[some], base_ref),
            (frac_hbm.at[:, wide], frac_ref),
            (pvel_hbm.at[:, wide], pvel_ref),
            (coef_hbm.at[some], coef_ref),
            (pvol_hbm.at[some], pvol_ref),
        ],
        sems,
    )
    rows, lane = rows_iota(), lanes_iota()
    tiles_x = velocity_ref.shape[2] // 8

    def convert(number, carry):
        for k in range(2):
            tx = number * 2 + k
            at = pl.ds(pl.multiple_of(tx * 8, 8), 8)
            for c in range(3):
                tiles = transpose_granules([velocity_ref[c, z, at, :] for z in range(8)], lane)
                for t3 in range(8):
                    table_ref[(tx * 3 + c) * 8 + t3] = tiles[t3]
        return carry

    copies[0].wait()
    lax.fori_loop(0, tiles_x // 2, convert, 0)
    for copy in copies[1:]:
        copy.wait()

    def step(number, carry):
        for k in range(UNROLL):
            block = number * UNROLL + k
            at, zb, xb, yb, fz, fx, fy = particles(base_ref, frac_ref, block)
            tx, t3, t1 = brick_place(brick_ref[first + block])
            kx = axis_weights(rows, xb, fx)
            corners = corner_terms(zb, yb, fz, fy, t1 * 64)
            rel = [
                interpolate(table_ref[(tx * 3 + c) * 8 + t3], kx, corners) - pvel_ref[c : c + 1, at]
                for c in range(3)
            ]
            speed = rel[0] * rel[0] + rel[1] * rel[1] + rel[2] * rel[2]
            factor = coef_ref[pl.ds(block, 1), :] * pvol_ref[pl.ds(block, 1), :]
            factor = factor * jnp.exp(FLOW_POWER * jnp.log(speed + 0.01))
            for c in range(3):
                out_ref[c : c + 1, at] = factor * rel[c]
        return carry

    lax.fori_loop(0, count // UNROLL, step, 0)


def drag_kernel(
    brick_ref, base_ref, frac_ref, slip_a_ref, slip_b_ref, eps_ref,
    drag_ref, out_hbm, tick_ref,
    force_ref, sems,
):
    subs = force_ref.shape[0]
    rows, lane = rows_iota(), lanes_iota()
    for j in range(subs):
        force_ref[j] = jnp.zeros(force_ref.shape[1:], F32)

    for slip_ref, start in ((slip_a_ref, 0), (slip_b_ref, slip_a_ref.shape[1] // BLOCK)):

        def step(number, carry, slip_ref=slip_ref, start=start):
            found = []
            for k in range(UNROLL):
                inner = number * UNROLL + k
                block = inner + start
                at, zb, xb, yb, fz, fx, fy = particles(base_ref, frac_ref, block)
                inner_at = pl.ds(pl.multiple_of(inner * BLOCK, BLOCK), BLOCK)
                tx, t3, t1 = brick_place(brick_ref[block])
                kx = axis_weights(rows, xb, fx)
                eps = interpolate(eps_ref[tx * 8 + t3], kx, corner_terms(zb, yb, fz, fy, t1 * 64))
                factor = jnp.exp(DRAG_POWER * jnp.log(eps))
                parts = []
                for c in range(3):
                    force = factor * slip_ref[c : c + 1, inner_at]
                    drag_ref[c : c + 1, at] = force
                    parts.append(kx * spread(force))
                found.append((parts, plane_weights(rows, zb, yb, fz, fy)))
            found = sum((deposit(found[k : k + 2]) for k in range(0, UNROLL, 2)), [])
            for k in range(UNROLL):
                tx, t3, t1 = brick_place(brick_ref[number * UNROLL + k + start])
                mine = (lane >> 6) == t1
                for c in range(3):
                    tile = (tx & 1) * 24 + c * 8 + t3
                    force_ref[tx >> 1, tile] += jnp.where(mine, found[k][8 * c : 8 * c + 8], 0.0)
            return carry

        lax.fori_loop(0, slip_ref.shape[1] // BLOCK // UNROLL, step, 0)
    tick_ref[...] = jnp.zeros_like(tick_ref)
    for copy in fetch([(force_ref.at[j], out_hbm.at[j]) for j in range(subs)], sems):
        copy.wait()


def source_kernel(place_ref, parts_ref, eps_ref, first_any, own_ref, *out_refs):
    sub_refs, slab_refs, both_refs = out_refs[:2], out_refs[2:4], out_refs[4:]
    lane, rows = lanes_iota(), rows_iota()
    slab_even, sub_even = place_ref[0] % 2 == 0, place_ref[1] % 2 == 0

    def swapped(flag, one, two):
        return jnp.where(flag, one, two), jnp.where(flag, two, one)

    for c in range(3):
        grid = []
        for t in range(2):
            tiles = []
            for t3 in range(8):
                at = (t * 3 + c) * 8 + t3
                total = parts_ref[0, at]
                for j in range(1, parts_ref.shape[0]):
                    total = total + parts_ref[j, at]
                tiles.append(-total / eps_ref[t * 8 + t3])
            tiles = transpose_granules(tiles, lane)
            for z in range(8):
                own_ref[c, z, 8 * t : 8 * t + 8, :] = tiles[z]
            grid.append(tiles)

        def packed(z, y):
            first = jnp.where(rows < 4, grid[0][z], pltpu.roll(grid[0][y], 4, 0))
            last = jnp.where(rows < 4, pltpu.roll(grid[1][z], 4, 0), grid[1][y])
            return swapped(sub_even, last, first)

        for q in range(4):
            for ref, tile in zip(sub_refs, packed(2 * q, 2 * q + 1)):
                ref[c, q] = tile
        for n in range(3):
            for t in range(2):
                pair = swapped(slab_even, grid[t][5 + n], grid[t][n])
                for ref, tile in zip(slab_refs, pair):
                    ref[c, n, 8 * t : 8 * t + 8, :] = tile
        for q in range(2):
            high, low = packed(5 + 2 * q, 6 + q), packed(2 * q, 1 + q)
            for m in range(2):
                pair = swapped(slab_even, high[m], low[m])
                for p in range(2):
                    both_refs[2 * p + m][c, q] = pair[p]


def window_kernel(place_ref, after_any, velocity_hbm, out_ref, even_ref, odd_ref, sems):
    even = place_ref[0] % 2 == 0
    depth = velocity_hbm.shape[1]
    tiles_x = velocity_hbm.shape[2] // 8
    pairs, inside = [], []
    for r in range(4):
        want = place_ref[1] * 2 + r - 1
        inside.append(jnp.logical_and(want >= 0, want < tiles_x))
        at = pl.ds(pl.multiple_of(jnp.clip(want, 0, tiles_x - 1) * 8, 8), 8)
        pairs.append((velocity_hbm.at[:, :, at, :], out_ref.at[:, :, 8 * r : 8 * r + 8, :]))
    for copy in fetch(pairs, sems):
        copy.wait()
    for r in range(4):
        at = slice(8 * r, 8 * r + 8)
        rows = jnp.where(inside[r], out_ref[:, :, at, :], 0.0)
        out_ref[:, :, at, :] = rows
        even_ref[:, :, at, :] = jnp.where(even, rows[:, depth - 4 :], rows[:, :4])
        odd_ref[:, :, at, :] = jnp.where(even, rows[:, :4], rows[:, depth - 4 :])


def void_kernel(place_ref, after_any, eps_ref, out_ref, own_ref):
    lane = lanes_iota()

    def convert(number, carry):
        for k in range(4):
            tx = number * 4 + k
            tiles = transpose_granules([eps_ref[tx * 8 + t3] for t3 in range(8)], lane)
            for z in range(8):
                out_ref[z, pl.ds(pl.multiple_of(tx * 8, 8), 8), :] = tiles[z]
        return carry

    lax.fori_loop(0, out_ref.shape[1] // 32, convert, 0)
    own_ref[...] = eps_ref[pl.ds(place_ref[1] * own_ref.shape[0], own_ref.shape[0])]


def edges(slab, sub, planes, width):
    row = lax.broadcasted_iota(jnp.int32, (32, LANES), 0) + sub * 16 - 8
    inside_x = jnp.logical_and(row >= 0, row < width)

    def keep(z):
        height = slab * 8 - 4 + z
        return jnp.logical_and(inside_x, jnp.logical_and(height >= 0, height < planes))

    return keep


def unforced(old, z, lane):
    shear = None
    centres, laps = [], []
    for c in range(3):
        centre = old[c, z]
        upper = old[c, z + 1]
        lower = old[c, z - 1]
        east = pltpu.roll(centre, 31, 0)
        west = pltpu.roll(centre, 1, 0)
        north = jnp.where(lane == LANES - 1, 0.0, pltpu.roll(centre, LANES - 1, 1))
        south = jnp.where(lane == 0, 0.0, pltpu.roll(centre, 1, 1))
        term = (upper - centre) ** 2 + (east - centre) ** 2 + (north - centre) ** 2
        shear = term if shear is None else shear + term
        centres.append(centre)
        laps.append(upper + lower + east + west + north + south - 6.0 * centre)
    viscous = (TIME_STEP * VISCOSITY) * jnp.exp(FLOW_POWER * jnp.log(shear + 0.01))
    return [centres[c] + viscous * laps[c] for c in range(3)]


def first_kernel(place_ref, window_ref, even_ref, odd_ref, out_ref, tick_ref, old):
    tick_ref[...] = jnp.zeros_like(tick_ref)
    side = place_ref[0] % 2
    old[:, pl.ds(12 - 12 * side, 4)] = even_ref[...]
    old[:, pl.ds(12 * side, 4)] = odd_ref[...]
    old[:, 4:12] = window_ref[...]
    lane = lax.broadcasted_iota(jnp.int32, (32, LANES), 1)

    def plane(number, carry):
        for k in range(2):
            z = number * 2 + k
            moved = unforced(old, z + 1, lane)
            for c in range(3):
                out_ref[c, z] = moved[c]
        return carry

    lax.fori_loop(0, 7, plane, 0)


def stencil_kernel(
    place_ref, first_ref, own_ref, *refs
):
    sub_refs, slab_refs, both_refs = refs[:2], refs[2:4], refs[4:8]
    out_ref, even, odd, source = refs[8:]
    keep = edges(place_ref[0], place_ref[1], place_ref[2], place_ref[3])
    lane = lax.broadcasted_iota(jnp.int32, (32, LANES), 1)
    above, after = place_ref[0] % 2 == 0, place_ref[1] % 2 == 0
    top = jnp.where(above, 11, 0)
    right = pl.multiple_of(jnp.where(after, 24, 0), 8)
    source[:, 3:11, 8:24, :] = own_ref[...]
    planes = (pl.ds(top, 3), pl.ds(11 - top, 3))
    for p in range(2):
        source[:, planes[p], 8:24, :] = slab_refs[p][...]
    for m in range(2):
        row = pl.ds(pl.multiple_of(24 * m + (1 - 2 * m) * right, 8), 8)
        front = after if m == 0 else jnp.logical_not(after)
        for c in range(3):
            for ref, start, count in (
                (sub_refs[m], 3, 8),
                (both_refs[m], top, 3),
                (both_refs[2 + m], 11 - top, 3),
            ):
                for n in range(count):
                    tile = ref[c, n // 2]
                    moved = pltpu.roll(tile, 4, 0)
                    straight = front if n % 2 == 0 else jnp.logical_not(front)
                    source[c, start + n, row, :] = jnp.where(straight, tile, moved)

    def first(number, carry):
        for k in range(2):
            z = number * 2 + k
            inside = keep(z + 1)
            for c in range(3):
                moved = first_ref[c, z] + TIME_STEP * source[c, z]
                odd[c, z + 1] = jnp.where(inside, moved, 0.0)
        return carry

    lax.fori_loop(0, 7, first, 0)
    buffers = (even, odd)
    for step in range(1, ITERS):
        old, new = buffers[step % 2], buffers[(step + 1) % 2]

        def plane(number, carry, old=old, new=new, step=step):
            for k in range(2):
                z = number * 2 + k + step + 1
                moved = unforced(old, z, lane)
                inside = keep(z)
                for c in range(3):
                    forced = moved[c] + TIME_STEP * source[c, z - 1]
                    new[c, z] = jnp.where(inside, forced, 0.0)
            return carry

        lax.fori_loop(0, 7 - step, plane, 0)
    for j in range(out_ref.shape[0]):
        out_ref[j] = even[:, 4:12, 8:24, :]


def place_kernel(parts_ref, out_ref, sems):
    rows = parts_ref.shape[3]
    pairs = []
    for j in range(parts_ref.shape[0]):
        pairs.append((parts_ref.at[j], out_ref.at[:, :, j * rows : (j + 1) * rows, :]))
    for copy in fetch(pairs, sems):
        copy.wait()


def pinned(*arrays):
    return [pltpu.with_memory_space_constraint(x, pltpu.HBM) for x in arrays]


def call(kernel, out_shapes, ins, scratch=(), outs=None, us=1.0):
    outs = outs or [VMEM] * len(out_shapes)
    return pl.pallas_call(
        kernel,
        out_shape=[
            pltpu.HBM(s, F32) if spec is HBM else jax.ShapeDtypeStruct(s, F32)
            for s, spec in zip(out_shapes, outs)
        ],
        in_specs=ins,
        out_specs=outs,
        scratch_shapes=list(scratch),
        compiler_params=PARAMS,
        cost_estimate=pl.CostEstimate(flops=int(us * 1e9), bytes_accessed=int(us * 3.6e6), transcendentals=0),
    )


def pair_up(x, slab_first, sub_first):
    partners = []
    for axis, first in (("slab", slab_first), ("sub", sub_first)):
        size = lax.axis_size(axis)
        if first is None:
            partners.append({i: i for i in range(size)})
        else:
            pairs = [(i, i + 1) for i in range(first, size - 1, 2)]
            partners.append(dict(pairs + [(j, i) for i, j in pairs]))
    subs = lax.axis_size("sub")
    moves = [(i * subs + j, k * subs + n) for i, k in partners[0].items() for j, n in partners[1].items()]
    return lax.ppermute(x, ("slab", "sub"), moves)


def body(velocity, part_vel, fraction, base_cell, drag_coeff, part_volume, brick_of_block):
    depth, width_x = velocity.shape[1], velocity.shape[2]
    blocks = brick_of_block.shape[0]
    subs = lax.axis_size("sub")
    slab = lax.axis_index("slab").astype(jnp.int32)
    sub = lax.axis_index("sub").astype(jnp.int32)
    tiles_x = width_x // 8
    tiles = tiles_x * 8
    share = tiles // subs
    base = base_cell.reshape(blocks, BLOCK)
    coef = drag_coeff.reshape(blocks, BLOCK)
    pvol = part_volume.reshape(blocks, BLOCK)

    particles_vmem = [
        pltpu.SMEM((blocks,), jnp.int32),
        pltpu.VMEM((blocks, BLOCK), jnp.int32),
        pltpu.VMEM((3, blocks * BLOCK), F32),
    ]
    row_vmem = pltpu.VMEM((blocks, BLOCK), F32)
    solid, solid_tick = call(
        solid_kernel,
        [(tiles, 8, LANES), (8, LANES)],
        [HBM] * 4,
        [pltpu.VMEM((tiles, 8, LANES), F32)]
        + particles_vmem
        + [row_vmem, pltpu.SemaphoreType.DMA((4,))],
        outs=[HBM, VMEM],
        us=5.0,
    )(*pinned(brick_of_block, base, fraction, pvol))
    solid_parts = lax.all_to_all(solid.reshape(subs, share, 8, LANES), "sub", 0, 0)
    half = blocks // 2

    def slip_of(first, after):
        (slip,) = call(
            functools.partial(slip_kernel, first, half),
            [(3, half * BLOCK)],
            [ANY] + [HBM] * 7,
            [
                pltpu.SMEM((blocks,), jnp.int32),
                pltpu.VMEM((half, BLOCK), jnp.int32),
                pltpu.VMEM((3, half * BLOCK), F32),
                pltpu.VMEM((3, half * BLOCK), F32),
                pltpu.VMEM((half, BLOCK), F32),
                pltpu.VMEM((half, BLOCK), F32),
                pltpu.VMEM(velocity.shape, F32),
                pltpu.VMEM((3 * tiles, 8, LANES), F32),
                pltpu.SemaphoreType.DMA((7,)),
            ],
            us=5.0,
            )(after, brick_of_block, base, fraction, part_vel, coef, pvol, velocity)
        return slip

    slip_a = slip_of(0, solid_tick)
    eps_copies, eps_tick = call(
        eps_kernel,
        [(subs, share, 8, LANES), (8, LANES)],
        [VMEM],
        [pltpu.VMEM((share, 8, LANES), F32), pltpu.SemaphoreType.DMA((subs,))],
        outs=[HBM, VMEM],
        us=0.5,
    )(solid_parts)
    slip_b = slip_of(half, eps_tick)
    eps = lax.all_to_all(eps_copies, "sub", 0, 0).reshape(tiles, 8, LANES)
    drag, force, tick = call(
        drag_kernel,
        [(3, blocks * BLOCK), (subs, 48, 8, LANES), (8, LANES)],
        [SMEM] + [VMEM] * 5,
        [
            pltpu.VMEM((subs, 48, 8, LANES), F32),
            pltpu.SemaphoreType.DMA((subs,)),
        ],
        outs=[VMEM, HBM, VMEM],
        us=6.0,
    )(brick_of_block, base, fraction, slip_a, slip_b, eps)
    forces = lax.all_to_all(force, "sub", 0, 0)
    planes = depth * lax.axis_size("slab")
    place = jnp.stack([slab, sub, jnp.int32(planes), jnp.int32(width_x)])
    window, even, odd = call(
        window_kernel,
        [(3, depth, 32, LANES), (3, 4, 32, LANES), (3, 4, 32, LANES)],
        [SMEM, ANY, HBM],
        [pltpu.SemaphoreType.DMA((4,))],
    )(place, tick, *pinned(velocity))
    even, odd = pair_up(even, 0, None), pair_up(odd, 1, None)
    voidfraction, eps_own = call(
        void_kernel, [(depth, width_x, LANES), (share, 8, LANES)], [SMEM, ANY, VMEM], us=2.0
    )(place, tick, eps)
    first, first_tick = call(
        first_kernel,
        [(3, 14, 32, LANES), (8, LANES)],
        [SMEM] + [VMEM] * 3,
        [pltpu.VMEM((3, 16, 32, LANES), F32)],
        us=1.0,
    )(place, window, even, odd)

    rows = width_x // subs
    own, *sent = call(
        source_kernel,
        [(3, depth, rows, LANES)]
        + [(3, 4, 8, LANES)] * 2
        + [(3, 3, rows, LANES)] * 2
        + [(3, 2, 8, LANES)] * 4,
        [SMEM, VMEM, VMEM, ANY],
    )(place, forces, eps_own, first_tick)
    pairings = [(None, 0), (None, 1), (0, None), (1, None), (0, 0), (0, 1), (1, 0), (1, 1)]
    halos = [pair_up(x, *pairing) for x, pairing in zip(sent, pairings)]
    (moved,) = call(
        stencil_kernel,
        [(subs, 3, depth, rows, LANES)],
        [SMEM] + [VMEM] * 10,
        [
            pltpu.VMEM((3, 16, 32, LANES), F32),
            pltpu.VMEM((3, 16, 32, LANES), F32),
            pltpu.VMEM((3, 14, 32, LANES), F32),
        ],
        us=4.0,
    )(place, first, own, *halos)
    moved = lax.all_to_all(moved, "sub", 0, 0)
    (new_velocity,) = call(
        place_kernel,
        [velocity.shape],
        [ANY],
        [pltpu.SemaphoreType.DMA((subs,))],
        outs=[HBM],
    )(moved)
    return new_velocity, voidfraction, drag


def solution(mesh):
    in_specs = (
        P(None, "slab", None, None),
        P(None, ("slab", "sub")),
        P(None, ("slab", "sub")),
        P(("slab", "sub")),
        P(("slab", "sub")),
        P(("slab", "sub")),
        P(("slab", "sub")),
    )
    out_specs = (P(None, "slab", None, None), P("slab", None, None), P(None, ("slab", "sub")))
    return jax.shard_map(body, mesh=mesh, in_specs=in_specs, out_specs=out_specs, check_vma=False)
```

```python
import functools

import jax
import jax.numpy as jnp
from jax import lax
from jax.experimental import pallas as pl
from jax.experimental.pallas import tpu as pltpu
from jax.sharding import PartitionSpec as P

BLOCK = 128
LANES = 128
EPS_MIN = 0.35
FLOW_POWER = -0.2
DRAG_POWER = -2.65
VISCOSITY = 1.2
TIME_STEP = 0.05
ITERS = 4
UNROLL = 16
F32 = jnp.float32
PARAMS = pltpu.CompilerParams(vmem_limit_bytes=16 * 1024 * 1024)
VMEM = pl.BlockSpec(memory_space=pltpu.VMEM)
SMEM = pl.BlockSpec(memory_space=pltpu.SMEM)
HBM = pl.BlockSpec(memory_space=pltpu.HBM)
ANY = pl.BlockSpec(memory_space=pl.ANY)


def transpose_granules(tiles, lane):
    for bit in (1, 2, 4):
        shift = 8 * bit
        high = (lane & shift) != 0
        new = list(tiles)
        for a in range(8):
            if a & bit:
                continue
            b = a | bit
            va, vb = tiles[a], tiles[b]
            new[a] = jnp.where(high, pltpu.roll(vb, shift, 1), va)
            new[b] = jnp.where(high, vb, pltpu.roll(va, LANES - shift, 1))
        tiles = new
    return tiles


def fetch(pairs, sems):
    copies = [pltpu.make_async_copy(a, b, sems.at[i]) for i, (a, b) in enumerate(pairs)]
    for copy in copies:
        copy.start()
    return copies


def lanes_iota():
    return lax.broadcasted_iota(jnp.int32, (8, LANES), 1)


def rows_iota():
    return lax.broadcasted_iota(jnp.int32, (8, LANES), 0)


def spread(row):
    return jnp.broadcast_to(row, (8, LANES))


def particles(base_ref, frac_ref, block):
    at = pl.ds(pl.multiple_of(block * BLOCK, BLOCK), BLOCK)
    base = spread(base_ref[pl.ds(block, 1), :])
    fz = spread(frac_ref[0:1, at])
    fx = spread(frac_ref[1:2, at])
    fy = spread(frac_ref[2:3, at])
    return at, base >> 6, (base >> 3) & 7, base & 7, fz, fx, fy


def axis_weights(rows, first, frac):
    zero = jnp.zeros_like(frac)
    return jnp.where(rows == first, 1.0 - frac, jnp.where(rows == first + 1, frac, zero))


def halves(value):
    high = value.astype(jnp.bfloat16).astype(F32)
    return high, value - high


def plane_weights(rows, zb, yb, fz, fy):
    ky = axis_weights(rows, yb, fy)
    zero = jnp.zeros_like(fz)
    at = [zb == z for z in range(7)]
    parts = []
    for here, above in zip(halves((1.0 - fz) * ky), halves(fz * ky)):
        for z in range(8):
            part = zero if z == 0 else jnp.where(at[z - 1], above, zero)
            parts.append(part if z == 7 else jnp.where(at[z], here, part))
    return jnp.concatenate(parts, axis=0).astype(jnp.bfloat16)


def split_rows(parts):
    full = jnp.concatenate(parts, axis=0)
    high = full.astype(jnp.bfloat16).astype(F32)
    return jnp.concatenate([high, full - high], axis=0).astype(jnp.bfloat16)


def deposit(blocks):
    left = []
    for n, (parts, _) in enumerate(blocks):
        rows = split_rows(parts)
        pair = [rows, jnp.zeros_like(rows)]
        left.append(jnp.concatenate(pair if n == 0 else pair[::-1], axis=1))
    both = lax.dot_general(
        jnp.concatenate(left, axis=0),
        jnp.concatenate([weights for _, weights in blocks], axis=1),
        (((1,), (1,)), ((), ())),
        preferred_element_type=F32,
    )
    half = both.shape[0] // 4
    found = []
    for n in range(2):
        total = both[2 * n * half : (2 * n + 1) * half] + both[(2 * n + 1) * half : (2 * n + 2) * half]
        found.append(total + pltpu.roll(total, 64, 1))
    return found


def corner_terms(zb, yb, fz, fy, offset):
    index = (zb << 3) + yb + offset
    gz, gy = 1.0 - fz, 1.0 - fy
    return (
        (index, gz * gy),
        (index + 1, gz * fy),
        (index + 8, fz * gy),
        (index + 9, fz * fy),
    )


def interpolate(tile, kx, corners):
    total = None
    for index, weight in corners:
        term = weight * jnp.take_along_axis(tile, index, axis=1, mode="promise_in_bounds")
        total = term if total is None else total + term
    return jnp.sum(kx * total, axis=0, keepdims=True)


def interpolate_pair(blocks):
    lane = lanes_iota()
    left = []
    for n, (tile, t1, _, _) in enumerate(blocks):
        brick = jnp.where((lane >> 6) == t1, tile, 0.0)
        rows = split_rows([brick + pltpu.roll(brick, 64, 1)])
        pair = [rows, jnp.zeros_like(rows)]
        left.append(jnp.concatenate(pair if n == 0 else pair[::-1], axis=1))
    both = jnp.dot(
        jnp.concatenate(left, axis=0),
        jnp.concatenate([weights for _, _, _, weights in blocks], axis=0),
        preferred_element_type=F32,
    )
    found = []
    for n, (_, _, kx, _) in enumerate(blocks):
        total = both[16 * n : 16 * n + 8] + both[16 * n + 8 : 16 * n + 16]
        found.append(jnp.sum(kx * total, axis=0, keepdims=True))
    return found


def brick_place(brick):
    return brick >> 4, brick & 7, (brick >> 3) & 1


def solid_kernel(
    brick_hbm, base_hbm, frac_hbm, pvol_hbm, out_hbm, tick_ref,
    out_ref, brick_ref, base_ref, frac_ref, pvol_ref, sems,
):
    copies = fetch(
        [(brick_hbm, brick_ref), (base_hbm, base_ref), (frac_hbm, frac_ref), (pvol_hbm, pvol_ref)],
        sems,
    )
    out_ref[...] = jnp.zeros_like(out_ref)
    for copy in copies:
        copy.wait()
    rows, lane = rows_iota(), lanes_iota()

    def step(number, carry):
        found = []
        for k in range(UNROLL):
            block = number * UNROLL + k
            _, zb, xb, yb, fz, fx, fy = particles(base_ref, frac_ref, block)
            kx = axis_weights(rows, xb, fx) * spread(pvol_ref[pl.ds(block, 1), :])
            found.append(([kx], plane_weights(rows, zb, yb, fz, fy)))
        found = sum((deposit(found[k : k + 2]) for k in range(0, UNROLL, 2)), [])
        for k in range(UNROLL):
            tx, t3, t1 = brick_place(brick_ref[number * UNROLL + k])
            tile = tx * 8 + t3
            out_ref[tile] += jnp.where((lane >> 6) == t1, found[k], 0.0)
        return carry

    lax.fori_loop(0, base_ref.shape[0] // UNROLL, step, 0)
    (copy,) = fetch([(out_ref, out_hbm)], sems)
    tick_ref[...] = jnp.zeros_like(tick_ref)
    copy.wait()


def eps_kernel(parts_ref, copies_hbm, tick_ref, out_ref, sems):
    tick_ref[...] = jnp.zeros_like(tick_ref)
    total = parts_ref[0]
    for j in range(1, parts_ref.shape[0]):
        total = total + parts_ref[j]
    total = jnp.maximum(1.0 - total, EPS_MIN)
    out_ref[...] = total
    for copy in fetch([(out_ref, copies_hbm.at[j]) for j in range(copies_hbm.shape[0])], sems):
        copy.wait()


def slip_kernel(
    first, count,
    after_any, brick_hbm, base_hbm, frac_hbm, pvel_hbm, coef_hbm, pvol_hbm, velocity_hbm,
    out_ref,
    brick_ref, base_ref, frac_ref, pvel_ref, coef_ref, pvol_ref, velocity_ref, table_ref, sems,
):
    some = pl.ds(first, count)
    wide = pl.ds(first * BLOCK, count * BLOCK)
    copies = fetch(
        [
            (velocity_hbm, velocity_ref),
            (brick_hbm, brick_ref),
            (base_hbm.at[some], base_ref),
            (frac_hbm.at[:, wide], frac_ref),
            (pvel_hbm.at[:, wide], pvel_ref),
            (coef_hbm.at[some], coef_ref),
            (pvol_hbm.at[some], pvol_ref),
        ],
        sems,
    )
    rows, lane = rows_iota(), lanes_iota()
    tiles_x = velocity_ref.shape[2] // 8

    def convert(number, carry):
        for k in range(2):
            tx = number * 2 + k
            at = pl.ds(pl.multiple_of(tx * 8, 8), 8)
            for c in range(3):
                tiles = transpose_granules([velocity_ref[c, z, at, :] for z in range(8)], lane)
                for t3 in range(8):
                    table_ref[(tx * 3 + c) * 8 + t3] = tiles[t3]
        return carry

    copies[0].wait()
    lax.fori_loop(0, tiles_x // 2, convert, 0)
    for copy in copies[1:]:
        copy.wait()

    def step(number, carry):
        for k in range(UNROLL):
            block = number * UNROLL + k
            at, zb, xb, yb, fz, fx, fy = particles(base_ref, frac_ref, block)
            tx, t3, t1 = brick_place(brick_ref[first + block])
            kx = axis_weights(rows, xb, fx)
            corners = corner_terms(zb, yb, fz, fy, t1 * 64)
            rel = [
                interpolate(table_ref[(tx * 3 + c) * 8 + t3], kx, corners) - pvel_ref[c : c + 1, at]
                for c in range(3)
            ]
            speed = rel[0] * rel[0] + rel[1] * rel[1] + rel[2] * rel[2]
            factor = coef_ref[pl.ds(block, 1), :] * pvol_ref[pl.ds(block, 1), :]
            factor = factor * jnp.exp(FLOW_POWER * jnp.log(speed + 0.01))
            for c in range(3):
                out_ref[c : c + 1, at] = factor * rel[c]
        return carry

    lax.fori_loop(0, count // UNROLL, step, 0)


def pack_halo(rows, tiles):
    a, b, c, d = tiles
    middle = jnp.logical_or(rows == 3, rows == 4)
    first = jnp.where(middle, pltpu.roll(d, 3, 0), a)
    second = jnp.where(rows == 3, pltpu.roll(d, 1, 0), jnp.where(rows == 4, pltpu.roll(d, 7, 0), b))
    third = jnp.where(middle, pltpu.roll(d, 5, 0), c)
    return first, second, third


def unpack_halo(rows, tiles):
    a, b, c = tiles
    inner = jnp.where(rows == 2, pltpu.roll(b, 7, 0), pltpu.roll(b, 1, 0))
    d = jnp.where(rows < 2, pltpu.roll(a, 5, 0), jnp.where(rows > 5, pltpu.roll(c, 3, 0), inner))
    return a, b, c, d


def drag_kernel(
    brick_ref, base_ref, frac_ref, slip_a_ref, slip_b_ref, eps_ref,
    drag_ref, out_hbm, tick_ref,
    force_ref, sems,
):
    subs = force_ref.shape[0]
    rows, lane = rows_iota(), lanes_iota()
    for j in range(subs):
        force_ref[j, 0:48] = jnp.zeros((48, 8, LANES), F32)

    for slip_ref, start in ((slip_a_ref, 0), (slip_b_ref, slip_a_ref.shape[1] // BLOCK)):

        def step(number, carry, slip_ref=slip_ref, start=start):
            known = []
            for k in range(UNROLL):
                block = number * UNROLL + k + start
                _, zb, xb, yb, fz, fx, fy = particles(base_ref, frac_ref, block)
                tx, t3, t1 = brick_place(brick_ref[block])
                kx = axis_weights(rows, xb, fx)
                known.append((eps_ref[tx * 8 + t3], t1, kx, plane_weights(rows, zb, yb, fz, fy)))
            at_particles = sum((interpolate_pair(known[k : k + 2]) for k in range(0, UNROLL, 2)), [])
            found = []
            for k in range(UNROLL):
                inner = number * UNROLL + k
                inner_at = pl.ds(pl.multiple_of(inner * BLOCK, BLOCK), BLOCK)
                at = pl.ds(pl.multiple_of((inner + start) * BLOCK, BLOCK), BLOCK)
                _, _, kx, weights = known[k]
                factor = jnp.exp(DRAG_POWER * jnp.log(at_particles[k]))
                parts = []
                for c in range(3):
                    force = factor * slip_ref[c : c + 1, inner_at]
                    drag_ref[c : c + 1, at] = force
                    parts.append(kx * spread(force))
                found.append((parts, weights))
            found = sum((deposit(found[k : k + 2]) for k in range(0, UNROLL, 2)), [])
            for k in range(UNROLL):
                tx, t3, t1 = brick_place(brick_ref[number * UNROLL + k + start])
                mine = (lane >> 6) == t1
                for c in range(3):
                    tile = (tx & 1) * 24 + c * 8 + t3
                    force_ref[tx >> 1, tile] += jnp.where(mine, found[k][8 * c : 8 * c + 8], 0.0)
            return carry

        lax.fori_loop(0, slip_ref.shape[1] // BLOCK // UNROLL, step, 0)
    copies = fetch([(force_ref.at[j, 0:48], out_hbm.at[j, 0:48]) for j in range(subs)], sems)
    zero = jnp.zeros((8, LANES), F32)
    tick_ref[...] = zero
    for j in range(subs):
        for quad in range(6):
            tiles = []
            for at in range(quad * 4, quad * 4 + 4):
                after = force_ref[j + 1, at] if j + 1 < subs else zero
                before = force_ref[j - 1, 24 + at] if j > 0 else zero
                tiles.append(jnp.where(rows < 4, after, before))
            for n, tile in enumerate(pack_halo(rows, tiles)):
                force_ref[j, 48 + quad * 3 + n] = tile
        copy = pltpu.make_async_copy(
            force_ref.at[j, 48:66], out_hbm.at[j, 48:66], sems.at[subs + j]
        )
        copy.start()
        copies.append(copy)
    for copy in copies:
        copy.wait()


def source_kernel(place_ref, parts_ref, eps_ref, first_any, own_ref, even_ref, odd_ref):
    lane, rows = lanes_iota(), rows_iota()
    even = place_ref[0] % 2 == 0

    def summed(at):
        total = parts_ref[0, at]
        for j in range(1, parts_ref.shape[0]):
            total = total + parts_ref[j, at]
        return total

    for t in range(3):
        for c in range(3):
            if t < 2:
                forces = [summed(t * 24 + c * 8 + t3) for t3 in range(8)]
            else:
                forces = []
                for quad in (2 * c, 2 * c + 1):
                    forces += unpack_halo(rows, [summed(48 + quad * 3 + k) for k in range(3)])
            tiles = []
            for t3 in range(8):
                tiles.append(-forces[t3] / eps_ref[t * 8 + t3])
            tiles = transpose_granules(tiles, lane)
            first = 8 * (t + 1) % 24
            for z in range(8):
                own_ref[c, z, first : first + 8, :] = tiles[z]
            for n in range(3):
                at = slice(first, first + 8)
                even_ref[c, n, at, :] = jnp.where(even, tiles[5 + n], tiles[n])
                odd_ref[c, n, at, :] = jnp.where(even, tiles[n], tiles[5 + n])


def window_kernel(place_ref, after_any, velocity_hbm, out_ref, even_ref, odd_ref, sems):
    even = place_ref[0] % 2 == 0
    depth = velocity_hbm.shape[1]
    tiles_x = velocity_hbm.shape[2] // 8
    pairs, inside = [], []
    for r in range(4):
        want = place_ref[1] * 2 + r - 1
        inside.append(jnp.logical_and(want >= 0, want < tiles_x))
        at = pl.ds(pl.multiple_of(jnp.clip(want, 0, tiles_x - 1) * 8, 8), 8)
        pairs.append((velocity_hbm.at[:, :, at, :], out_ref.at[:, :, 8 * r : 8 * r + 8, :]))
    for copy in fetch(pairs, sems):
        copy.wait()
    for r in range(4):
        at = slice(8 * r, 8 * r + 8)
        rows = jnp.where(inside[r], out_ref[:, :, at, :], 0.0)
        out_ref[:, :, at, :] = rows
        even_ref[:, :, at, :] = jnp.where(even, rows[:, depth - 4 :], rows[:, :4])
        odd_ref[:, :, at, :] = jnp.where(even, rows[:, :4], rows[:, depth - 4 :])


def void_kernel(place_ref, after_any, eps_ref, out_ref, near_ref):
    lane, rows = lanes_iota(), rows_iota()
    tiles_x = out_ref.shape[1] // 8

    def convert(number, carry):
        for k in range(4):
            tx = number * 4 + k
            tiles = transpose_granules([eps_ref[tx * 8 + t3] for t3 in range(8)], lane)
            for z in range(8):
                out_ref[z, pl.ds(pl.multiple_of(tx * 8, 8), 8), :] = tiles[z]
        return carry

    lax.fori_loop(0, tiles_x // 4, convert, 0)
    own = place_ref[1] * 2
    near_ref[0:16] = eps_ref[pl.ds(own * 8, 16)]
    after = eps_ref[pl.ds(jnp.minimum(own + 2, tiles_x - 1) * 8, 8)]
    before = eps_ref[pl.ds(jnp.maximum(own - 1, 0) * 8, 8)]
    near_ref[16:24] = jnp.where(rows[None] < 4, after, before)


def edges(slab, sub, planes, width):
    row = lax.broadcasted_iota(jnp.int32, (32, LANES), 0) + sub * 16 - 8
    inside_x = jnp.logical_and(row >= 0, row < width)

    def keep(z):
        height = slab * 8 - 4 + z
        return jnp.logical_and(inside_x, jnp.logical_and(height >= 0, height < planes))

    return keep


def unforced(old, z, lane):
    shear = None
    centres, laps = [], []
    for c in range(3):
        centre = old[c, z]
        upper = old[c, z + 1]
        lower = old[c, z - 1]
        east = pltpu.roll(centre, 31, 0)
        west = pltpu.roll(centre, 1, 0)
        north = jnp.where(lane == LANES - 1, 0.0, pltpu.roll(centre, LANES - 1, 1))
        south = jnp.where(lane == 0, 0.0, pltpu.roll(centre, 1, 1))
        term = (upper - centre) ** 2 + (east - centre) ** 2 + (north - centre) ** 2
        shear = term if shear is None else shear + term
        centres.append(centre)
        laps.append(upper + lower + east + west + north + south - 6.0 * centre)
    viscous = (TIME_STEP * VISCOSITY) * jnp.exp(FLOW_POWER * jnp.log(shear + 0.01))
    return [centres[c] + viscous * laps[c] for c in range(3)]


def first_kernel(place_ref, window_ref, even_ref, odd_ref, out_ref, tick_ref, old):
    tick_ref[...] = jnp.zeros_like(tick_ref)
    side = place_ref[0] % 2
    old[:, pl.ds(12 - 12 * side, 4)] = even_ref[...]
    old[:, pl.ds(12 * side, 4)] = odd_ref[...]
    old[:, 4:12] = window_ref[...]
    lane = lax.broadcasted_iota(jnp.int32, (32, LANES), 1)

    def plane(number, carry):
        for k in range(2):
            z = number * 2 + k
            moved = unforced(old, z + 1, lane)
            for c in range(3):
                out_ref[c, z] = moved[c]
        return carry

    lax.fori_loop(0, 7, plane, 0)


def forced(old, new, source, z, keep, lane):
    moved = unforced(old, z, lane)
    inside = keep(z)
    for c in range(3):
        total = moved[c] + TIME_STEP * source[c, z - 1]
        new[c, z] = jnp.where(inside, total, 0.0)


def near_kernel(place_ref, first_ref, own_ref, even_ref, *refs):
    keeps, last_ref, levels, source = refs[:3], refs[3], refs[4:8], refs[8]
    keep = edges(place_ref[0], place_ref[1], place_ref[2], place_ref[3])
    lane = lax.broadcasted_iota(jnp.int32, (32, LANES), 1)
    side = place_ref[0] % 2

    def plane(n):
        return n + side * (15 - 2 * n)

    for part, planes in ((own_ref, slice(3, 11)), (even_ref, pl.ds(11 - 11 * side, 3))):
        source[:, planes, 0:24, :] = part[...]
        source[:, planes, 24:32, :] = part[:, :, 0:8, :]
    for n in range(4, 15):
        z = plane(n)
        inside = keep(z)
        for c in range(3):
            moved = first_ref[c, z - 1] + TIME_STEP * source[c, z - 1]
            levels[0][c, z] = jnp.where(inside, moved, 0.0)
    for step in range(1, ITERS):

        def run(n, carry, step=step):
            forced(levels[step - 1], levels[step], source, plane(n), keep, lane)
            return carry

        lax.fori_loop(4 + step, 15 - step, run, 0)
    for step in range(3):
        for n in range(2):
            for c in range(3):
                keeps[step][c, n] = levels[step][c, plane(4 + step + n)]
    for n in range(5):
        for c in range(3):
            last_ref[c, n] = levels[3][c, plane(7 + n), 8:24, :]


def far_kernel(place_ref, first_ref, own_ref, odd_ref, *refs):
    keeps, last_ref, out_ref, levels, source = refs[:3], refs[3], refs[4], refs[5:9], refs[9]
    keep = edges(place_ref[0], place_ref[1], place_ref[2], place_ref[3])
    lane = lax.broadcasted_iota(jnp.int32, (32, LANES), 1)
    side = place_ref[0] % 2

    def plane(n):
        return n + side * (15 - 2 * n)

    for part, planes in ((own_ref, slice(3, 11)), (odd_ref, pl.ds(11 * side, 3))):
        source[:, planes, 0:24, :] = part[...]
        source[:, planes, 24:32, :] = part[:, :, 0:8, :]
    for step in range(3):
        for n in range(2):
            for c in range(3):
                levels[step][c, plane(4 + step + n)] = keeps[step][c, n]
    for n in range(1, 4):
        z = plane(n)
        inside = keep(z)
        for c in range(3):
            moved = first_ref[c, z - 1] + TIME_STEP * source[c, z - 1]
            levels[0][c, z] = jnp.where(inside, moved, 0.0)
    for step in range(1, ITERS):
        for n in range(1 + step, 4 + step):
            forced(levels[step - 1], levels[step], source, plane(n), keep, lane)
    for c in range(3):
        for n in range(3):
            z = plane(4 + n)
            rows = levels[3][c, z, 8:24, :]
            for j in range(out_ref.shape[0]):
                out_ref[j, c, z - 4] = rows
        for n in range(5):
            rows = last_ref[c, n]
            for j in range(out_ref.shape[0]):
                out_ref[j, c, plane(7 + n) - 4] = rows


def place_kernel(parts_ref, out_ref, sems):
    rows = parts_ref.shape[3]
    pairs = []
    for j in range(parts_ref.shape[0]):
        pairs.append((parts_ref.at[j], out_ref.at[:, :, j * rows : (j + 1) * rows, :]))
    for copy in fetch(pairs, sems):
        copy.wait()


def pinned(*arrays):
    return [pltpu.with_memory_space_constraint(x, pltpu.HBM) for x in arrays]


def call(kernel, out_shapes, ins, scratch=(), outs=None, us=1.0):
    outs = outs or [VMEM] * len(out_shapes)
    return pl.pallas_call(
        kernel,
        out_shape=[
            pltpu.HBM(s, F32) if spec is HBM else jax.ShapeDtypeStruct(s, F32)
            for s, spec in zip(out_shapes, outs)
        ],
        in_specs=ins,
        out_specs=outs,
        scratch_shapes=list(scratch),
        compiler_params=PARAMS,
        cost_estimate=pl.CostEstimate(flops=int(us * 1e9), bytes_accessed=int(us * 3.6e6), transcendentals=0),
    )


def pair_up(x, first):
    pairs = [(i, i + 1) for i in range(first, lax.axis_size("slab") - 1, 2)]
    return lax.ppermute(x, "slab", pairs + [(j, i) for i, j in pairs])


def body(velocity, part_vel, fraction, base_cell, drag_coeff, part_volume, brick_of_block):
    depth, width_x = velocity.shape[1], velocity.shape[2]
    blocks = brick_of_block.shape[0]
    subs = lax.axis_size("sub")
    slab = lax.axis_index("slab").astype(jnp.int32)
    sub = lax.axis_index("sub").astype(jnp.int32)
    tiles_x = width_x // 8
    tiles = tiles_x * 8
    share = tiles // subs
    base = base_cell.reshape(blocks, BLOCK)
    coef = drag_coeff.reshape(blocks, BLOCK)
    pvol = part_volume.reshape(blocks, BLOCK)

    particles_vmem = [
        pltpu.SMEM((blocks,), jnp.int32),
        pltpu.VMEM((blocks, BLOCK), jnp.int32),
        pltpu.VMEM((3, blocks * BLOCK), F32),
    ]
    row_vmem = pltpu.VMEM((blocks, BLOCK), F32)
    solid, solid_tick = call(
        solid_kernel,
        [(tiles, 8, LANES), (8, LANES)],
        [HBM] * 4,
        [pltpu.VMEM((tiles, 8, LANES), F32)]
        + particles_vmem
        + [row_vmem, pltpu.SemaphoreType.DMA((4,))],
        outs=[HBM, VMEM],
        us=5.0,
    )(*pinned(brick_of_block, base, fraction, pvol))
    solid_parts = lax.all_to_all(solid.reshape(subs, share, 8, LANES), "sub", 0, 0)
    half = blocks // 2

    def slip_of(first, after):
        (slip,) = call(
            functools.partial(slip_kernel, first, half),
            [(3, half * BLOCK)],
            [ANY] + [HBM] * 7,
            [
                pltpu.SMEM((blocks,), jnp.int32),
                pltpu.VMEM((half, BLOCK), jnp.int32),
                pltpu.VMEM((3, half * BLOCK), F32),
                pltpu.VMEM((3, half * BLOCK), F32),
                pltpu.VMEM((half, BLOCK), F32),
                pltpu.VMEM((half, BLOCK), F32),
                pltpu.VMEM(velocity.shape, F32),
                pltpu.VMEM((3 * tiles, 8, LANES), F32),
                pltpu.SemaphoreType.DMA((7,)),
            ],
            us=5.0,
            )(after, brick_of_block, base, fraction, part_vel, coef, pvol, velocity)
        return slip

    slip_a = slip_of(0, solid_tick)
    eps_copies, eps_tick = call(
        eps_kernel,
        [(subs, share, 8, LANES), (8, LANES)],
        [VMEM],
        [pltpu.VMEM((share, 8, LANES), F32), pltpu.SemaphoreType.DMA((subs,))],
        outs=[HBM, VMEM],
        us=0.5,
    )(solid_parts)
    slip_b = slip_of(half, eps_tick)
    eps = lax.all_to_all(eps_copies, "sub", 0, 0).reshape(tiles, 8, LANES)
    drag, force, tick = call(
        drag_kernel,
        [(3, blocks * BLOCK), (subs, 66, 8, LANES), (8, LANES)],
        [SMEM] + [VMEM] * 5,
        [
            pltpu.VMEM((subs, 66, 8, LANES), F32),
            pltpu.SemaphoreType.DMA((2 * subs,)),
        ],
        outs=[VMEM, HBM, VMEM],
        us=6.0,
    )(brick_of_block, base, fraction, slip_a, slip_b, eps)
    forces = lax.all_to_all(force, "sub", 0, 0)
    planes = depth * lax.axis_size("slab")
    place = jnp.stack([slab, sub, jnp.int32(planes), jnp.int32(width_x)])
    window, even, odd = call(
        window_kernel,
        [(3, depth, 32, LANES), (3, 4, 32, LANES), (3, 4, 32, LANES)],
        [SMEM, ANY, HBM],
        [pltpu.SemaphoreType.DMA((4,))],
    )(place, tick, *pinned(velocity))
    even, odd = pair_up(even, 0), pair_up(odd, 1)
    voidfraction, near = call(
        void_kernel, [(depth, width_x, LANES), (24, 8, LANES)], [SMEM, ANY, VMEM], us=2.0
    )(place, tick, eps)
    first, first_tick = call(
        first_kernel,
        [(3, 14, 32, LANES), (8, LANES)],
        [SMEM] + [VMEM] * 3,
        [pltpu.VMEM((3, 16, 32, LANES), F32)],
        us=1.0,
    )(place, window, even, odd)

    rows = width_x // subs
    own, even, odd = call(
        source_kernel,
        [(3, depth, 24, LANES), (3, 3, 24, LANES), (3, 3, 24, LANES)],
        [SMEM, VMEM, VMEM, ANY],
    )(place, forces, near, first_tick)
    even, odd = pair_up(even, 0), pair_up(odd, 1)
    buffers = [pltpu.VMEM((3, 16, 32, LANES), F32)] * 4 + [pltpu.VMEM((3, 14, 32, LANES), F32)]
    known = call(
        near_kernel,
        [(3, 2, 32, LANES)] * 3 + [(3, 5, rows, LANES)],
        [SMEM] + [VMEM] * 3,
        buffers,
        us=2.0,
    )(place, first, own, even)
    (moved,) = call(
        far_kernel, [(subs, 3, depth, rows, LANES)], [SMEM] + [VMEM] * 7, buffers, us=1.0
    )(place, first, own, odd, *known)
    moved = lax.all_to_all(moved, "sub", 0, 0)
    (new_velocity,) = call(
        place_kernel,
        [velocity.shape],
        [ANY],
        [pltpu.SemaphoreType.DMA((subs,))],
        outs=[HBM],
    )(moved)
    return new_velocity, voidfraction, drag


def solution(mesh):
    in_specs = (
        P(None, "slab", None, None),
        P(None, ("slab", "sub")),
        P(None, ("slab", "sub")),
        P(("slab", "sub")),
        P(("slab", "sub")),
        P(("slab", "sub")),
        P(("slab", "sub")),
    )
    out_specs = (P(None, "slab", None, None), P("slab", None, None), P(None, ("slab", "sub")))
    return jax.shard_map(body, mesh=mesh, in_specs=in_specs, out_specs=out_specs, check_vma=False)
```

```python
import functools

import jax
import jax.numpy as jnp
from jax import lax
from jax.experimental import pallas as pl
from jax.experimental.pallas import tpu as pltpu
from jax.sharding import PartitionSpec as P

BLOCK = 128
LANES = 128
EPS_MIN = 0.35
FLOW_POWER = -0.2
DRAG_POWER = -2.65
VISCOSITY = 1.2
TIME_STEP = 0.05
ITERS = 4
UNROLL = 16
F32 = jnp.float32
PARAMS = pltpu.CompilerParams(vmem_limit_bytes=16 * 1024 * 1024)
VMEM = pl.BlockSpec(memory_space=pltpu.VMEM)
SMEM = pl.BlockSpec(memory_space=pltpu.SMEM)
HBM = pl.BlockSpec(memory_space=pltpu.HBM)
ANY = pl.BlockSpec(memory_space=pl.ANY)


def transpose_granules(tiles, lane):
    for bit in (1, 2, 4):
        shift = 8 * bit
        high = (lane & shift) != 0
        new = list(tiles)
        for a in range(8):
            if a & bit:
                continue
            b = a | bit
            va, vb = tiles[a], tiles[b]
            new[a] = jnp.where(high, pltpu.roll(vb, shift, 1), va)
            new[b] = jnp.where(high, vb, pltpu.roll(va, LANES - shift, 1))
        tiles = new
    return tiles


def fetch(pairs, sems):
    copies = [pltpu.make_async_copy(a, b, sems.at[i]) for i, (a, b) in enumerate(pairs)]
    for copy in copies:
        copy.start()
    return copies


def lanes_iota():
    return lax.broadcasted_iota(jnp.int32, (8, LANES), 1)


def rows_iota():
    return lax.broadcasted_iota(jnp.int32, (8, LANES), 0)


def spread(row):
    return jnp.broadcast_to(row, (8, LANES))


def particles(base_ref, frac_ref, block):
    at = pl.ds(pl.multiple_of(block * BLOCK, BLOCK), BLOCK)
    base = spread(base_ref[pl.ds(block, 1), :])
    fz = spread(frac_ref[0:1, at])
    fx = spread(frac_ref[1:2, at])
    fy = spread(frac_ref[2:3, at])
    return at, base >> 6, (base >> 3) & 7, base & 7, fz, fx, fy


def axis_weights(rows, first, frac):
    zero = jnp.zeros_like(frac)
    return jnp.where(rows == first, 1.0 - frac, jnp.where(rows == first + 1, frac, zero))


def halves(value):
    high = value.astype(jnp.bfloat16).astype(F32)
    return high, value - high


def plane_weights(rows, zb, yb, fz, fy):
    ky = axis_weights(rows, yb, fy)
    number = zb.astype(F32)
    offset = jnp.concatenate([number, number - 1.0], axis=0).astype(jnp.bfloat16)
    zero = jnp.zeros((16, LANES), jnp.bfloat16)

    def twice(value):
        return jnp.concatenate([value, value], axis=0).astype(jnp.bfloat16)

    parts = []
    for here, above in zip(halves((1.0 - fz) * ky), halves(fz * ky)):
        here, above = twice(here), twice(above)
        for q in range(4):
            upper = jnp.where(offset == 2 * q - 1, above, zero)
            parts.append(jnp.where(offset == 2 * q, here, upper))
    return jnp.concatenate(parts, axis=0)


def split_rows(parts):
    full = jnp.concatenate(parts, axis=0)
    high = full.astype(jnp.bfloat16).astype(F32)
    return jnp.concatenate([high, full - high], axis=0).astype(jnp.bfloat16)


def deposit(blocks):
    left = []
    for n, (parts, _) in enumerate(blocks):
        rows = split_rows(parts)
        pair = [rows, jnp.zeros_like(rows)]
        left.append(jnp.concatenate(pair if n == 0 else pair[::-1], axis=1))
    both = lax.dot_general(
        jnp.concatenate(left, axis=0),
        jnp.concatenate([weights for _, weights in blocks], axis=1),
        (((1,), (1,)), ((), ())),
        preferred_element_type=F32,
    )
    half = both.shape[0] // 4
    found = []
    for n in range(2):
        total = both[2 * n * half : (2 * n + 1) * half] + both[(2 * n + 1) * half : (2 * n + 2) * half]
        found.append(total + pltpu.roll(total, 64, 1))
    return found


def corner_terms(zb, yb, fz, fy, offset):
    index = (zb << 3) + yb + offset
    gz, gy = 1.0 - fz, 1.0 - fy
    return (
        (index, gz * gy),
        (index + 1, gz * fy),
        (index + 8, fz * gy),
        (index + 9, fz * fy),
    )


def interpolate(tile, kx, corners):
    total = None
    for index, weight in corners:
        term = weight * jnp.take_along_axis(tile, index, axis=1, mode="promise_in_bounds")
        total = term if total is None else total + term
    return jnp.sum(kx * total, axis=0, keepdims=True)


def brick_place(brick):
    return brick >> 4, brick & 7, (brick >> 3) & 1


def solid_kernel(
    brick_hbm, base_hbm, frac_hbm, pvol_hbm, out_hbm, tick_ref,
    out_ref, brick_ref, base_ref, frac_ref, pvol_ref, sems,
):
    copies = fetch(
        [(brick_hbm, brick_ref), (base_hbm, base_ref), (frac_hbm, frac_ref), (pvol_hbm, pvol_ref)],
        sems,
    )
    out_ref[...] = jnp.zeros_like(out_ref)
    for copy in copies:
        copy.wait()
    rows, lane = rows_iota(), lanes_iota()

    def step(number, carry):
        found = []
        for k in range(UNROLL):
            block = number * UNROLL + k
            _, zb, xb, yb, fz, fx, fy = particles(base_ref, frac_ref, block)
            kx = axis_weights(rows, xb, fx) * spread(pvol_ref[pl.ds(block, 1), :])
            found.append(([kx], plane_weights(rows, zb, yb, fz, fy)))
        found = sum((deposit(found[k : k + 2]) for k in range(0, UNROLL, 2)), [])
        for k in range(UNROLL):
            tx, t3, t1 = brick_place(brick_ref[number * UNROLL + k])
            tile = tx * 8 + t3
            out_ref[tile] += jnp.where((lane >> 6) == t1, found[k], 0.0)
        return carry

    lax.fori_loop(0, base_ref.shape[0] // UNROLL, step, 0)
    (copy,) = fetch([(out_ref, out_hbm)], sems)
    tick_ref[...] = jnp.zeros_like(tick_ref)
    copy.wait()


def eps_kernel(parts_ref, copies_hbm, tick_ref, out_ref, sems):
    tick_ref[...] = jnp.zeros_like(tick_ref)
    total = parts_ref[0]
    for j in range(1, parts_ref.shape[0]):
        total = total + parts_ref[j]
    total = jnp.maximum(1.0 - total, EPS_MIN)
    out_ref[...] = total
    for copy in fetch([(out_ref, copies_hbm.at[j]) for j in range(copies_hbm.shape[0])], sems):
        copy.wait()


def slip_kernel(
    first, count,
    after_any, brick_hbm, base_hbm, frac_hbm, pvel_hbm, coef_hbm, pvol_hbm, velocity_hbm,
    out_ref,
    brick_ref, base_ref, frac_ref, pvel_ref, coef_ref, pvol_ref, velocity_ref, table_ref, sems,
):
    some = pl.ds(first, count)
    wide = pl.ds(first * BLOCK, count * BLOCK)
    copies = fetch(
        [
            (velocity_hbm, velocity_ref),
            (brick_hbm, brick_ref),
            (base_hbm.at[some], base_ref),
            (frac_hbm.at[:, wide], frac_ref),
            (pvel_hbm.at[:, wide], pvel_ref),
            (coef_hbm.at[some], coef_ref),
            (pvol_hbm.at[some], pvol_ref),
        ],
        sems,
    )
    rows, lane = rows_iota(), lanes_iota()
    tiles_x = velocity_ref.shape[2] // 8

    def convert(number, carry):
        for k in range(2):
            tx = number * 2 + k
            at = pl.ds(pl.multiple_of(tx * 8, 8), 8)
            for c in range(3):
                tiles = transpose_granules([velocity_ref[c, z, at, :] for z in range(8)], lane)
                for t3 in range(8):
                    table_ref[(tx * 3 + c) * 8 + t3] = tiles[t3]
        return carry

    copies[0].wait()
    lax.fori_loop(0, tiles_x // 2, convert, 0)
    for copy in copies[1:]:
        copy.wait()

    def step(number, carry):
        for k in range(UNROLL):
            block = number * UNROLL + k
            at, zb, xb, yb, fz, fx, fy = particles(base_ref, frac_ref, block)
            tx, t3, t1 = brick_place(brick_ref[first + block])
            kx = axis_weights(rows, xb, fx)
            corners = corner_terms(zb, yb, fz, fy, t1 * 64)
            rel = [
                interpolate(table_ref[(tx * 3 + c) * 8 + t3], kx, corners) - pvel_ref[c : c + 1, at]
                for c in range(3)
            ]
            speed = rel[0] * rel[0] + rel[1] * rel[1] + rel[2] * rel[2]
            factor = coef_ref[pl.ds(block, 1), :] * pvol_ref[pl.ds(block, 1), :]
            factor = factor * jnp.exp(FLOW_POWER * jnp.log(speed + 0.01))
            for c in range(3):
                out_ref[c : c + 1, at] = factor * rel[c]
        return carry

    lax.fori_loop(0, count // UNROLL, step, 0)


def pack_halo(rows, tiles):
    a, b, c, d = tiles
    middle = jnp.logical_or(rows == 3, rows == 4)
    first = jnp.where(middle, pltpu.roll(d, 3, 0), a)
    second = jnp.where(rows == 3, pltpu.roll(d, 1, 0), jnp.where(rows == 4, pltpu.roll(d, 7, 0), b))
    third = jnp.where(middle, pltpu.roll(d, 5, 0), c)
    return first, second, third


def unpack_halo(rows, tiles):
    a, b, c = tiles
    inner = jnp.where(rows == 2, pltpu.roll(b, 7, 0), pltpu.roll(b, 1, 0))
    d = jnp.where(rows < 2, pltpu.roll(a, 5, 0), jnp.where(rows > 5, pltpu.roll(c, 3, 0), inner))
    return a, b, c, d


def drag_kernel(
    brick_hbm, base_ref, frac_ref, slip_a_ref, slip_b_ref, eps_ref,
    drag_ref, out_hbm, tick_ref,
    force_ref, brick_ref, sems,
):
    subs = force_ref.shape[0]
    rows, lane = rows_iota(), lanes_iota()
    (copy,) = fetch([(brick_hbm, brick_ref)], sems)
    for j in range(subs):
        force_ref[j, 0:48] = jnp.zeros((48, 8, LANES), F32)
    copy.wait()

    for slip_ref, start in ((slip_a_ref, 0), (slip_b_ref, slip_a_ref.shape[1] // BLOCK)):

        def step(number, carry, slip_ref=slip_ref, start=start):
            found = []
            for k in range(UNROLL):
                inner = number * UNROLL + k
                block = inner + start
                at, zb, xb, yb, fz, fx, fy = particles(base_ref, frac_ref, block)
                inner_at = pl.ds(pl.multiple_of(inner * BLOCK, BLOCK), BLOCK)
                tx, t3, t1 = brick_place(brick_ref[block])
                kx = axis_weights(rows, xb, fx)
                eps = interpolate(eps_ref[tx * 8 + t3], kx, corner_terms(zb, yb, fz, fy, t1 * 64))
                factor = jnp.exp(DRAG_POWER * jnp.log(eps))
                parts = []
                for c in range(3):
                    force = factor * slip_ref[c : c + 1, inner_at]
                    drag_ref[c : c + 1, at] = force
                    parts.append(kx * spread(force))
                found.append((parts, plane_weights(rows, zb, yb, fz, fy)))
            found = sum((deposit(found[k : k + 2]) for k in range(0, UNROLL, 2)), [])
            for k in range(UNROLL):
                tx, t3, t1 = brick_place(brick_ref[number * UNROLL + k + start])
                mine = (lane >> 6) == t1
                for c in range(3):
                    tile = (tx & 1) * 24 + c * 8 + t3
                    force_ref[tx >> 1, tile] += jnp.where(mine, found[k][8 * c : 8 * c + 8], 0.0)
            return carry

        lax.fori_loop(0, slip_ref.shape[1] // BLOCK // UNROLL, step, 0)
    copies = fetch([(force_ref.at[j, 0:48], out_hbm.at[j, 0:48]) for j in range(subs)], sems)
    zero = jnp.zeros((8, LANES), F32)
    tick_ref[...] = zero
    for j in range(subs):
        for quad in range(6):
            tiles = []
            for at in range(quad * 4, quad * 4 + 4):
                after = force_ref[j + 1, at] if j + 1 < subs else zero
                before = force_ref[j - 1, 24 + at] if j > 0 else zero
                tiles.append(jnp.where(rows < 4, after, before))
            for n, tile in enumerate(pack_halo(rows, tiles)):
                force_ref[j, 48 + quad * 3 + n] = tile
        copy = pltpu.make_async_copy(
            force_ref.at[j, 48:66], out_hbm.at[j, 48:66], sems.at[subs + j]
        )
        copy.start()
        copies.append(copy)
    for copy in copies:
        copy.wait()


def source_kernel(parts_ref, eps_ref, first_any, own_ref, even_ref, odd_ref):
    lane, rows = lanes_iota(), rows_iota()
    even = lax.axis_index("slab") % 2 == 0

    def summed(at):
        total = parts_ref[0, at]
        for j in range(1, parts_ref.shape[0]):
            total = total + parts_ref[j, at]
        return total

    for t in range(3):
        for c in range(3):
            if t < 2:
                forces = [summed(t * 24 + c * 8 + t3) for t3 in range(8)]
            else:
                forces = []
                for quad in (2 * c, 2 * c + 1):
                    forces += unpack_halo(rows, [summed(48 + quad * 3 + k) for k in range(3)])
            tiles = []
            for t3 in range(8):
                tiles.append(-forces[t3] / eps_ref[t * 8 + t3])
            tiles = transpose_granules(tiles, lane)
            first = 8 * (t + 1) % 24
            for z in range(8):
                own_ref[c, z, first : first + 8, :] = tiles[z]
            for n in range(3):
                at = slice(first, first + 8)
                even_ref[c, n, at, :] = jnp.where(even, tiles[5 + n], tiles[n])
                odd_ref[c, n, at, :] = jnp.where(even, tiles[n], tiles[5 + n])


def window_kernel(after_any, velocity_hbm, out_ref, even_ref, odd_ref, sems):
    even = lax.axis_index("slab") % 2 == 0
    depth = velocity_hbm.shape[1]
    tiles_x = velocity_hbm.shape[2] // 8
    pairs, inside = [], []
    for r in range(4):
        want = lax.axis_index("sub") * 2 + r - 1
        inside.append(jnp.logical_and(want >= 0, want < tiles_x))
        at = pl.ds(pl.multiple_of(jnp.clip(want, 0, tiles_x - 1) * 8, 8), 8)
        pairs.append((velocity_hbm.at[:, :, at, :], out_ref.at[:, :, 8 * r : 8 * r + 8, :]))
    for copy in fetch(pairs, sems):
        copy.wait()
    for r in range(4):
        at = slice(8 * r, 8 * r + 8)
        rows = jnp.where(inside[r], out_ref[:, :, at, :], 0.0)
        out_ref[:, :, at, :] = rows
        even_ref[:, :, at, :] = jnp.where(even, rows[:, depth - 4 :], rows[:, :4])
        odd_ref[:, :, at, :] = jnp.where(even, rows[:, :4], rows[:, depth - 4 :])


def void_kernel(after_any, eps_ref, out_ref, near_ref):
    lane, rows = lanes_iota(), rows_iota()
    tiles_x = out_ref.shape[1] // 8

    def convert(number, carry):
        for k in range(4):
            tx = number * 4 + k
            tiles = transpose_granules([eps_ref[tx * 8 + t3] for t3 in range(8)], lane)
            for z in range(8):
                out_ref[z, pl.ds(pl.multiple_of(tx * 8, 8), 8), :] = tiles[z]
        return carry

    lax.fori_loop(0, tiles_x // 4, convert, 0)
    own = lax.axis_index("sub") * 2
    near_ref[0:16] = eps_ref[pl.ds(own * 8, 16)]
    after = eps_ref[pl.ds(jnp.minimum(own + 2, tiles_x - 1) * 8, 8)]
    before = eps_ref[pl.ds(jnp.maximum(own - 1, 0) * 8, 8)]
    near_ref[16:24] = jnp.where(rows[None] < 4, after, before)


def edges():
    slab, sub = lax.axis_index("slab"), lax.axis_index("sub")
    planes, width = lax.axis_size("slab") * 8, lax.axis_size("sub") * 16
    row = lax.broadcasted_iota(jnp.int32, (32, LANES), 0) + sub * 16 - 8
    inside_x = jnp.logical_and(row >= 0, row < width)

    def keep(z):
        height = slab * 8 - 4 + z
        return jnp.logical_and(inside_x, jnp.logical_and(height >= 0, height < planes))

    return keep


def unforced(old, z, lane):
    shear = None
    centres, laps = [], []
    for c in range(3):
        centre = old[c, z]
        upper = old[c, z + 1]
        lower = old[c, z - 1]
        east = pltpu.roll(centre, 31, 0)
        west = pltpu.roll(centre, 1, 0)
        north = jnp.where(lane == LANES - 1, 0.0, pltpu.roll(centre, LANES - 1, 1))
        south = jnp.where(lane == 0, 0.0, pltpu.roll(centre, 1, 1))
        term = (upper - centre) ** 2 + (east - centre) ** 2 + (north - centre) ** 2
        shear = term if shear is None else shear + term
        centres.append(centre)
        laps.append(upper + lower + east + west + north + south - 6.0 * centre)
    viscous = (TIME_STEP * VISCOSITY) * jnp.exp(FLOW_POWER * jnp.log(shear + 0.01))
    return [centres[c] + viscous * laps[c] for c in range(3)]


def first_kernel(window_ref, even_ref, odd_ref, out_ref, tick_ref, old):
    tick_ref[...] = jnp.zeros_like(tick_ref)
    side = lax.axis_index("slab") % 2
    old[:, pl.ds(12 - 12 * side, 4)] = even_ref[...]
    old[:, pl.ds(12 * side, 4)] = odd_ref[...]
    old[:, 4:12] = window_ref[...]
    lane = lax.broadcasted_iota(jnp.int32, (32, LANES), 1)

    def plane(number, carry):
        for k in range(2):
            z = number * 2 + k
            moved = unforced(old, z + 1, lane)
            for c in range(3):
                out_ref[c, z] = moved[c]
        return carry

    lax.fori_loop(0, 7, plane, 0)


def forced(old, new, source, z, keep, lane):
    moved = unforced(old, z, lane)
    inside = keep(z)
    for c in range(3):
        total = moved[c] + TIME_STEP * source[c, z - 1]
        new[c, z] = jnp.where(inside, total, 0.0)


def near_kernel(first_ref, own_ref, even_ref, *refs):
    keeps, last_ref, levels, source = refs[:3], refs[3], refs[4:8], refs[8]
    keep = edges()
    lane = lax.broadcasted_iota(jnp.int32, (32, LANES), 1)
    side = lax.axis_index("slab") % 2

    def plane(n):
        return n + side * (15 - 2 * n)

    for part, planes in ((own_ref, slice(3, 11)), (even_ref, pl.ds(11 - 11 * side, 3))):
        source[:, planes, 0:24, :] = part[...]
        source[:, planes, 24:32, :] = part[:, :, 0:8, :]
    for n in range(4, 15):
        z = plane(n)
        inside = keep(z)
        for c in range(3):
            moved = first_ref[c, z - 1] + TIME_STEP * source[c, z - 1]
            levels[0][c, z] = jnp.where(inside, moved, 0.0)
    for step in range(1, ITERS):

        def run(n, carry, step=step):
            forced(levels[step - 1], levels[step], source, plane(n), keep, lane)
            return carry

        lax.fori_loop(4 + step, 15 - step, run, 0)
    for step in range(3):
        for n in range(2):
            for c in range(3):
                keeps[step][c, n] = levels[step][c, plane(4 + step + n)]
    for n in range(5):
        for c in range(3):
            last_ref[c, n] = levels[3][c, plane(7 + n), 8:24, :]


def far_kernel(first_ref, own_ref, odd_ref, *refs):
    keeps, last_ref, out_ref, levels, source = refs[:3], refs[3], refs[4], refs[5:9], refs[9]
    keep = edges()
    lane = lax.broadcasted_iota(jnp.int32, (32, LANES), 1)
    side = lax.axis_index("slab") % 2

    def plane(n):
        return n + side * (15 - 2 * n)

    for part, planes in ((own_ref, slice(3, 11)), (odd_ref, pl.ds(11 * side, 3))):
        source[:, planes, 0:24, :] = part[...]
        source[:, planes, 24:32, :] = part[:, :, 0:8, :]
    for step in range(3):
        for n in range(2):
            for c in range(3):
                levels[step][c, plane(4 + step + n)] = keeps[step][c, n]
    for n in range(1, 4):
        z = plane(n)
        inside = keep(z)
        for c in range(3):
            moved = first_ref[c, z - 1] + TIME_STEP * source[c, z - 1]
            levels[0][c, z] = jnp.where(inside, moved, 0.0)
    for step in range(1, ITERS):
        for n in range(1 + step, 4 + step):
            forced(levels[step - 1], levels[step], source, plane(n), keep, lane)
    for c in range(3):
        for n in range(3):
            z = plane(4 + n)
            rows = levels[3][c, z, 8:24, :]
            for j in range(out_ref.shape[0]):
                out_ref[j, c, z - 4] = rows
        for n in range(5):
            rows = last_ref[c, n]
            for j in range(out_ref.shape[0]):
                out_ref[j, c, plane(7 + n) - 4] = rows


def place_kernel(parts_ref, out_ref, sems):
    rows = parts_ref.shape[3]
    pairs = []
    for j in range(parts_ref.shape[0]):
        pairs.append((parts_ref.at[j], out_ref.at[:, :, j * rows : (j + 1) * rows, :]))
    for copy in fetch(pairs, sems):
        copy.wait()


def pinned(*arrays):
    return [pltpu.with_memory_space_constraint(x, pltpu.HBM) for x in arrays]


def call(kernel, out_shapes, ins, scratch=(), outs=None, us=1.0):
    outs = outs or [VMEM] * len(out_shapes)
    return pl.pallas_call(
        kernel,
        out_shape=[
            pltpu.HBM(s, F32) if spec is HBM else jax.ShapeDtypeStruct(s, F32)
            for s, spec in zip(out_shapes, outs)
        ],
        in_specs=ins,
        out_specs=outs,
        scratch_shapes=list(scratch),
        compiler_params=PARAMS,
        cost_estimate=pl.CostEstimate(flops=int(us * 1e9), bytes_accessed=int(us * 3.6e6), transcendentals=0),
    )


def pair_up(x, first):
    pairs = [(i, i + 1) for i in range(first, lax.axis_size("slab") - 1, 2)]
    return lax.ppermute(x, "slab", pairs + [(j, i) for i, j in pairs])


def body(velocity, part_vel, fraction, base_cell, drag_coeff, part_volume, brick_of_block):
    depth, width_x = velocity.shape[1], velocity.shape[2]
    blocks = brick_of_block.shape[0]
    subs = lax.axis_size("sub")
    tiles_x = width_x // 8
    tiles = tiles_x * 8
    share = tiles // subs
    base = base_cell.reshape(blocks, BLOCK)
    coef = drag_coeff.reshape(blocks, BLOCK)
    pvol = part_volume.reshape(blocks, BLOCK)

    particles_vmem = [
        pltpu.SMEM((blocks,), jnp.int32),
        pltpu.VMEM((blocks, BLOCK), jnp.int32),
        pltpu.VMEM((3, blocks * BLOCK), F32),
    ]
    row_vmem = pltpu.VMEM((blocks, BLOCK), F32)
    solid, solid_tick = call(
        solid_kernel,
        [(tiles, 8, LANES), (8, LANES)],
        [HBM] * 4,
        [pltpu.VMEM((tiles, 8, LANES), F32)]
        + particles_vmem
        + [row_vmem, pltpu.SemaphoreType.DMA((4,))],
        outs=[HBM, VMEM],
        us=5.0,
    )(*pinned(brick_of_block, base, fraction, pvol))
    solid_parts = lax.all_to_all(solid.reshape(subs, share, 8, LANES), "sub", 0, 0)
    half = blocks // 2

    def slip_of(first, after):
        (slip,) = call(
            functools.partial(slip_kernel, first, half),
            [(3, half * BLOCK)],
            [ANY] + [HBM] * 7,
            [
                pltpu.SMEM((blocks,), jnp.int32),
                pltpu.VMEM((half, BLOCK), jnp.int32),
                pltpu.VMEM((3, half * BLOCK), F32),
                pltpu.VMEM((3, half * BLOCK), F32),
                pltpu.VMEM((half, BLOCK), F32),
                pltpu.VMEM((half, BLOCK), F32),
                pltpu.VMEM(velocity.shape, F32),
                pltpu.VMEM((3 * tiles, 8, LANES), F32),
                pltpu.SemaphoreType.DMA((7,)),
            ],
            us=5.0,
            )(after, brick_of_block, base, fraction, part_vel, coef, pvol, velocity)
        return slip

    slip_a = slip_of(0, solid_tick)
    eps_copies, eps_tick = call(
        eps_kernel,
        [(subs, share, 8, LANES), (8, LANES)],
        [VMEM],
        [pltpu.VMEM((share, 8, LANES), F32), pltpu.SemaphoreType.DMA((subs,))],
        outs=[HBM, VMEM],
        us=0.5,
    )(solid_parts)
    slip_b = slip_of(half, eps_tick)
    eps = lax.all_to_all(eps_copies, "sub", 0, 0).reshape(tiles, 8, LANES)
    drag, force, tick = call(
        drag_kernel,
        [(3, blocks * BLOCK), (subs, 66, 8, LANES), (8, LANES)],
        [HBM] + [VMEM] * 5,
        [
            pltpu.VMEM((subs, 66, 8, LANES), F32),
            pltpu.SMEM((blocks,), jnp.int32),
            pltpu.SemaphoreType.DMA((2 * subs,)),
        ],
        outs=[VMEM, HBM, VMEM],
        us=6.0,
    )(*pinned(brick_of_block), base, fraction, slip_a, slip_b, eps)
    forces = lax.all_to_all(force, "sub", 0, 0)
    window, even, odd = call(
        window_kernel,
        [(3, depth, 32, LANES), (3, 4, 32, LANES), (3, 4, 32, LANES)],
        [ANY, HBM],
        [pltpu.SemaphoreType.DMA((4,))],
    )(tick, *pinned(velocity))
    even, odd = pair_up(even, 0), pair_up(odd, 1)
    voidfraction, near = call(
        void_kernel, [(depth, width_x, LANES), (24, 8, LANES)], [ANY, VMEM], us=2.0
    )(tick, eps)
    first, first_tick = call(
        first_kernel,
        [(3, 14, 32, LANES), (8, LANES)],
        [VMEM] * 3,
        [pltpu.VMEM((3, 16, 32, LANES), F32)],
        us=1.0,
    )(window, even, odd)

    rows = width_x // subs
    own, even, odd = call(
        source_kernel,
        [(3, depth, 24, LANES), (3, 3, 24, LANES), (3, 3, 24, LANES)],
        [VMEM, VMEM, ANY],
    )(forces, near, first_tick)
    even, odd = pair_up(even, 0), pair_up(odd, 1)
    buffers = [pltpu.VMEM((3, 16, 32, LANES), F32)] * 4 + [pltpu.VMEM((3, 14, 32, LANES), F32)]
    known = call(
        near_kernel,
        [(3, 2, 32, LANES)] * 3 + [(3, 5, rows, LANES)],
        [VMEM] * 3,
        buffers,
        us=2.0,
    )(first, own, even)
    (moved,) = call(
        far_kernel, [(subs, 3, depth, rows, LANES)], [VMEM] * 7, buffers, us=1.0
    )(first, own, odd, *known)
    moved = lax.all_to_all(moved, "sub", 0, 0)
    (new_velocity,) = call(
        place_kernel,
        [velocity.shape],
        [ANY],
        [pltpu.SemaphoreType.DMA((subs,))],
        outs=[HBM],
    )(moved)
    return new_velocity, voidfraction, drag


def solution(mesh):
    in_specs = (
        P(None, "slab", None, None),
        P(None, ("slab", "sub")),
        P(None, ("slab", "sub")),
        P(("slab", "sub")),
        P(("slab", "sub")),
        P(("slab", "sub")),
        P(("slab", "sub")),
    )
    out_specs = (P(None, "slab", None, None), P("slab", None, None), P(None, ("slab", "sub")))
    return jax.shard_map(body, mesh=mesh, in_specs=in_specs, out_specs=out_specs, check_vma=False)
```

```python
import functools

import jax
import jax.numpy as jnp
from jax import lax
from jax.experimental import pallas as pl
from jax.experimental.pallas import tpu as pltpu
from jax.sharding import PartitionSpec as P

BLOCK = 128
LANES = 128
EPS_MIN = 0.35
FLOW_POWER = -0.2
DRAG_POWER = -2.65
VISCOSITY = 1.2
TIME_STEP = 0.05
ITERS = 4
UNROLL = 16
LONG = 32
F32 = jnp.float32
PARAMS = pltpu.CompilerParams(vmem_limit_bytes=16 * 1024 * 1024)
VMEM = pl.BlockSpec(memory_space=pltpu.VMEM)
SMEM = pl.BlockSpec(memory_space=pltpu.SMEM)
HBM = pl.BlockSpec(memory_space=pltpu.HBM)
ANY = pl.BlockSpec(memory_space=pl.ANY)


def transpose_granules(tiles, lane):
    for bit in (1, 2, 4):
        shift = 8 * bit
        high = (lane & shift) != 0
        new = list(tiles)
        for a in range(8):
            if a & bit:
                continue
            b = a | bit
            va, vb = tiles[a], tiles[b]
            new[a] = jnp.where(high, pltpu.roll(vb, shift, 1), va)
            new[b] = jnp.where(high, vb, pltpu.roll(va, LANES - shift, 1))
        tiles = new
    return tiles


def fetch(pairs, sems):
    copies = [pltpu.make_async_copy(a, b, sems.at[i]) for i, (a, b) in enumerate(pairs)]
    for copy in copies:
        copy.start()
    return copies


def lanes_iota():
    return lax.broadcasted_iota(jnp.int32, (8, LANES), 1)


def rows_iota():
    return lax.broadcasted_iota(jnp.int32, (8, LANES), 0)


def spread(row):
    return jnp.broadcast_to(row, (8, LANES))


def particles(base_ref, frac_ref, block):
    at = pl.ds(pl.multiple_of(block * BLOCK, BLOCK), BLOCK)
    base = spread(base_ref[pl.ds(block, 1), :])
    fz = spread(frac_ref[0:1, at])
    fx = spread(frac_ref[1:2, at])
    fy = spread(frac_ref[2:3, at])
    return at, base >> 6, (base >> 3) & 7, base & 7, fz, fx, fy


def axis_weights(rows, first, frac):
    zero = jnp.zeros_like(frac)
    return jnp.where(rows == first, 1.0 - frac, jnp.where(rows == first + 1, frac, zero))


def halves(value):
    high = value.astype(jnp.bfloat16).astype(F32)
    return high, value - high


def plane_weights(rows, zb, yb, fz, fy):
    ky = axis_weights(rows, yb, fy)
    number = zb.astype(F32)
    offset = jnp.concatenate([number, number - 1.0], axis=0).astype(jnp.bfloat16)
    zero = jnp.zeros((16, LANES), jnp.bfloat16)

    def twice(value):
        return jnp.concatenate([value, value], axis=0).astype(jnp.bfloat16)

    parts = []
    for here, above in zip(halves((1.0 - fz) * ky), halves(fz * ky)):
        here, above = twice(here), twice(above)
        for q in range(4):
            upper = jnp.where(offset == 2 * q - 1, above, zero)
            parts.append(jnp.where(offset == 2 * q, here, upper))
    return jnp.concatenate(parts, axis=0)


def split_rows(parts):
    full = jnp.concatenate(parts, axis=0)
    high = full.astype(jnp.bfloat16).astype(F32)
    return jnp.concatenate([high, full - high], axis=0).astype(jnp.bfloat16)


def deposit(blocks):
    left = []
    for n, (parts, _) in enumerate(blocks):
        rows = split_rows(parts)
        pair = [rows, jnp.zeros_like(rows)]
        left.append(jnp.concatenate(pair if n == 0 else pair[::-1], axis=1))
    both = lax.dot_general(
        jnp.concatenate(left, axis=0),
        jnp.concatenate([weights for _, weights in blocks], axis=1),
        (((1,), (1,)), ((), ())),
        preferred_element_type=F32,
    )
    half = both.shape[0] // 4
    found = []
    for n in range(2):
        total = both[2 * n * half : (2 * n + 1) * half] + both[(2 * n + 1) * half : (2 * n + 2) * half]
        found.append(total + pltpu.roll(total, 64, 1))
    return found


def corner_terms(zb, yb, fz, fy, offset):
    index = (zb << 3) + yb + offset
    gz, gy = 1.0 - fz, 1.0 - fy
    return (
        (index, gz * gy),
        (index + 1, gz * fy),
        (index + 8, fz * gy),
        (index + 9, fz * fy),
    )


def interpolate(tile, kx, corners):
    total = None
    for index, weight in corners:
        term = weight * jnp.take_along_axis(tile, index, axis=1, mode="promise_in_bounds")
        total = term if total is None else total + term
    return jnp.sum(kx * total, axis=0, keepdims=True)


def brick_place(brick):
    return brick >> 4, brick & 7, (brick >> 3) & 1


def solid_kernel(
    brick_hbm, base_hbm, frac_hbm, pvol_hbm, out_hbm, tick_ref,
    out_ref, late_ref, brick_ref, base_ref, frac_ref, pvol_ref, sems,
):
    copies = fetch(
        [(brick_hbm, brick_ref), (base_hbm, base_ref), (frac_hbm, frac_ref), (pvol_hbm, pvol_ref)],
        sems,
    )
    out_ref[...] = jnp.zeros_like(out_ref)
    for copy in copies:
        copy.wait()
    rows, lane = rows_iota(), lanes_iota()
    late_ref[...] = jnp.zeros_like(late_ref)

    def add(number):
        for k in range(LONG):
            tx, t3, t1 = brick_place(brick_ref[number * LONG + k])
            out_ref[tx * 8 + t3] += jnp.where((lane >> 6) == t1, late_ref[k], 0.0)

    def step(number, carry):
        add(jnp.maximum(number - 1, 0))
        found = []
        for k in range(LONG):
            block = number * LONG + k
            _, zb, xb, yb, fz, fx, fy = particles(base_ref, frac_ref, block)
            kx = axis_weights(rows, xb, fx) * spread(pvol_ref[pl.ds(block, 1), :])
            found.append(([kx], plane_weights(rows, zb, yb, fz, fy)))
            if k % 2:
                late_ref[k - 1], late_ref[k] = deposit(found[-2:])
        return carry

    steps = base_ref.shape[0] // LONG
    lax.fori_loop(0, steps, step, 0)
    add(steps - 1)
    (copy,) = fetch([(out_ref, out_hbm)], sems)
    tick_ref[...] = jnp.zeros_like(tick_ref)
    copy.wait()


def eps_kernel(parts_ref, copies_hbm, tick_ref, out_ref, sems):
    tick_ref[...] = jnp.zeros_like(tick_ref)
    total = parts_ref[0]
    for j in range(1, parts_ref.shape[0]):
        total = total + parts_ref[j]
    total = jnp.maximum(1.0 - total, EPS_MIN)
    out_ref[...] = total
    for copy in fetch([(out_ref, copies_hbm.at[j]) for j in range(copies_hbm.shape[0])], sems):
        copy.wait()


def slip_kernel(
    first, count,
    after_any, brick_hbm, base_hbm, frac_hbm, pvel_hbm, coef_hbm, pvol_hbm, velocity_hbm,
    out_ref,
    brick_ref, base_ref, frac_ref, pvel_ref, coef_ref, pvol_ref, velocity_ref, table_ref, sems,
):
    some = pl.ds(first, count)
    wide = pl.ds(first * BLOCK, count * BLOCK)
    copies = fetch(
        [
            (velocity_hbm, velocity_ref),
            (brick_hbm, brick_ref),
            (base_hbm.at[some], base_ref),
            (frac_hbm.at[:, wide], frac_ref),
            (pvel_hbm.at[:, wide], pvel_ref),
            (coef_hbm.at[some], coef_ref),
            (pvol_hbm.at[some], pvol_ref),
        ],
        sems,
    )
    rows, lane = rows_iota(), lanes_iota()
    tiles_x = velocity_ref.shape[2] // 8

    def convert(number, carry):
        for k in range(2):
            tx = number * 2 + k
            at = pl.ds(pl.multiple_of(tx * 8, 8), 8)
            for c in range(3):
                tiles = transpose_granules([velocity_ref[c, z, at, :] for z in range(8)], lane)
                for t3 in range(8):
                    table_ref[(tx * 3 + c) * 8 + t3] = tiles[t3]
        return carry

    copies[0].wait()
    lax.fori_loop(0, tiles_x // 2, convert, 0)
    for copy in copies[1:]:
        copy.wait()

    def step(number, carry):
        for k in range(UNROLL):
            block = number * UNROLL + k
            at, zb, xb, yb, fz, fx, fy = particles(base_ref, frac_ref, block)
            tx, t3, t1 = brick_place(brick_ref[first + block])
            kx = axis_weights(rows, xb, fx)
            corners = corner_terms(zb, yb, fz, fy, t1 * 64)
            rel = [
                interpolate(table_ref[(tx * 3 + c) * 8 + t3], kx, corners) - pvel_ref[c : c + 1, at]
                for c in range(3)
            ]
            speed = rel[0] * rel[0] + rel[1] * rel[1] + rel[2] * rel[2]
            factor = coef_ref[pl.ds(block, 1), :] * pvol_ref[pl.ds(block, 1), :]
            factor = factor * jnp.exp(FLOW_POWER * jnp.log(speed + 0.01))
            for c in range(3):
                out_ref[c : c + 1, at] = factor * rel[c]
        return carry

    lax.fori_loop(0, count // UNROLL, step, 0)


def pack_halo(rows, tiles):
    a, b, c, d = tiles
    middle = jnp.logical_or(rows == 3, rows == 4)
    first = jnp.where(middle, pltpu.roll(d, 3, 0), a)
    second = jnp.where(rows == 3, pltpu.roll(d, 1, 0), jnp.where(rows == 4, pltpu.roll(d, 7, 0), b))
    third = jnp.where(middle, pltpu.roll(d, 5, 0), c)
    return first, second, third


def unpack_halo(rows, tiles):
    a, b, c = tiles
    inner = jnp.where(rows == 2, pltpu.roll(b, 7, 0), pltpu.roll(b, 1, 0))
    d = jnp.where(rows < 2, pltpu.roll(a, 5, 0), jnp.where(rows > 5, pltpu.roll(c, 3, 0), inner))
    return a, b, c, d


def drag_kernel(
    brick_hbm, base_ref, frac_ref, slip_a_ref, slip_b_ref, eps_ref,
    drag_ref, out_hbm, tick_ref,
    force_ref, late_ref, brick_ref, sems,
):
    subs = force_ref.shape[0]
    rows, lane = rows_iota(), lanes_iota()
    (copy,) = fetch([(brick_hbm, brick_ref)], sems)
    for j in range(subs):
        force_ref[j, 0:48] = jnp.zeros((48, 8, LANES), F32)
    copy.wait()

    late_ref[...] = jnp.zeros_like(late_ref)

    def add(number):
        for k in range(LONG):
            tx, t3, t1 = brick_place(brick_ref[number * LONG + k])
            mine = (lane >> 6) == t1
            for c in range(3):
                tile = (tx & 1) * 24 + c * 8 + t3
                force_ref[tx >> 1, tile] += jnp.where(mine, late_ref[k, 8 * c : 8 * c + 8], 0.0)

    steps = base_ref.shape[0] // LONG
    for slip_ref, start in ((slip_a_ref, 0), (slip_b_ref, steps // 2)):

        def step(number, carry, slip_ref=slip_ref, start=start):
            add(jnp.maximum(number - 1, 0))
            found = []
            for k in range(LONG):
                block = number * LONG + k
                inner = block - start * LONG
                at, zb, xb, yb, fz, fx, fy = particles(base_ref, frac_ref, block)
                inner_at = pl.ds(pl.multiple_of(inner * BLOCK, BLOCK), BLOCK)
                tx, t3, t1 = brick_place(brick_ref[block])
                kx = axis_weights(rows, xb, fx)
                eps = interpolate(eps_ref[tx * 8 + t3], kx, corner_terms(zb, yb, fz, fy, t1 * 64))
                factor = jnp.exp(DRAG_POWER * jnp.log(eps))
                parts = []
                for c in range(3):
                    force = factor * slip_ref[c : c + 1, inner_at]
                    drag_ref[c : c + 1, at] = force
                    parts.append(kx * spread(force))
                found.append((parts, plane_weights(rows, zb, yb, fz, fy)))
                if k % 2:
                    late_ref[k - 1], late_ref[k] = deposit(found[-2:])
            return carry

        lax.fori_loop(start, start + steps // 2, step, 0)
    add(steps - 1)
    copies = fetch([(force_ref.at[j, 0:48], out_hbm.at[j, 0:48]) for j in range(subs)], sems)
    zero = jnp.zeros((8, LANES), F32)
    tick_ref[...] = zero
    for j in range(subs):
        for quad in range(6):
            tiles = []
            for at in range(quad * 4, quad * 4 + 4):
                after = force_ref[j + 1, at] if j + 1 < subs else zero
                before = force_ref[j - 1, 24 + at] if j > 0 else zero
                tiles.append(jnp.where(rows < 4, after, before))
            for n, tile in enumerate(pack_halo(rows, tiles)):
                force_ref[j, 48 + quad * 3 + n] = tile
        copy = pltpu.make_async_copy(
            force_ref.at[j, 48:66], out_hbm.at[j, 48:66], sems.at[subs + j]
        )
        copy.start()
        copies.append(copy)
    for copy in copies:
        copy.wait()


def source_kernel(parts_ref, eps_ref, first_any, own_ref, even_ref, odd_ref):
    lane, rows = lanes_iota(), rows_iota()
    even = lax.axis_index("slab") % 2 == 0

    def summed(at):
        total = parts_ref[0, at]
        for j in range(1, parts_ref.shape[0]):
            total = total + parts_ref[j, at]
        return total

    for t in range(3):
        for c in range(3):
            if t < 2:
                forces = [summed(t * 24 + c * 8 + t3) for t3 in range(8)]
            else:
                forces = []
                for quad in (2 * c, 2 * c + 1):
                    forces += unpack_halo(rows, [summed(48 + quad * 3 + k) for k in range(3)])
            tiles = []
            for t3 in range(8):
                tiles.append(-forces[t3] / eps_ref[t * 8 + t3])
            tiles = transpose_granules(tiles, lane)
            first = 8 * (t + 1) % 24
            for z in range(8):
                own_ref[c, z, first : first + 8, :] = tiles[z]
            for n in range(3):
                at = slice(first, first + 8)
                even_ref[c, n, at, :] = jnp.where(even, tiles[5 + n], tiles[n])
                odd_ref[c, n, at, :] = jnp.where(even, tiles[n], tiles[5 + n])


def window_kernel(after_any, velocity_hbm, out_ref, even_ref, odd_ref, sems):
    even = lax.axis_index("slab") % 2 == 0
    depth = velocity_hbm.shape[1]
    tiles_x = velocity_hbm.shape[2] // 8
    pairs, inside = [], []
    for r in range(4):
        want = lax.axis_index("sub") * 2 + r - 1
        inside.append(jnp.logical_and(want >= 0, want < tiles_x))
        at = pl.ds(pl.multiple_of(jnp.clip(want, 0, tiles_x - 1) * 8, 8), 8)
        pairs.append((velocity_hbm.at[:, :, at, :], out_ref.at[:, :, 8 * r : 8 * r + 8, :]))
    for copy in fetch(pairs, sems):
        copy.wait()
    for r in range(4):
        at = slice(8 * r, 8 * r + 8)
        rows = jnp.where(inside[r], out_ref[:, :, at, :], 0.0)
        out_ref[:, :, at, :] = rows
        even_ref[:, :, at, :] = jnp.where(even, rows[:, depth - 4 :], rows[:, :4])
        odd_ref[:, :, at, :] = jnp.where(even, rows[:, :4], rows[:, depth - 4 :])


def void_kernel(after_any, eps_ref, out_ref, near_ref):
    lane, rows = lanes_iota(), rows_iota()
    tiles_x = out_ref.shape[1] // 8

    def convert(number, carry):
        for k in range(4):
            tx = number * 4 + k
            tiles = transpose_granules([eps_ref[tx * 8 + t3] for t3 in range(8)], lane)
            for z in range(8):
                out_ref[z, pl.ds(pl.multiple_of(tx * 8, 8), 8), :] = tiles[z]
        return carry

    lax.fori_loop(0, tiles_x // 4, convert, 0)
    own = lax.axis_index("sub") * 2
    near_ref[0:16] = eps_ref[pl.ds(own * 8, 16)]
    after = eps_ref[pl.ds(jnp.minimum(own + 2, tiles_x - 1) * 8, 8)]
    before = eps_ref[pl.ds(jnp.maximum(own - 1, 0) * 8, 8)]
    near_ref[16:24] = jnp.where(rows[None] < 4, after, before)


def edges():
    slab, sub = lax.axis_index("slab"), lax.axis_index("sub")
    planes, width = lax.axis_size("slab") * 8, lax.axis_size("sub") * 16
    row = lax.broadcasted_iota(jnp.int32, (32, LANES), 0) + sub * 16 - 8
    inside_x = jnp.logical_and(row >= 0, row < width)

    def keep(z):
        height = slab * 8 - 4 + z
        return jnp.logical_and(inside_x, jnp.logical_and(height >= 0, height < planes))

    return keep


def unforced(old, z, lane):
    shear = None
    centres, laps = [], []
    for c in range(3):
        centre = old[c, z]
        upper = old[c, z + 1]
        lower = old[c, z - 1]
        east = pltpu.roll(centre, 31, 0)
        west = pltpu.roll(centre, 1, 0)
        north = jnp.where(lane == LANES - 1, 0.0, pltpu.roll(centre, LANES - 1, 1))
        south = jnp.where(lane == 0, 0.0, pltpu.roll(centre, 1, 1))
        term = (upper - centre) ** 2 + (east - centre) ** 2 + (north - centre) ** 2
        shear = term if shear is None else shear + term
        centres.append(centre)
        laps.append(upper + lower + east + west + north + south - 6.0 * centre)
    viscous = (TIME_STEP * VISCOSITY) * jnp.exp(FLOW_POWER * jnp.log(shear + 0.01))
    return [centres[c] + viscous * laps[c] for c in range(3)]


def first_kernel(window_ref, even_ref, odd_ref, out_ref, tick_ref, old):
    tick_ref[...] = jnp.zeros_like(tick_ref)
    side = lax.axis_index("slab") % 2
    old[:, pl.ds(12 - 12 * side, 4)] = even_ref[...]
    old[:, pl.ds(12 * side, 4)] = odd_ref[...]
    old[:, 4:12] = window_ref[...]
    lane = lax.broadcasted_iota(jnp.int32, (32, LANES), 1)

    def plane(number, carry):
        for k in range(2):
            z = number * 2 + k
            moved = unforced(old, z + 1, lane)
            for c in range(3):
                out_ref[c, z] = moved[c]
        return carry

    lax.fori_loop(0, 7, plane, 0)


def forced(old, new, source, z, keep, lane):
    moved = unforced(old, z, lane)
    inside = keep(z)
    for c in range(3):
        total = moved[c] + TIME_STEP * source[c, z - 1]
        new[c, z] = jnp.where(inside, total, 0.0)


def near_kernel(first_ref, own_ref, even_ref, *refs):
    keeps, last_ref, levels, source = refs[:3], refs[3], refs[4:8], refs[8]
    keep = edges()
    lane = lax.broadcasted_iota(jnp.int32, (32, LANES), 1)
    side = lax.axis_index("slab") % 2

    def plane(n):
        return n + side * (15 - 2 * n)

    for part, planes in ((own_ref, slice(3, 11)), (even_ref, pl.ds(11 - 11 * side, 3))):
        source[:, planes, 0:24, :] = part[...]
        source[:, planes, 24:32, :] = part[:, :, 0:8, :]
    for n in range(4, 15):
        z = plane(n)
        inside = keep(z)
        for c in range(3):
            moved = first_ref[c, z - 1] + TIME_STEP * source[c, z - 1]
            levels[0][c, z] = jnp.where(inside, moved, 0.0)
    for step in range(1, ITERS):

        def run(n, carry, step=step):
            forced(levels[step - 1], levels[step], source, plane(n), keep, lane)
            return carry

        lax.fori_loop(4 + step, 15 - step, run, 0)
    for step in range(3):
        for n in range(2):
            for c in range(3):
                keeps[step][c, n] = levels[step][c, plane(4 + step + n)]
    for n in range(5):
        for c in range(3):
            last_ref[c, n] = levels[3][c, plane(7 + n), 8:24, :]


def far_kernel(first_ref, own_ref, odd_ref, *refs):
    keeps, last_ref, out_ref, levels, source = refs[:3], refs[3], refs[4], refs[5:9], refs[9]
    keep = edges()
    lane = lax.broadcasted_iota(jnp.int32, (32, LANES), 1)
    side = lax.axis_index("slab") % 2

    def plane(n):
        return n + side * (15 - 2 * n)

    for part, planes in ((own_ref, slice(3, 11)), (odd_ref, pl.ds(11 * side, 3))):
        source[:, planes, 0:24, :] = part[...]
        source[:, planes, 24:32, :] = part[:, :, 0:8, :]
    for step in range(3):
        for n in range(2):
            for c in range(3):
                levels[step][c, plane(4 + step + n)] = keeps[step][c, n]
    for n in range(1, 4):
        z = plane(n)
        inside = keep(z)
        for c in range(3):
            moved = first_ref[c, z - 1] + TIME_STEP * source[c, z - 1]
            levels[0][c, z] = jnp.where(inside, moved, 0.0)
    for step in range(1, ITERS):
        for n in range(1 + step, 4 + step):
            forced(levels[step - 1], levels[step], source, plane(n), keep, lane)
    for c in range(3):
        for n in range(3):
            z = plane(4 + n)
            rows = levels[3][c, z, 8:24, :]
            for j in range(out_ref.shape[0]):
                out_ref[j, c, z - 4] = rows
        for n in range(5):
            rows = last_ref[c, n]
            for j in range(out_ref.shape[0]):
                out_ref[j, c, plane(7 + n) - 4] = rows


def place_kernel(parts_ref, out_ref, sems):
    rows = parts_ref.shape[3]
    pairs = []
    for j in range(parts_ref.shape[0]):
        pairs.append((parts_ref.at[j], out_ref.at[:, :, j * rows : (j + 1) * rows, :]))
    for copy in fetch(pairs, sems):
        copy.wait()


def pinned(*arrays):
    return [pltpu.with_memory_space_constraint(x, pltpu.HBM) for x in arrays]


def call(kernel, out_shapes, ins, scratch=(), outs=None, us=1.0):
    outs = outs or [VMEM] * len(out_shapes)
    return pl.pallas_call(
        kernel,
        out_shape=[
            pltpu.HBM(s, F32) if spec is HBM else jax.ShapeDtypeStruct(s, F32)
            for s, spec in zip(out_shapes, outs)
        ],
        in_specs=ins,
        out_specs=outs,
        scratch_shapes=list(scratch),
        compiler_params=PARAMS,
        cost_estimate=pl.CostEstimate(flops=int(us * 1e9), bytes_accessed=int(us * 3.6e6), transcendentals=0),
    )


def pair_up(x, first):
    pairs = [(i, i + 1) for i in range(first, lax.axis_size("slab") - 1, 2)]
    return lax.ppermute(x, "slab", pairs + [(j, i) for i, j in pairs])


def body(velocity, part_vel, fraction, base_cell, drag_coeff, part_volume, brick_of_block):
    depth, width_x = velocity.shape[1], velocity.shape[2]
    blocks = brick_of_block.shape[0]
    subs = lax.axis_size("sub")
    tiles_x = width_x // 8
    tiles = tiles_x * 8
    share = tiles // subs
    base = base_cell.reshape(blocks, BLOCK)
    coef = drag_coeff.reshape(blocks, BLOCK)
    pvol = part_volume.reshape(blocks, BLOCK)

    particles_vmem = [
        pltpu.SMEM((blocks,), jnp.int32),
        pltpu.VMEM((blocks, BLOCK), jnp.int32),
        pltpu.VMEM((3, blocks * BLOCK), F32),
    ]
    row_vmem = pltpu.VMEM((blocks, BLOCK), F32)
    solid, solid_tick = call(
        solid_kernel,
        [(tiles, 8, LANES), (8, LANES)],
        [HBM] * 4,
        [pltpu.VMEM((tiles, 8, LANES), F32), pltpu.VMEM((LONG, 8, LANES), F32)]
        + particles_vmem
        + [row_vmem, pltpu.SemaphoreType.DMA((4,))],
        outs=[HBM, VMEM],
        us=5.0,
    )(*pinned(brick_of_block, base, fraction, pvol))
    solid_parts = lax.all_to_all(solid.reshape(subs, share, 8, LANES), "sub", 0, 0)
    half = blocks // 2

    def slip_of(first, after):
        (slip,) = call(
            functools.partial(slip_kernel, first, half),
            [(3, half * BLOCK)],
            [ANY] + [HBM] * 7,
            [
                pltpu.SMEM((blocks,), jnp.int32),
                pltpu.VMEM((half, BLOCK), jnp.int32),
                pltpu.VMEM((3, half * BLOCK), F32),
                pltpu.VMEM((3, half * BLOCK), F32),
                pltpu.VMEM((half, BLOCK), F32),
                pltpu.VMEM((half, BLOCK), F32),
                pltpu.VMEM(velocity.shape, F32),
                pltpu.VMEM((3 * tiles, 8, LANES), F32),
                pltpu.SemaphoreType.DMA((7,)),
            ],
            us=5.0,
            )(after, brick_of_block, base, fraction, part_vel, coef, pvol, velocity)
        return slip

    slip_a = slip_of(0, solid_tick)
    eps_copies, eps_tick = call(
        eps_kernel,
        [(subs, share, 8, LANES), (8, LANES)],
        [VMEM],
        [pltpu.VMEM((share, 8, LANES), F32), pltpu.SemaphoreType.DMA((subs,))],
        outs=[HBM, VMEM],
        us=0.5,
    )(solid_parts)
    slip_b = slip_of(half, eps_tick)
    eps = lax.all_to_all(eps_copies, "sub", 0, 0).reshape(tiles, 8, LANES)
    drag, force, tick = call(
        drag_kernel,
        [(3, blocks * BLOCK), (subs, 66, 8, LANES), (8, LANES)],
        [HBM] + [VMEM] * 5,
        [
            pltpu.VMEM((subs, 66, 8, LANES), F32),
            pltpu.VMEM((LONG, 24, LANES), F32),
            pltpu.SMEM((blocks,), jnp.int32),
            pltpu.SemaphoreType.DMA((2 * subs,)),
        ],
        outs=[VMEM, HBM, VMEM],
        us=6.0,
    )(*pinned(brick_of_block), base, fraction, slip_a, slip_b, eps)
    forces = lax.all_to_all(force, "sub", 0, 0)
    window, even, odd = call(
        window_kernel,
        [(3, depth, 32, LANES), (3, 4, 32, LANES), (3, 4, 32, LANES)],
        [ANY, HBM],
        [pltpu.SemaphoreType.DMA((4,))],
    )(tick, *pinned(velocity))
    even, odd = pair_up(even, 0), pair_up(odd, 1)
    voidfraction, near = call(
        void_kernel, [(depth, width_x, LANES), (24, 8, LANES)], [ANY, VMEM], us=2.0
    )(tick, eps)
    first, first_tick = call(
        first_kernel,
        [(3, 14, 32, LANES), (8, LANES)],
        [VMEM] * 3,
        [pltpu.VMEM((3, 16, 32, LANES), F32)],
        us=1.0,
    )(window, even, odd)

    rows = width_x // subs
    own, even, odd = call(
        source_kernel,
        [(3, depth, 24, LANES), (3, 3, 24, LANES), (3, 3, 24, LANES)],
        [VMEM, VMEM, ANY],
    )(forces, near, first_tick)
    even, odd = pair_up(even, 0), pair_up(odd, 1)
    buffers = [pltpu.VMEM((3, 16, 32, LANES), F32)] * 4 + [pltpu.VMEM((3, 14, 32, LANES), F32)]
    known = call(
        near_kernel,
        [(3, 2, 32, LANES)] * 3 + [(3, 5, rows, LANES)],
        [VMEM] * 3,
        buffers,
        us=2.0,
    )(first, own, even)
    (moved,) = call(
        far_kernel, [(subs, 3, depth, rows, LANES)], [VMEM] * 7, buffers, us=1.0
    )(first, own, odd, *known)
    moved = lax.all_to_all(moved, "sub", 0, 0)
    (new_velocity,) = call(
        place_kernel,
        [velocity.shape],
        [ANY],
        [pltpu.SemaphoreType.DMA((subs,))],
        outs=[HBM],
    )(moved)
    return new_velocity, voidfraction, drag


def solution(mesh):
    in_specs = (
        P(None, "slab", None, None),
        P(None, ("slab", "sub")),
        P(None, ("slab", "sub")),
        P(("slab", "sub")),
        P(("slab", "sub")),
        P(("slab", "sub")),
        P(("slab", "sub")),
    )
    out_specs = (P(None, "slab", None, None), P("slab", None, None), P(None, ("slab", "sub")))
    return jax.shard_map(body, mesh=mesh, in_specs=in_specs, out_specs=out_specs, check_vma=False)
```

```python
import functools

import jax
import jax.numpy as jnp
from jax import lax
from jax.experimental import pallas as pl
from jax.experimental.pallas import tpu as pltpu
from jax.sharding import PartitionSpec as P

BLOCK = 128
LANES = 128
EPS_MIN = 0.35
FLOW_POWER = -0.2
DRAG_POWER = -2.65
VISCOSITY = 1.2
TIME_STEP = 0.05
ITERS = 4
UNROLL = 16
LONG = 32
F32 = jnp.float32
PARAMS = pltpu.CompilerParams(vmem_limit_bytes=16 * 1024 * 1024)
VMEM = pl.BlockSpec(memory_space=pltpu.VMEM)
SMEM = pl.BlockSpec(memory_space=pltpu.SMEM)
HBM = pl.BlockSpec(memory_space=pltpu.HBM)
ANY = pl.BlockSpec(memory_space=pl.ANY)


def transpose_granules(tiles, lane):
    for bit in (1, 2, 4):
        shift = 8 * bit
        high = (lane & shift) != 0
        new = list(tiles)
        for a in range(8):
            if a & bit:
                continue
            b = a | bit
            va, vb = tiles[a], tiles[b]
            new[a] = jnp.where(high, pltpu.roll(vb, shift, 1), va)
            new[b] = jnp.where(high, vb, pltpu.roll(va, LANES - shift, 1))
        tiles = new
    return tiles


def fetch(pairs, sems):
    copies = [pltpu.make_async_copy(a, b, sems.at[i]) for i, (a, b) in enumerate(pairs)]
    for copy in copies:
        copy.start()
    return copies


def lanes_iota():
    return lax.broadcasted_iota(jnp.int32, (8, LANES), 1)


def rows_iota():
    return lax.broadcasted_iota(jnp.int32, (8, LANES), 0)


def spread(row):
    return jnp.broadcast_to(row, (8, LANES))


def particles(base_ref, frac_ref, block):
    at = pl.ds(pl.multiple_of(block * BLOCK, BLOCK), BLOCK)
    base = spread(base_ref[pl.ds(block, 1), :])
    fz = spread(frac_ref[0:1, at])
    fx = spread(frac_ref[1:2, at])
    fy = spread(frac_ref[2:3, at])
    return at, base >> 6, (base >> 3) & 7, base & 7, fz, fx, fy


def axis_weights(rows, first, frac):
    zero = jnp.zeros_like(frac)
    return jnp.where(rows == first, 1.0 - frac, jnp.where(rows == first + 1, frac, zero))


def halves(value):
    high = value.astype(jnp.bfloat16).astype(F32)
    return high, value - high


def plane_weights(rows, zb, yb, fz, fy):
    ky = axis_weights(rows, yb, fy)
    number = zb.astype(F32)
    offset = jnp.concatenate([number, number - 1.0], axis=0).astype(jnp.bfloat16)
    zero = jnp.zeros((16, LANES), jnp.bfloat16)

    def twice(value):
        return jnp.concatenate([value, value], axis=0).astype(jnp.bfloat16)

    parts = []
    for here, above in zip(halves((1.0 - fz) * ky), halves(fz * ky)):
        here, above = twice(here), twice(above)
        for q in range(4):
            upper = jnp.where(offset == 2 * q - 1, above, zero)
            parts.append(jnp.where(offset == 2 * q, here, upper))
    return jnp.concatenate(parts, axis=0)


def split_rows(parts):
    full = jnp.concatenate(parts, axis=0)
    high = full.astype(jnp.bfloat16).astype(F32)
    return jnp.concatenate([high, full - high], axis=0).astype(jnp.bfloat16)


def deposit(blocks):
    left = []
    for n, (parts, _) in enumerate(blocks):
        rows = split_rows(parts)
        pair = [rows, jnp.zeros_like(rows)]
        left.append(jnp.concatenate(pair if n == 0 else pair[::-1], axis=1))
    both = lax.dot_general(
        jnp.concatenate(left, axis=0),
        jnp.concatenate([weights for _, weights in blocks], axis=1),
        (((1,), (1,)), ((), ())),
        preferred_element_type=F32,
    )
    half = both.shape[0] // 4
    found = []
    for n in range(2):
        total = both[2 * n * half : (2 * n + 1) * half] + both[(2 * n + 1) * half : (2 * n + 2) * half]
        found.append(total + pltpu.roll(total, 64, 1))
    return found


def corner_terms(zb, yb, fz, fy, offset):
    index = (zb << 3) + yb + offset
    gz, gy = 1.0 - fz, 1.0 - fy
    return (
        (index, gz * gy),
        (index + 1, gz * fy),
        (index + 8, fz * gy),
        (index + 9, fz * fy),
    )


def interpolate(tile, kx, corners):
    total = None
    for index, weight in corners:
        term = weight * jnp.take_along_axis(tile, index, axis=1, mode="promise_in_bounds")
        total = term if total is None else total + term
    return jnp.sum(kx * total, axis=0, keepdims=True)


def brick_place(brick):
    return brick >> 4, brick & 7, (brick >> 3) & 1


def solid_kernel(
    brick_hbm, base_hbm, frac_hbm, pvol_hbm, out_hbm, tick_ref,
    out_ref, late_ref, brick_ref, base_ref, frac_ref, pvol_ref, sems,
):
    copies = fetch(
        [(brick_hbm, brick_ref), (base_hbm, base_ref), (frac_hbm, frac_ref), (pvol_hbm, pvol_ref)],
        sems,
    )
    out_ref[...] = jnp.zeros_like(out_ref)
    for copy in copies:
        copy.wait()
    rows, lane = rows_iota(), lanes_iota()
    late_ref[...] = jnp.zeros_like(late_ref)

    def add(number):
        for k in range(LONG):
            tx, t3, t1 = brick_place(brick_ref[number * LONG + k])
            out_ref[tx * 8 + t3] += jnp.where((lane >> 6) == t1, late_ref[k], 0.0)

    def step(number, carry):
        add(jnp.maximum(number - 1, 0))
        found = []
        for k in range(LONG):
            block = number * LONG + k
            _, zb, xb, yb, fz, fx, fy = particles(base_ref, frac_ref, block)
            kx = axis_weights(rows, xb, fx) * spread(pvol_ref[pl.ds(block, 1), :])
            found.append(([kx], plane_weights(rows, zb, yb, fz, fy)))
            if k % 2:
                late_ref[k - 1], late_ref[k] = deposit(found[-2:])
        return carry

    steps = base_ref.shape[0] // LONG
    lax.fori_loop(0, steps, step, 0)
    add(steps - 1)
    (copy,) = fetch([(out_ref, out_hbm)], sems)
    tick_ref[...] = jnp.zeros_like(tick_ref)
    copy.wait()


def eps_kernel(parts_ref, copies_hbm, tick_ref, out_ref, sems):
    tick_ref[...] = jnp.zeros_like(tick_ref)
    total = parts_ref[0]
    for j in range(1, parts_ref.shape[0]):
        total = total + parts_ref[j]
    total = jnp.maximum(1.0 - total, EPS_MIN)
    out_ref[...] = total
    for copy in fetch([(out_ref, copies_hbm.at[j]) for j in range(copies_hbm.shape[0])], sems):
        copy.wait()


def slip_work(
    first, count,
    brick_hbm, base_hbm, frac_hbm, pvel_hbm, coef_hbm, pvol_hbm, velocity_hbm,
    out_ref,
    brick_ref, base_ref, frac_ref, pvel_ref, coef_ref, pvol_ref, velocity_ref, table_ref, sems,
):
    some = pl.ds(first, count)
    wide = pl.ds(first * BLOCK, count * BLOCK)
    copies = fetch(
        [
            (velocity_hbm, velocity_ref),
            (brick_hbm, brick_ref),
            (base_hbm.at[some], base_ref),
            (frac_hbm.at[:, wide], frac_ref),
            (pvel_hbm.at[:, wide], pvel_ref),
            (coef_hbm.at[some], coef_ref),
            (pvol_hbm.at[some], pvol_ref),
        ],
        sems,
    )
    rows, lane = rows_iota(), lanes_iota()
    tiles_x = velocity_ref.shape[2] // 8

    def convert(number, carry):
        for k in range(2):
            tx = number * 2 + k
            at = pl.ds(pl.multiple_of(tx * 8, 8), 8)
            for c in range(3):
                tiles = transpose_granules([velocity_ref[c, z, at, :] for z in range(8)], lane)
                for t3 in range(8):
                    table_ref[(tx * 3 + c) * 8 + t3] = tiles[t3]
        return carry

    copies[0].wait()
    lax.fori_loop(0, tiles_x // 2, convert, 0)
    for copy in copies[1:]:
        copy.wait()

    def step(number, carry):
        for k in range(UNROLL):
            block = number * UNROLL + k
            at, zb, xb, yb, fz, fx, fy = particles(base_ref, frac_ref, block)
            tx, t3, t1 = brick_place(brick_ref[first + block])
            kx = axis_weights(rows, xb, fx)
            corners = corner_terms(zb, yb, fz, fy, t1 * 64)
            rel = [
                interpolate(table_ref[(tx * 3 + c) * 8 + t3], kx, corners) - pvel_ref[c : c + 1, at]
                for c in range(3)
            ]
            speed = rel[0] * rel[0] + rel[1] * rel[1] + rel[2] * rel[2]
            factor = coef_ref[pl.ds(block, 1), :] * pvol_ref[pl.ds(block, 1), :]
            factor = factor * jnp.exp(FLOW_POWER * jnp.log(speed + 0.01))
            for c in range(3):
                out_ref[c : c + 1, at] = factor * rel[c]
        return carry

    lax.fori_loop(0, count // UNROLL, step, 0)


def pack_halo(rows, tiles):
    a, b, c, d = tiles
    middle = jnp.logical_or(rows == 3, rows == 4)
    first = jnp.where(middle, pltpu.roll(d, 3, 0), a)
    second = jnp.where(rows == 3, pltpu.roll(d, 1, 0), jnp.where(rows == 4, pltpu.roll(d, 7, 0), b))
    third = jnp.where(middle, pltpu.roll(d, 5, 0), c)
    return first, second, third


def unpack_halo(rows, tiles):
    a, b, c = tiles
    inner = jnp.where(rows == 2, pltpu.roll(b, 7, 0), pltpu.roll(b, 1, 0))
    d = jnp.where(rows < 2, pltpu.roll(a, 5, 0), jnp.where(rows > 5, pltpu.roll(c, 3, 0), inner))
    return a, b, c, d


def slip_kernel(first, count, after_any, *refs):
    slip_work(first, count, *refs)


def even_slip_kernel(count, after_any, early_ref, *refs):
    out_ref = refs[7]
    odd = lax.axis_index("slab") % 2 == 1

    @pl.when(odd)
    def _():
        out_ref[...] = early_ref[...]

    @pl.when(jnp.logical_not(odd))
    def _():
        slip_work(0, count, *refs)


def start_kernel(
    count,
    brick_hbm, base_hbm, frac_hbm, pvel_hbm, coef_hbm, pvol_hbm, velocity_hbm,
    out_hbm, tick_ref, early_ref,
    *scratch,
):
    @pl.when(lax.axis_index("slab") % 2 == 1)
    def _():
        slip_work(
            0, count,
            brick_hbm, base_hbm, frac_hbm, pvel_hbm, coef_hbm, pvol_hbm, velocity_hbm,
            early_ref, *scratch[7:],
        )

    solid_kernel(brick_hbm, base_hbm, frac_hbm, pvol_hbm, out_hbm, tick_ref, *scratch[:7])


def drag_kernel(
    brick_hbm, base_ref, frac_ref, slip_a_ref, slip_b_ref, eps_ref,
    drag_ref, out_hbm, tick_ref,
    force_ref, late_ref, brick_ref, sems,
):
    subs = force_ref.shape[0]
    rows, lane = rows_iota(), lanes_iota()
    (copy,) = fetch([(brick_hbm, brick_ref)], sems)
    for j in range(subs):
        force_ref[j, 0:48] = jnp.zeros((48, 8, LANES), F32)
    copy.wait()

    late_ref[...] = jnp.zeros_like(late_ref)

    def add(number):
        for k in range(LONG):
            tx, t3, t1 = brick_place(brick_ref[number * LONG + k])
            mine = (lane >> 6) == t1
            for c in range(3):
                tile = (tx & 1) * 24 + c * 8 + t3
                force_ref[tx >> 1, tile] += jnp.where(mine, late_ref[k, 8 * c : 8 * c + 8], 0.0)

    steps = base_ref.shape[0] // LONG
    for slip_ref, start in ((slip_a_ref, 0), (slip_b_ref, steps // 2)):

        def step(number, carry, slip_ref=slip_ref, start=start):
            add(jnp.maximum(number - 1, 0))
            found = []
            for k in range(LONG):
                block = number * LONG + k
                inner = block - start * LONG
                at, zb, xb, yb, fz, fx, fy = particles(base_ref, frac_ref, block)
                inner_at = pl.ds(pl.multiple_of(inner * BLOCK, BLOCK), BLOCK)
                tx, t3, t1 = brick_place(brick_ref[block])
                kx = axis_weights(rows, xb, fx)
                eps = interpolate(eps_ref[tx * 8 + t3], kx, corner_terms(zb, yb, fz, fy, t1 * 64))
                factor = jnp.exp(DRAG_POWER * jnp.log(eps))
                parts = []
                for c in range(3):
                    force = factor * slip_ref[c : c + 1, inner_at]
                    drag_ref[c : c + 1, at] = force
                    parts.append(kx * spread(force))
                found.append((parts, plane_weights(rows, zb, yb, fz, fy)))
                if k % 2:
                    late_ref[k - 1], late_ref[k] = deposit(found[-2:])
            return carry

        lax.fori_loop(start, start + steps // 2, step, 0)
    add(steps - 1)
    copies = fetch([(force_ref.at[j, 0:48], out_hbm.at[j, 0:48]) for j in range(subs)], sems)
    zero = jnp.zeros((8, LANES), F32)
    tick_ref[...] = zero
    for j in range(subs):
        for quad in range(6):
            tiles = []
            for at in range(quad * 4, quad * 4 + 4):
                after = force_ref[j + 1, at] if j + 1 < subs else zero
                before = force_ref[j - 1, 24 + at] if j > 0 else zero
                tiles.append(jnp.where(rows < 4, after, before))
            for n, tile in enumerate(pack_halo(rows, tiles)):
                force_ref[j, 48 + quad * 3 + n] = tile
        copy = pltpu.make_async_copy(
            force_ref.at[j, 48:66], out_hbm.at[j, 48:66], sems.at[subs + j]
        )
        copy.start()
        copies.append(copy)
    for copy in copies:
        copy.wait()


def source_kernel(parts_ref, eps_ref, first_any, own_ref, even_ref, odd_ref):
    lane, rows = lanes_iota(), rows_iota()
    even = lax.axis_index("slab") % 2 == 0

    def summed(at):
        total = parts_ref[0, at]
        for j in range(1, parts_ref.shape[0]):
            total = total + parts_ref[j, at]
        return total

    for t in range(3):
        for c in range(3):
            if t < 2:
                forces = [summed(t * 24 + c * 8 + t3) for t3 in range(8)]
            else:
                forces = []
                for quad in (2 * c, 2 * c + 1):
                    forces += unpack_halo(rows, [summed(48 + quad * 3 + k) for k in range(3)])
            tiles = []
            for t3 in range(8):
                tiles.append(-forces[t3] / eps_ref[t * 8 + t3])
            tiles = transpose_granules(tiles, lane)
            first = 8 * (t + 1) % 24
            for z in range(8):
                own_ref[c, z, first : first + 8, :] = tiles[z]
            for n in range(3):
                at = slice(first, first + 8)
                even_ref[c, n, at, :] = jnp.where(even, tiles[5 + n], tiles[n])
                odd_ref[c, n, at, :] = jnp.where(even, tiles[n], tiles[5 + n])


def window_kernel(after_any, velocity_hbm, out_ref, even_ref, odd_ref, sems):
    even = lax.axis_index("slab") % 2 == 0
    depth = velocity_hbm.shape[1]
    tiles_x = velocity_hbm.shape[2] // 8
    pairs, inside = [], []
    for r in range(4):
        want = lax.axis_index("sub") * 2 + r - 1
        inside.append(jnp.logical_and(want >= 0, want < tiles_x))
        at = pl.ds(pl.multiple_of(jnp.clip(want, 0, tiles_x - 1) * 8, 8), 8)
        pairs.append((velocity_hbm.at[:, :, at, :], out_ref.at[:, :, 8 * r : 8 * r + 8, :]))
    for copy in fetch(pairs, sems):
        copy.wait()
    for r in range(4):
        at = slice(8 * r, 8 * r + 8)
        rows = jnp.where(inside[r], out_ref[:, :, at, :], 0.0)
        out_ref[:, :, at, :] = rows
        even_ref[:, :, at, :] = jnp.where(even, rows[:, depth - 4 :], rows[:, :4])
        odd_ref[:, :, at, :] = jnp.where(even, rows[:, :4], rows[:, depth - 4 :])


def void_kernel(after_any, eps_ref, out_ref, near_ref):
    lane, rows = lanes_iota(), rows_iota()
    tiles_x = out_ref.shape[1] // 8

    def convert(number, carry):
        for k in range(4):
            tx = number * 4 + k
            tiles = transpose_granules([eps_ref[tx * 8 + t3] for t3 in range(8)], lane)
            for z in range(8):
                out_ref[z, pl.ds(pl.multiple_of(tx * 8, 8), 8), :] = tiles[z]
        return carry

    lax.fori_loop(0, tiles_x // 4, convert, 0)
    own = lax.axis_index("sub") * 2
    near_ref[0:16] = eps_ref[pl.ds(own * 8, 16)]
    after = eps_ref[pl.ds(jnp.minimum(own + 2, tiles_x - 1) * 8, 8)]
    before = eps_ref[pl.ds(jnp.maximum(own - 1, 0) * 8, 8)]
    near_ref[16:24] = jnp.where(rows[None] < 4, after, before)


def edges():
    slab, sub = lax.axis_index("slab"), lax.axis_index("sub")
    planes, width = lax.axis_size("slab") * 8, lax.axis_size("sub") * 16
    row = lax.broadcasted_iota(jnp.int32, (32, LANES), 0) + sub * 16 - 8
    inside_x = jnp.logical_and(row >= 0, row < width)

    def keep(z):
        height = slab * 8 - 4 + z
        return jnp.logical_and(inside_x, jnp.logical_and(height >= 0, height < planes))

    return keep


def unforced(old, z, lane):
    shear = None
    centres, laps = [], []
    for c in range(3):
        centre = old[c, z]
        upper = old[c, z + 1]
        lower = old[c, z - 1]
        east = pltpu.roll(centre, 31, 0)
        west = pltpu.roll(centre, 1, 0)
        north = jnp.where(lane == LANES - 1, 0.0, pltpu.roll(centre, LANES - 1, 1))
        south = jnp.where(lane == 0, 0.0, pltpu.roll(centre, 1, 1))
        term = (upper - centre) ** 2 + (east - centre) ** 2 + (north - centre) ** 2
        shear = term if shear is None else shear + term
        centres.append(centre)
        laps.append(upper + lower + east + west + north + south - 6.0 * centre)
    viscous = (TIME_STEP * VISCOSITY) * jnp.exp(FLOW_POWER * jnp.log(shear + 0.01))
    return [centres[c] + viscous * laps[c] for c in range(3)]


def first_kernel(window_ref, even_ref, odd_ref, out_ref, tick_ref, old):
    tick_ref[...] = jnp.zeros_like(tick_ref)
    side = lax.axis_index("slab") % 2
    old[:, pl.ds(12 - 12 * side, 4)] = even_ref[...]
    old[:, pl.ds(12 * side, 4)] = odd_ref[...]
    old[:, 4:12] = window_ref[...]
    lane = lax.broadcasted_iota(jnp.int32, (32, LANES), 1)

    def plane(number, carry):
        for k in range(2):
            z = number * 2 + k
            moved = unforced(old, z + 1, lane)
            for c in range(3):
                out_ref[c, z] = moved[c]
        return carry

    lax.fori_loop(0, 7, plane, 0)


def forced(old, new, source, z, keep, lane):
    moved = unforced(old, z, lane)
    inside = keep(z)
    for c in range(3):
        total = moved[c] + TIME_STEP * source[c, z - 1]
        new[c, z] = jnp.where(inside, total, 0.0)


def near_kernel(first_ref, own_ref, even_ref, *refs):
    keeps, last_ref, levels, source = refs[:3], refs[3], refs[4:8], refs[8]
    keep = edges()
    lane = lax.broadcasted_iota(jnp.int32, (32, LANES), 1)
    side = lax.axis_index("slab") % 2

    def plane(n):
        return n + side * (15 - 2 * n)

    for part, planes in ((own_ref, slice(3, 11)), (even_ref, pl.ds(11 - 11 * side, 3))):
        source[:, planes, 0:24, :] = part[...]
        source[:, planes, 24:32, :] = part[:, :, 0:8, :]
    for n in range(4, 15):
        z = plane(n)
        inside = keep(z)
        for c in range(3):
            moved = first_ref[c, z - 1] + TIME_STEP * source[c, z - 1]
            levels[0][c, z] = jnp.where(inside, moved, 0.0)
    for step in range(1, ITERS):

        def run(n, carry, step=step):
            forced(levels[step - 1], levels[step], source, plane(n), keep, lane)
            return carry

        lax.fori_loop(4 + step, 15 - step, run, 0)
    for step in range(3):
        for n in range(2):
            for c in range(3):
                keeps[step][c, n] = levels[step][c, plane(4 + step + n)]
    for n in range(5):
        for c in range(3):
            last_ref[c, n] = levels[3][c, plane(7 + n), 8:24, :]


def far_kernel(first_ref, own_ref, odd_ref, *refs):
    keeps, last_ref, out_ref, levels, source = refs[:3], refs[3], refs[4], refs[5:9], refs[9]
    keep = edges()
    lane = lax.broadcasted_iota(jnp.int32, (32, LANES), 1)
    side = lax.axis_index("slab") % 2

    def plane(n):
        return n + side * (15 - 2 * n)

    for part, planes in ((own_ref, slice(3, 11)), (odd_ref, pl.ds(11 * side, 3))):
        source[:, planes, 0:24, :] = part[...]
        source[:, planes, 24:32, :] = part[:, :, 0:8, :]
    for step in range(3):
        for n in range(2):
            for c in range(3):
                levels[step][c, plane(4 + step + n)] = keeps[step][c, n]
    for n in range(1, 4):
        z = plane(n)
        inside = keep(z)
        for c in range(3):
            moved = first_ref[c, z - 1] + TIME_STEP * source[c, z - 1]
            levels[0][c, z] = jnp.where(inside, moved, 0.0)
    for step in range(1, ITERS):
        for n in range(1 + step, 4 + step):
            forced(levels[step - 1], levels[step], source, plane(n), keep, lane)
    for c in range(3):
        for n in range(3):
            z = plane(4 + n)
            rows = levels[3][c, z, 8:24, :]
            for j in range(out_ref.shape[0]):
                out_ref[j, c, z - 4] = rows
        for n in range(5):
            rows = last_ref[c, n]
            for j in range(out_ref.shape[0]):
                out_ref[j, c, plane(7 + n) - 4] = rows


def place_kernel(parts_ref, out_ref, sems):
    rows = parts_ref.shape[3]
    pairs = []
    for j in range(parts_ref.shape[0]):
        pairs.append((parts_ref.at[j], out_ref.at[:, :, j * rows : (j + 1) * rows, :]))
    for copy in fetch(pairs, sems):
        copy.wait()


def pinned(*arrays):
    return [pltpu.with_memory_space_constraint(x, pltpu.HBM) for x in arrays]


def call(kernel, out_shapes, ins, scratch=(), outs=None, us=1.0):
    outs = outs or [VMEM] * len(out_shapes)
    return pl.pallas_call(
        kernel,
        out_shape=[
            pltpu.HBM(s, F32) if spec is HBM else jax.ShapeDtypeStruct(s, F32)
            for s, spec in zip(out_shapes, outs)
        ],
        in_specs=ins,
        out_specs=outs,
        scratch_shapes=list(scratch),
        compiler_params=PARAMS,
        cost_estimate=pl.CostEstimate(flops=int(us * 1e9), bytes_accessed=int(us * 3.6e6), transcendentals=0),
    )


def pair_up(x, first):
    pairs = [(i, i + 1) for i in range(first, lax.axis_size("slab") - 1, 2)]
    return lax.ppermute(x, "slab", pairs + [(j, i) for i, j in pairs])


def body(velocity, part_vel, fraction, base_cell, drag_coeff, part_volume, brick_of_block):
    depth, width_x = velocity.shape[1], velocity.shape[2]
    blocks = brick_of_block.shape[0]
    subs = lax.axis_size("sub")
    tiles_x = width_x // 8
    tiles = tiles_x * 8
    share = tiles // subs
    base = base_cell.reshape(blocks, BLOCK)
    coef = drag_coeff.reshape(blocks, BLOCK)
    pvol = part_volume.reshape(blocks, BLOCK)

    particles_vmem = [
        pltpu.SMEM((blocks,), jnp.int32),
        pltpu.VMEM((blocks, BLOCK), jnp.int32),
        pltpu.VMEM((3, blocks * BLOCK), F32),
    ]
    row_vmem = pltpu.VMEM((blocks, BLOCK), F32)
    half = blocks // 2
    slip_scratch = [
        pltpu.SMEM((blocks,), jnp.int32),
        pltpu.VMEM((half, BLOCK), jnp.int32),
        pltpu.VMEM((3, half * BLOCK), F32),
        pltpu.VMEM((3, half * BLOCK), F32),
        pltpu.VMEM((half, BLOCK), F32),
        pltpu.VMEM((half, BLOCK), F32),
        pltpu.VMEM(velocity.shape, F32),
        pltpu.VMEM((3 * tiles, 8, LANES), F32),
        pltpu.SemaphoreType.DMA((7,)),
    ]
    particle_args = pinned(brick_of_block, base, fraction, part_vel, coef, pvol, velocity)
    solid, solid_tick, early = call(
        functools.partial(start_kernel, half),
        [(tiles, 8, LANES), (8, LANES), (3, half * BLOCK)],
        [HBM] * 7,
        [pltpu.VMEM((tiles, 8, LANES), F32), pltpu.VMEM((LONG, 8, LANES), F32)]
        + particles_vmem
        + [row_vmem, pltpu.SemaphoreType.DMA((4,))]
        + slip_scratch,
        outs=[HBM, VMEM, VMEM],
        us=5.0,
    )(*particle_args)
    solid_parts = lax.all_to_all(solid.reshape(subs, share, 8, LANES), "sub", 0, 0)
    (slip_a,) = call(
        functools.partial(even_slip_kernel, half),
        [(3, half * BLOCK)],
        [ANY, VMEM] + [HBM] * 7,
        slip_scratch,
        us=5.0,
    )(solid_tick, early, *particle_args)
    eps_copies, eps_tick = call(
        eps_kernel,
        [(subs, share, 8, LANES), (8, LANES)],
        [VMEM],
        [pltpu.VMEM((share, 8, LANES), F32), pltpu.SemaphoreType.DMA((subs,))],
        outs=[HBM, VMEM],
        us=0.5,
    )(solid_parts)
    (slip_b,) = call(
        functools.partial(slip_kernel, half, half),
        [(3, half * BLOCK)],
        [ANY] + [HBM] * 7,
        slip_scratch,
        us=5.0,
    )(eps_tick, *particle_args)
    eps = lax.all_to_all(eps_copies, "sub", 0, 0).reshape(tiles, 8, LANES)
    drag, force, tick = call(
        drag_kernel,
        [(3, blocks * BLOCK), (subs, 66, 8, LANES), (8, LANES)],
        [HBM] + [VMEM] * 5,
        [
            pltpu.VMEM((subs, 66, 8, LANES), F32),
            pltpu.VMEM((LONG, 24, LANES), F32),
            pltpu.SMEM((blocks,), jnp.int32),
            pltpu.SemaphoreType.DMA((2 * subs,)),
        ],
        outs=[VMEM, HBM, VMEM],
        us=6.0,
    )(*pinned(brick_of_block), base, fraction, slip_a, slip_b, eps)
    forces = lax.all_to_all(force, "sub", 0, 0)
    window, even, odd = call(
        window_kernel,
        [(3, depth, 32, LANES), (3, 4, 32, LANES), (3, 4, 32, LANES)],
        [ANY, HBM],
        [pltpu.SemaphoreType.DMA((4,))],
    )(tick, *pinned(velocity))
    even, odd = pair_up(even, 0), pair_up(odd, 1)
    voidfraction, near = call(
        void_kernel, [(depth, width_x, LANES), (24, 8, LANES)], [ANY, VMEM], us=2.0
    )(tick, eps)
    first, first_tick = call(
        first_kernel,
        [(3, 14, 32, LANES), (8, LANES)],
        [VMEM] * 3,
        [pltpu.VMEM((3, 16, 32, LANES), F32)],
        us=1.0,
    )(window, even, odd)

    rows = width_x // subs
    own, even, odd = call(
        source_kernel,
        [(3, depth, 24, LANES), (3, 3, 24, LANES), (3, 3, 24, LANES)],
        [VMEM, VMEM, ANY],
    )(forces, near, first_tick)
    even, odd = pair_up(even, 0), pair_up(odd, 1)
    buffers = [pltpu.VMEM((3, 16, 32, LANES), F32)] * 4 + [pltpu.VMEM((3, 14, 32, LANES), F32)]
    known = call(
        near_kernel,
        [(3, 2, 32, LANES)] * 3 + [(3, 5, rows, LANES)],
        [VMEM] * 3,
        buffers,
        us=2.0,
    )(first, own, even)
    (moved,) = call(
        far_kernel, [(subs, 3, depth, rows, LANES)], [VMEM] * 7, buffers, us=1.0
    )(first, own, odd, *known)
    moved = lax.all_to_all(moved, "sub", 0, 0)
    (new_velocity,) = call(
        place_kernel,
        [velocity.shape],
        [ANY],
        [pltpu.SemaphoreType.DMA((subs,))],
        outs=[HBM],
    )(moved)
    return new_velocity, voidfraction, drag


def solution(mesh):
    in_specs = (
        P(None, "slab", None, None),
        P(None, ("slab", "sub")),
        P(None, ("slab", "sub")),
        P(("slab", "sub")),
        P(("slab", "sub")),
        P(("slab", "sub")),
        P(("slab", "sub")),
    )
    out_specs = (P(None, "slab", None, None), P("slab", None, None), P(None, ("slab", "sub")))
    return jax.shard_map(body, mesh=mesh, in_specs=in_specs, out_specs=out_specs, check_vma=False)
```

```python
import functools

import jax
import jax.numpy as jnp
from jax import lax
from jax.experimental import pallas as pl
from jax.experimental.pallas import tpu as pltpu
from jax.sharding import PartitionSpec as P

BLOCK = 128
LANES = 128
EPS_MIN = 0.35
FLOW_POWER = -0.2
DRAG_POWER = -2.65
VISCOSITY = 1.2
TIME_STEP = 0.05
ITERS = 4
LONG = 32
F32 = jnp.float32
PARAMS = pltpu.CompilerParams(vmem_limit_bytes=16 * 1024 * 1024)
VMEM = pl.BlockSpec(memory_space=pltpu.VMEM)
SMEM = pl.BlockSpec(memory_space=pltpu.SMEM)
HBM = pl.BlockSpec(memory_space=pltpu.HBM)
ANY = pl.BlockSpec(memory_space=pl.ANY)


def transpose_granules(tiles, lane):
    for bit in (1, 2, 4):
        shift = 8 * bit
        high = (lane & shift) != 0
        new = list(tiles)
        for a in range(8):
            if a & bit:
                continue
            b = a | bit
            va, vb = tiles[a], tiles[b]
            new[a] = jnp.where(high, pltpu.roll(vb, shift, 1), va)
            new[b] = jnp.where(high, vb, pltpu.roll(va, LANES - shift, 1))
        tiles = new
    return tiles


def fetch(pairs, sems):
    copies = [pltpu.make_async_copy(a, b, sems.at[i]) for i, (a, b) in enumerate(pairs)]
    for copy in copies:
        copy.start()
    return copies


def lanes_iota():
    return lax.broadcasted_iota(jnp.int32, (8, LANES), 1)


def rows_iota():
    return lax.broadcasted_iota(jnp.int32, (8, LANES), 0)


def spread(row):
    return jnp.broadcast_to(row, (8, LANES))


def particles(base_ref, frac_ref, block):
    at = pl.ds(pl.multiple_of(block * BLOCK, BLOCK), BLOCK)
    base = spread(base_ref[pl.ds(block, 1), :])
    fz = spread(frac_ref[0:1, at])
    fx = spread(frac_ref[1:2, at])
    fy = spread(frac_ref[2:3, at])
    return at, base >> 6, (base >> 3) & 7, base & 7, fz, fx, fy


def axis_weights(rows, first, frac):
    zero = jnp.zeros_like(frac)
    return jnp.where(rows == first, 1.0 - frac, jnp.where(rows == first + 1, frac, zero))


def halves(value):
    high = value.astype(jnp.bfloat16).astype(F32)
    return high, value - high


def plane_weights(rows, zb, yb, fz, fy):
    ky = axis_weights(rows, yb, fy)
    number = zb.astype(F32)
    offset = jnp.concatenate([number, number - 1.0], axis=0).astype(jnp.bfloat16)
    zero = jnp.zeros((16, LANES), jnp.bfloat16)

    def twice(value):
        return jnp.concatenate([value, value], axis=0).astype(jnp.bfloat16)

    parts = []
    for here, above in zip(halves((1.0 - fz) * ky), halves(fz * ky)):
        here, above = twice(here), twice(above)
        for q in range(4):
            upper = jnp.where(offset == 2 * q - 1, above, zero)
            parts.append(jnp.where(offset == 2 * q, here, upper))
    return jnp.concatenate(parts, axis=0)


def split_rows(parts):
    full = jnp.concatenate(parts, axis=0)
    high = full.astype(jnp.bfloat16).astype(F32)
    return jnp.concatenate([high, full - high], axis=0).astype(jnp.bfloat16)


def deposit(blocks):
    left = []
    for n, (parts, _) in enumerate(blocks):
        rows = split_rows(parts)
        pair = [rows, jnp.zeros_like(rows)]
        left.append(jnp.concatenate(pair if n == 0 else pair[::-1], axis=1))
    both = lax.dot_general(
        jnp.concatenate(left, axis=0),
        jnp.concatenate([weights for _, weights in blocks], axis=1),
        (((1,), (1,)), ((), ())),
        preferred_element_type=F32,
    )
    half = both.shape[0] // 4
    found = []
    for n in range(2):
        total = both[2 * n * half : (2 * n + 1) * half] + both[(2 * n + 1) * half : (2 * n + 2) * half]
        found.append(total + pltpu.roll(total, 64, 1))
    return found


def corner_terms(zb, yb, fz, fy, offset):
    index = (zb << 3) + yb + offset
    gz, gy = 1.0 - fz, 1.0 - fy
    return (
        (index, gz * gy),
        (index + 1, gz * fy),
        (index + 8, fz * gy),
        (index + 9, fz * fy),
    )


def interpolate(tile, kx, corners):
    total = None
    for index, weight in corners:
        term = weight * jnp.take_along_axis(tile, index, axis=1, mode="promise_in_bounds")
        total = term if total is None else total + term
    return jnp.sum(kx * total, axis=0, keepdims=True)


def brick_place(brick):
    return brick >> 4, brick & 7, (brick >> 3) & 1


def solid_kernel(
    brick_hbm, base_hbm, frac_hbm, pvol_hbm, out_hbm, tick_ref,
    out_ref, late_ref, brick_ref, base_ref, frac_ref, pvol_ref, sems,
):
    copies = fetch(
        [(brick_hbm, brick_ref), (base_hbm, base_ref), (frac_hbm, frac_ref), (pvol_hbm, pvol_ref)],
        sems,
    )
    out_ref[...] = jnp.zeros_like(out_ref)
    for copy in copies:
        copy.wait()
    rows, lane = rows_iota(), lanes_iota()
    late_ref[...] = jnp.zeros_like(late_ref)

    def add(number):
        for k in range(LONG):
            tx, t3, t1 = brick_place(brick_ref[number * LONG + k])
            out_ref[tx * 8 + t3] += jnp.where((lane >> 6) == t1, late_ref[k], 0.0)

    def step(number, carry):
        add(jnp.maximum(number - 1, 0))
        found = []
        for k in range(LONG):
            block = number * LONG + k
            _, zb, xb, yb, fz, fx, fy = particles(base_ref, frac_ref, block)
            kx = axis_weights(rows, xb, fx) * spread(pvol_ref[pl.ds(block, 1), :])
            found.append(([kx], plane_weights(rows, zb, yb, fz, fy)))
            if k % 2:
                late_ref[k - 1], late_ref[k] = deposit(found[-2:])
        return carry

    steps = base_ref.shape[0] // LONG
    lax.fori_loop(0, steps, step, 0)
    add(steps - 1)
    (copy,) = fetch([(out_ref, out_hbm)], sems)
    tick_ref[...] = jnp.zeros_like(tick_ref)
    copy.wait()


def eps_kernel(parts_ref, copies_hbm, tick_ref, out_ref, sems):
    tick_ref[...] = jnp.zeros_like(tick_ref)
    total = parts_ref[0]
    for j in range(1, parts_ref.shape[0]):
        total = total + parts_ref[j]
    total = jnp.maximum(1.0 - total, EPS_MIN)
    out_ref[...] = total
    for copy in fetch([(out_ref, copies_hbm.at[j]) for j in range(copies_hbm.shape[0])], sems):
        copy.wait()


def slip_work(
    first, count,
    brick_hbm, base_hbm, frac_hbm, pvel_hbm, coef_hbm, pvol_hbm, velocity_hbm,
    out_ref,
    brick_ref, base_ref, frac_ref, pvel_ref, coef_ref, pvol_ref, velocity_ref, table_ref, sems,
):
    some = pl.ds(first, count)
    wide = pl.ds(first * BLOCK, count * BLOCK)
    middle = velocity_hbm.shape[2] // 2
    sides = (slice(0, middle), slice(middle, 2 * middle))
    copies = fetch(
        [(velocity_hbm.at[:, :, side, :], velocity_ref.at[:, :, side, :]) for side in sides]
        + [
            (brick_hbm, brick_ref),
            (base_hbm.at[some], base_ref),
            (frac_hbm.at[:, wide], frac_ref),
            (pvel_hbm.at[:, wide], pvel_ref),
            (coef_hbm.at[some], coef_ref),
            (pvol_hbm.at[some], pvol_ref),
        ],
        sems,
    )
    rows, lane = rows_iota(), lanes_iota()
    tiles_x = velocity_ref.shape[2] // 8

    def convert(number, carry):
        for k in range(2):
            tx = number * 2 + k
            at = pl.ds(pl.multiple_of(tx * 8, 8), 8)
            for c in range(3):
                tiles = transpose_granules([velocity_ref[c, z, at, :] for z in range(8)], lane)
                for t3 in range(8):
                    table_ref[(tx * 3 + c) * 8 + t3] = tiles[t3]
        return carry

    for n in range(2):
        copies[n].wait()
        lax.fori_loop(n * tiles_x // 4, (n + 1) * tiles_x // 4, convert, 0)
    for copy in copies[2:]:
        copy.wait()

    def step(number, carry):
        for k in range(LONG):
            block = number * LONG + k
            at, zb, xb, yb, fz, fx, fy = particles(base_ref, frac_ref, block)
            tx, t3, t1 = brick_place(brick_ref[first + block])
            kx = axis_weights(rows, xb, fx)
            corners = corner_terms(zb, yb, fz, fy, t1 * 64)
            rel = [
                interpolate(table_ref[(tx * 3 + c) * 8 + t3], kx, corners) - pvel_ref[c : c + 1, at]
                for c in range(3)
            ]
            speed = rel[0] * rel[0] + rel[1] * rel[1] + rel[2] * rel[2]
            factor = coef_ref[pl.ds(block, 1), :] * pvol_ref[pl.ds(block, 1), :]
            factor = factor * jnp.exp(FLOW_POWER * jnp.log(speed + 0.01))
            for c in range(3):
                out_ref[c : c + 1, at] = factor * rel[c]
        return carry

    lax.fori_loop(0, count // LONG, step, 0)


def pack_halo(rows, tiles):
    a, b, c, d = tiles
    middle = jnp.logical_or(rows == 3, rows == 4)
    first = jnp.where(middle, pltpu.roll(d, 3, 0), a)
    second = jnp.where(rows == 3, pltpu.roll(d, 1, 0), jnp.where(rows == 4, pltpu.roll(d, 7, 0), b))
    third = jnp.where(middle, pltpu.roll(d, 5, 0), c)
    return first, second, third


def unpack_halo(rows, tiles):
    a, b, c = tiles
    inner = jnp.where(rows == 2, pltpu.roll(b, 7, 0), pltpu.roll(b, 1, 0))
    d = jnp.where(rows < 2, pltpu.roll(a, 5, 0), jnp.where(rows > 5, pltpu.roll(c, 3, 0), inner))
    return a, b, c, d


def slip_kernel(first, count, after_any, *refs):
    slip_work(first, count, *refs)


def even_slip_kernel(count, after_any, early_ref, *refs):
    out_ref = refs[7]
    odd = lax.axis_index("slab") % 2 == 1

    @pl.when(odd)
    def _():
        out_ref[...] = early_ref[...]

    @pl.when(jnp.logical_not(odd))
    def _():
        slip_work(0, count, *refs)


def start_kernel(
    count,
    brick_hbm, base_hbm, frac_hbm, pvel_hbm, coef_hbm, pvol_hbm, velocity_hbm,
    out_hbm, tick_ref, early_ref,
    *scratch,
):
    @pl.when(lax.axis_index("slab") % 2 == 1)
    def _():
        slip_work(
            0, count,
            brick_hbm, base_hbm, frac_hbm, pvel_hbm, coef_hbm, pvol_hbm, velocity_hbm,
            early_ref, *scratch[7:],
        )

    solid_kernel(brick_hbm, base_hbm, frac_hbm, pvol_hbm, out_hbm, tick_ref, *scratch[:7])


def drag_kernel(
    brick_hbm, base_ref, frac_ref, slip_a_ref, slip_b_ref, eps_ref,
    drag_ref, out_hbm, tick_ref,
    force_ref, late_ref, brick_ref, sems,
):
    subs = force_ref.shape[0]
    rows, lane = rows_iota(), lanes_iota()
    (copy,) = fetch([(brick_hbm, brick_ref)], sems)
    for j in range(subs):
        force_ref[j, 0:48] = jnp.zeros((48, 8, LANES), F32)
    copy.wait()

    late_ref[...] = jnp.zeros_like(late_ref)

    def add(number):
        for k in range(LONG):
            tx, t3, t1 = brick_place(brick_ref[number * LONG + k])
            mine = (lane >> 6) == t1
            for c in range(3):
                tile = (tx & 1) * 24 + c * 8 + t3
                force_ref[tx >> 1, tile] += jnp.where(mine, late_ref[k, 8 * c : 8 * c + 8], 0.0)

    steps = base_ref.shape[0] // LONG
    for slip_ref, start in ((slip_a_ref, 0), (slip_b_ref, steps // 2)):

        def step(number, carry, slip_ref=slip_ref, start=start):
            add(jnp.maximum(number - 1, 0))
            found = []
            for k in range(LONG):
                block = number * LONG + k
                inner = block - start * LONG
                at, zb, xb, yb, fz, fx, fy = particles(base_ref, frac_ref, block)
                inner_at = pl.ds(pl.multiple_of(inner * BLOCK, BLOCK), BLOCK)
                tx, t3, t1 = brick_place(brick_ref[block])
                kx = axis_weights(rows, xb, fx)
                eps = interpolate(eps_ref[tx * 8 + t3], kx, corner_terms(zb, yb, fz, fy, t1 * 64))
                factor = jnp.exp(DRAG_POWER * jnp.log(eps))
                parts = []
                for c in range(3):
                    force = factor * slip_ref[c : c + 1, inner_at]
                    drag_ref[c : c + 1, at] = force
                    parts.append(kx * spread(force))
                found.append((parts, plane_weights(rows, zb, yb, fz, fy)))
                if k % 2:
                    late_ref[k - 1], late_ref[k] = deposit(found[-2:])
            return carry

        lax.fori_loop(start, start + steps // 2, step, 0)
    add(steps - 1)
    copies = fetch([(force_ref.at[j, 0:48], out_hbm.at[j, 0:48]) for j in range(subs)], sems)
    zero = jnp.zeros((8, LANES), F32)
    tick_ref[...] = zero
    for j in range(subs):
        for quad in range(6):
            tiles = []
            for at in range(quad * 4, quad * 4 + 4):
                after = force_ref[j + 1, at] if j + 1 < subs else zero
                before = force_ref[j - 1, 24 + at] if j > 0 else zero
                tiles.append(jnp.where(rows < 4, after, before))
            for n, tile in enumerate(pack_halo(rows, tiles)):
                force_ref[j, 48 + quad * 3 + n] = tile
        copy = pltpu.make_async_copy(
            force_ref.at[j, 48:66], out_hbm.at[j, 48:66], sems.at[subs + j]
        )
        copy.start()
        copies.append(copy)
    for copy in copies:
        copy.wait()


def source_kernel(parts_ref, eps_ref, first_any, own_ref, even_ref, odd_ref):
    lane, rows = lanes_iota(), rows_iota()
    even = lax.axis_index("slab") % 2 == 0

    def summed(at):
        total = parts_ref[0, at]
        for j in range(1, parts_ref.shape[0]):
            total = total + parts_ref[j, at]
        return total

    for t in range(3):
        for c in range(3):
            if t < 2:
                forces = [summed(t * 24 + c * 8 + t3) for t3 in range(8)]
            else:
                forces = []
                for quad in (2 * c, 2 * c + 1):
                    forces += unpack_halo(rows, [summed(48 + quad * 3 + k) for k in range(3)])
            tiles = []
            for t3 in range(8):
                tiles.append(-forces[t3] / eps_ref[t * 8 + t3])
            tiles = transpose_granules(tiles, lane)
            first = 8 * (t + 1) % 24
            for z in range(8):
                own_ref[c, z, first : first + 8, :] = tiles[z]
            for n in range(3):
                at = slice(first, first + 8)
                even_ref[c, n, at, :] = jnp.where(even, tiles[5 + n], tiles[n])
                odd_ref[c, n, at, :] = jnp.where(even, tiles[n], tiles[5 + n])


def window_kernel(after_any, velocity_hbm, out_ref, even_ref, odd_ref, sems):
    even = lax.axis_index("slab") % 2 == 0
    depth = velocity_hbm.shape[1]
    tiles_x = velocity_hbm.shape[2] // 8
    pairs, inside = [], []
    for r in range(4):
        want = lax.axis_index("sub") * 2 + r - 1
        inside.append(jnp.logical_and(want >= 0, want < tiles_x))
        at = pl.ds(pl.multiple_of(jnp.clip(want, 0, tiles_x - 1) * 8, 8), 8)
        pairs.append((velocity_hbm.at[:, :, at, :], out_ref.at[:, :, 8 * r : 8 * r + 8, :]))
    for copy in fetch(pairs, sems):
        copy.wait()
    for r in range(4):
        at = slice(8 * r, 8 * r + 8)
        rows = jnp.where(inside[r], out_ref[:, :, at, :], 0.0)
        out_ref[:, :, at, :] = rows
        even_ref[:, :, at, :] = jnp.where(even, rows[:, depth - 4 :], rows[:, :4])
        odd_ref[:, :, at, :] = jnp.where(even, rows[:, :4], rows[:, depth - 4 :])


def void_kernel(after_any, eps_ref, out_ref, near_ref):
    lane, rows = lanes_iota(), rows_iota()
    tiles_x = out_ref.shape[1] // 8

    def convert(number, carry):
        for k in range(4):
            tx = number * 4 + k
            tiles = transpose_granules([eps_ref[tx * 8 + t3] for t3 in range(8)], lane)
            for z in range(8):
                out_ref[z, pl.ds(pl.multiple_of(tx * 8, 8), 8), :] = tiles[z]
        return carry

    lax.fori_loop(0, tiles_x // 4, convert, 0)
    own = lax.axis_index("sub") * 2
    near_ref[0:16] = eps_ref[pl.ds(own * 8, 16)]
    after = eps_ref[pl.ds(jnp.minimum(own + 2, tiles_x - 1) * 8, 8)]
    before = eps_ref[pl.ds(jnp.maximum(own - 1, 0) * 8, 8)]
    near_ref[16:24] = jnp.where(rows[None] < 4, after, before)


def edges():
    slab, sub = lax.axis_index("slab"), lax.axis_index("sub")
    planes, width = lax.axis_size("slab") * 8, lax.axis_size("sub") * 16
    row = lax.broadcasted_iota(jnp.int32, (32, LANES), 0) + sub * 16 - 8
    inside_x = jnp.logical_and(row >= 0, row < width)

    def keep(z):
        height = slab * 8 - 4 + z
        return jnp.logical_and(inside_x, jnp.logical_and(height >= 0, height < planes))

    return keep


def unforced(old, z, lane):
    shear = None
    centres, laps = [], []
    for c in range(3):
        centre = old[c, z]
        upper = old[c, z + 1]
        lower = old[c, z - 1]
        east = pltpu.roll(centre, 31, 0)
        west = pltpu.roll(centre, 1, 0)
        north = jnp.where(lane == LANES - 1, 0.0, pltpu.roll(centre, LANES - 1, 1))
        south = jnp.where(lane == 0, 0.0, pltpu.roll(centre, 1, 1))
        term = (upper - centre) ** 2 + (east - centre) ** 2 + (north - centre) ** 2
        shear = term if shear is None else shear + term
        centres.append(centre)
        laps.append(upper + lower + east + west + north + south - 6.0 * centre)
    viscous = (TIME_STEP * VISCOSITY) * jnp.exp(FLOW_POWER * jnp.log(shear + 0.01))
    return [centres[c] + viscous * laps[c] for c in range(3)]


def first_kernel(window_ref, even_ref, odd_ref, out_ref, tick_ref, old):
    tick_ref[...] = jnp.zeros_like(tick_ref)
    side = lax.axis_index("slab") % 2
    old[:, pl.ds(12 - 12 * side, 4)] = even_ref[...]
    old[:, pl.ds(12 * side, 4)] = odd_ref[...]
    old[:, 4:12] = window_ref[...]
    lane = lax.broadcasted_iota(jnp.int32, (32, LANES), 1)

    def plane(number, carry):
        for k in range(2):
            z = number * 2 + k
            moved = unforced(old, z + 1, lane)
            for c in range(3):
                out_ref[c, z] = moved[c]
        return carry

    lax.fori_loop(0, 7, plane, 0)


def forced(old, new, source, z, keep, lane):
    moved = unforced(old, z, lane)
    inside = keep(z)
    for c in range(3):
        total = moved[c] + TIME_STEP * source[c, z - 1]
        new[c, z] = jnp.where(inside, total, 0.0)


def near_kernel(first_ref, own_ref, even_ref, *refs):
    keeps, last_ref, levels, source = refs[:3], refs[3], refs[4:8], refs[8]
    keep = edges()
    lane = lax.broadcasted_iota(jnp.int32, (32, LANES), 1)
    side = lax.axis_index("slab") % 2

    def plane(n):
        return n + side * (15 - 2 * n)

    for part, planes in ((own_ref, slice(3, 11)), (even_ref, pl.ds(11 - 11 * side, 3))):
        source[:, planes, 0:24, :] = part[...]
        source[:, planes, 24:32, :] = part[:, :, 0:8, :]
    for n in range(4, 15):
        z = plane(n)
        inside = keep(z)
        for c in range(3):
            moved = first_ref[c, z - 1] + TIME_STEP * source[c, z - 1]
            levels[0][c, z] = jnp.where(inside, moved, 0.0)
    for step in range(1, ITERS):

        def run(n, carry, step=step):
            forced(levels[step - 1], levels[step], source, plane(n), keep, lane)
            return carry

        lax.fori_loop(4 + step, 15 - step, run, 0)
    for step in range(3):
        for n in range(2):
            for c in range(3):
                keeps[step][c, n] = levels[step][c, plane(4 + step + n)]
    for n in range(5):
        for c in range(3):
            last_ref[c, n] = levels[3][c, plane(7 + n), 8:24, :]


def far_kernel(first_ref, own_ref, odd_ref, *refs):
    keeps, last_ref, out_ref, levels, source = refs[:3], refs[3], refs[4], refs[5:9], refs[9]
    keep = edges()
    lane = lax.broadcasted_iota(jnp.int32, (32, LANES), 1)
    side = lax.axis_index("slab") % 2

    def plane(n):
        return n + side * (15 - 2 * n)

    for part, planes in ((own_ref, slice(3, 11)), (odd_ref, pl.ds(11 * side, 3))):
        source[:, planes, 0:24, :] = part[...]
        source[:, planes, 24:32, :] = part[:, :, 0:8, :]
    for step in range(3):
        for n in range(2):
            for c in range(3):
                levels[step][c, plane(4 + step + n)] = keeps[step][c, n]
    for n in range(1, 4):
        z = plane(n)
        inside = keep(z)
        for c in range(3):
            moved = first_ref[c, z - 1] + TIME_STEP * source[c, z - 1]
            levels[0][c, z] = jnp.where(inside, moved, 0.0)
    for step in range(1, ITERS):
        for n in range(1 + step, 4 + step):
            forced(levels[step - 1], levels[step], source, plane(n), keep, lane)
    for c in range(3):
        for n in range(3):
            z = plane(4 + n)
            rows = levels[3][c, z, 8:24, :]
            for j in range(out_ref.shape[0]):
                out_ref[j, c, z - 4] = rows
        for n in range(5):
            rows = last_ref[c, n]
            for j in range(out_ref.shape[0]):
                out_ref[j, c, plane(7 + n) - 4] = rows


def place_kernel(parts_ref, out_ref, sems):
    rows = parts_ref.shape[3]
    pairs = []
    for j in range(parts_ref.shape[0]):
        pairs.append((parts_ref.at[j], out_ref.at[:, :, j * rows : (j + 1) * rows, :]))
    for copy in fetch(pairs, sems):
        copy.wait()


def pinned(*arrays):
    return [pltpu.with_memory_space_constraint(x, pltpu.HBM) for x in arrays]


def call(kernel, out_shapes, ins, scratch=(), outs=None, us=1.0):
    outs = outs or [VMEM] * len(out_shapes)
    return pl.pallas_call(
        kernel,
        out_shape=[
            pltpu.HBM(s, F32) if spec is HBM else jax.ShapeDtypeStruct(s, F32)
            for s, spec in zip(out_shapes, outs)
        ],
        in_specs=ins,
        out_specs=outs,
        scratch_shapes=list(scratch),
        compiler_params=PARAMS,
        cost_estimate=pl.CostEstimate(flops=int(us * 1e9), bytes_accessed=int(us * 3.6e6), transcendentals=0),
    )


def pair_up(x, first):
    pairs = [(i, i + 1) for i in range(first, lax.axis_size("slab") - 1, 2)]
    return lax.ppermute(x, "slab", pairs + [(j, i) for i, j in pairs])


def body(velocity, part_vel, fraction, base_cell, drag_coeff, part_volume, brick_of_block):
    depth, width_x = velocity.shape[1], velocity.shape[2]
    blocks = brick_of_block.shape[0]
    subs = lax.axis_size("sub")
    tiles_x = width_x // 8
    tiles = tiles_x * 8
    share = tiles // subs
    base = base_cell.reshape(blocks, BLOCK)
    coef = drag_coeff.reshape(blocks, BLOCK)
    pvol = part_volume.reshape(blocks, BLOCK)

    particles_vmem = [
        pltpu.SMEM((blocks,), jnp.int32),
        pltpu.VMEM((blocks, BLOCK), jnp.int32),
        pltpu.VMEM((3, blocks * BLOCK), F32),
    ]
    row_vmem = pltpu.VMEM((blocks, BLOCK), F32)
    half = blocks // 2
    slip_scratch = [
        pltpu.SMEM((blocks,), jnp.int32),
        pltpu.VMEM((half, BLOCK), jnp.int32),
        pltpu.VMEM((3, half * BLOCK), F32),
        pltpu.VMEM((3, half * BLOCK), F32),
        pltpu.VMEM((half, BLOCK), F32),
        pltpu.VMEM((half, BLOCK), F32),
        pltpu.VMEM(velocity.shape, F32),
        pltpu.VMEM((3 * tiles, 8, LANES), F32),
        pltpu.SemaphoreType.DMA((8,)),
    ]
    particle_args = pinned(brick_of_block, base, fraction, part_vel, coef, pvol, velocity)
    solid, solid_tick, early = call(
        functools.partial(start_kernel, half),
        [(tiles, 8, LANES), (8, LANES), (3, half * BLOCK)],
        [HBM] * 7,
        [pltpu.VMEM((tiles, 8, LANES), F32), pltpu.VMEM((LONG, 8, LANES), F32)]
        + particles_vmem
        + [row_vmem, pltpu.SemaphoreType.DMA((4,))]
        + slip_scratch,
        outs=[HBM, VMEM, VMEM],
        us=5.0,
    )(*particle_args)
    solid_parts = lax.all_to_all(solid.reshape(subs, share, 8, LANES), "sub", 0, 0)
    (slip_a,) = call(
        functools.partial(even_slip_kernel, half),
        [(3, half * BLOCK)],
        [ANY, VMEM] + [HBM] * 7,
        slip_scratch,
        us=5.0,
    )(solid_tick, early, *particle_args)
    eps_copies, eps_tick = call(
        eps_kernel,
        [(subs, share, 8, LANES), (8, LANES)],
        [VMEM],
        [pltpu.VMEM((share, 8, LANES), F32), pltpu.SemaphoreType.DMA((subs,))],
        outs=[HBM, VMEM],
        us=0.5,
    )(solid_parts)
    (slip_b,) = call(
        functools.partial(slip_kernel, half, half),
        [(3, half * BLOCK)],
        [ANY] + [HBM] * 7,
        slip_scratch,
        us=5.0,
    )(eps_tick, *particle_args)
    eps = lax.all_to_all(eps_copies, "sub", 0, 0).reshape(tiles, 8, LANES)
    drag, force, tick = call(
        drag_kernel,
        [(3, blocks * BLOCK), (subs, 66, 8, LANES), (8, LANES)],
        [HBM] + [VMEM] * 5,
        [
            pltpu.VMEM((subs, 66, 8, LANES), F32),
            pltpu.VMEM((LONG, 24, LANES), F32),
            pltpu.SMEM((blocks,), jnp.int32),
            pltpu.SemaphoreType.DMA((2 * subs,)),
        ],
        outs=[VMEM, HBM, VMEM],
        us=6.0,
    )(*pinned(brick_of_block), base, fraction, slip_a, slip_b, eps)
    forces = lax.all_to_all(force, "sub", 0, 0)
    window, even, odd = call(
        window_kernel,
        [(3, depth, 32, LANES), (3, 4, 32, LANES), (3, 4, 32, LANES)],
        [ANY, HBM],
        [pltpu.SemaphoreType.DMA((4,))],
    )(tick, *pinned(velocity))
    even, odd = pair_up(even, 0), pair_up(odd, 1)
    voidfraction, near = call(
        void_kernel, [(depth, width_x, LANES), (24, 8, LANES)], [ANY, VMEM], us=2.0
    )(tick, eps)
    first, first_tick = call(
        first_kernel,
        [(3, 14, 32, LANES), (8, LANES)],
        [VMEM] * 3,
        [pltpu.VMEM((3, 16, 32, LANES), F32)],
        us=1.0,
    )(window, even, odd)

    rows = width_x // subs
    own, even, odd = call(
        source_kernel,
        [(3, depth, 24, LANES), (3, 3, 24, LANES), (3, 3, 24, LANES)],
        [VMEM, VMEM, ANY],
    )(forces, near, first_tick)
    even, odd = pair_up(even, 0), pair_up(odd, 1)
    buffers = [pltpu.VMEM((3, 16, 32, LANES), F32)] * 4 + [pltpu.VMEM((3, 14, 32, LANES), F32)]
    known = call(
        near_kernel,
        [(3, 2, 32, LANES)] * 3 + [(3, 5, rows, LANES)],
        [VMEM] * 3,
        buffers,
        us=2.0,
    )(first, own, even)
    (moved,) = call(
        far_kernel, [(subs, 3, depth, rows, LANES)], [VMEM] * 7, buffers, us=1.0
    )(first, own, odd, *known)
    moved = lax.all_to_all(moved, "sub", 0, 0)
    (new_velocity,) = call(
        place_kernel,
        [velocity.shape],
        [ANY],
        [pltpu.SemaphoreType.DMA((subs,))],
        outs=[HBM],
    )(moved)
    return new_velocity, voidfraction, drag


def solution(mesh):
    in_specs = (
        P(None, "slab", None, None),
        P(None, ("slab", "sub")),
        P(None, ("slab", "sub")),
        P(("slab", "sub")),
        P(("slab", "sub")),
        P(("slab", "sub")),
        P(("slab", "sub")),
    )
    out_specs = (P(None, "slab", None, None), P("slab", None, None), P(None, ("slab", "sub")))
    return jax.shard_map(body, mesh=mesh, in_specs=in_specs, out_specs=out_specs, check_vma=False)
```
